128 devices in a mesh: shard: 32 (over y, z, core), dp: 2 (over x_lo), tensor: 2 (over x_hi).
Axes of the slice: x: 4 (x_hi: 2, x_lo: 2; x = x_hi * 2 + x_lo), y: 4, z: 4, core: 2. Of those that a mesh axis runs over, the one named last changes fastest.
Arguments:
- tokens: bfloat16 [16384, 2048], P(('shard', 'dp')), may hold values from -6 to 6
- lengths: int32 [1, 32], replicated, may hold values from 1 to 1024, 16384 in all within a row
- attn_norm: bfloat16 [2048], P('shard'), may hold values from 0.5 to 1.5
- w_query: bfloat16 [2048, 2048], P('shard', 'tensor'), may hold values from -0.125 to 0.125
- key_projection_weight: bfloat16 [2048, 1024], P('shard', 'tensor'), may hold values from -0.125 to 0.125
- value_projection_weight: bfloat16 [2048, 1024], P('shard', 'tensor'), may hold values from -0.125 to 0.125
- w_output: bfloat16 [2048, 2048], P('tensor', 'shard'), may hold values from -0.75 to 0.75
- q_gain: bfloat16 [128], replicated, may hold values from 0.5 to 1.5
- k_gain: bfloat16 [128], replicated, may hold values from 0.5 to 1.5
- mlp_norm: bfloat16 [2048], P('shard'), may hold values from 0.5 to 1.5
- w_gate: bfloat16 [2048, 6144], P('shard', 'tensor'), may hold values from -0.125 to 0.125
- w_up: bfloat16 [2048, 6144], P('shard', 'tensor'), may hold values from -0.125 to 0.125
- w_down: bfloat16 [6144, 2048], P('tensor', 'shard'), may hold values from -0.125 to 0.125
- cotangent: bfloat16 [16384, 2048], P(('shard', 'dp')), may hold values from -6 to 6
Outputs:
- output: bfloat16 [16384, 2048], P(('shard', 'dp'))
- grad_tokens: float32 [16384, 2048], P(('shard', 'dp'))
- grad_attn_norm: float32 [2048], P('shard')
- grad_query: float32 [2048, 2048], P('shard', 'tensor')
- grad_key: float32 [2048, 1024], P('shard', 'tensor')
- grad_value: float32 [2048, 1024], P('shard', 'tensor')
- grad_output: float32 [2048, 2048], P('tensor', 'shard')
- grad_q_gain: float32 [128], replicated
- grad_k_gain: float32 [128], replicated
- grad_mlp_norm: float32 [2048], P('shard')
- grad_gate: float32 [2048, 6144], P('shard', 'tensor')
- grad_up: float32 [2048, 6144], P('shard', 'tensor')
- grad_down: float32 [6144, 2048], P('tensor', 'shard')
The draws below stay inside these ranges and needn't reach their ends.
Inputs may be any that keep to these rules, and one draw needn't show every extreme that they name: Each row of lengths is one pack's documents in order; they sum to 16384, and the longest of each row has exactly 1024 tokens.
All inputs are finite; a program needn't handle non-finite values.
Results may differ from the reference program's by a relative error of at most 0.03.
Values may be sent and summed in bfloat16 or wider, within the bound.
A program may use at most 256 MiB of HBM per device.

```python
import math
import jax
import jax.numpy as jnp
import numpy as np
from jax import lax

MODEL_WIDTH = 2048
FF = 6144
QUERY_HEADS = 16
KEY_VALUE_HEADS = 8
HEAD_SIZE = 128
PACK_TOKENS = 16384
DOC_MAX = 1024
SEGS = 32
PACK_TOTAL = 1
TOKEN_TOTAL = 16384


def level_of(own_key, extent, shards, smallest, top_value):
    def one(dim, shards_of):
        heights = jax.random.uniform(jax.random.fold_in(jax.random.fold_in(own_key, 6), dim), (shards_of,), jnp.float32, smallest / len(shards), top_value / len(shards))
        return jnp.repeat(jnp.exp(heights), extent[dim] // shards_of).reshape((-1,) + (1,) * (len(extent) - dim - 1))

    loudness = one(*shards[0])
    for cut in shards[1:]:
        loudness = loudness * one(*cut)
    return loudness


def length_profile(amount, total, reach, slope):
    loads = [(1 << 20) // math.isqrt(grade ** slope) + 1 for grade in range(2, amount + 1)]
    rest, counts = total - reach - (amount - 1), [1] * (amount - 1)
    while rest > 0:
        movable = [i for i in range(amount - 1) if counts[i] < reach]
        whole, left = sum([loads[i] for i in movable]), rest
        for i in movable:
            more = min(reach - counts[i], max(1, left * loads[i] // whole), rest)
            counts[i] = counts[i] + more
            rest = rest - more
    return np.array([reach] + counts)


def ragged_sizes(own_key, number_of, total, limit, slope):
    if number_of == 2:
        one = jax.random.randint(own_key, (), max(1, total - limit), min(limit, total - 1) + 1)
        return jnp.stack([one, total - one])
    sizes = jnp.asarray(length_profile(number_of, total, limit, slope), jnp.int32)
    couples = (number_of - 1) // 2
    source_of, taker = sizes[1:1 + 2 * couples:2], sizes[2:2 + 2 * couples:2]
    room = jnp.minimum(source_of - 1, limit - taker)
    shifted = jax.random.randint(jax.random.fold_in(own_key, 1), (couples,), 0, 1 << 20) % (room + 1)
    sizes = sizes.at[1:1 + 2 * couples:2].set(source_of - shifted).at[2:2 + 2 * couples:2].set(taker + shifted)
    return sizes[jax.random.permutation(jax.random.fold_in(own_key, 2), number_of)]


def centred(key, extent, deviation, reach, cuts=(), kind=jnp.bfloat16):
    result = jax.random.normal(key, extent, jnp.float32) * deviation
    if len(cuts) > 0:
        result = level_of(key, extent, cuts, -0.22, 0.18) * result
    return jnp.clip(result, min=-reach, max=reach).astype(kind)


def setup_inputs(seed: int = 0) -> dict:
    splits = jax.random.split(jax.random.key(seed), 15)
    return {
        "tokens": centred(splits[0], (TOKEN_TOTAL, MODEL_WIDTH), 1.0, 6.0, ((0, 64),)),
        "lengths": jax.vmap(lambda own: ragged_sizes(own, SEGS, PACK_TOKENS, DOC_MAX, 2))(jax.random.split(splits[1], PACK_TOTAL)).reshape((PACK_TOTAL, SEGS)).astype(jnp.int32),
        "attn_norm": jnp.clip(1.0 + 0.1 * jax.random.normal(splits[2], (MODEL_WIDTH,), jnp.float32), 0.5, 1.5).astype(jnp.bfloat16),
        "w_query": centred(splits[3], (MODEL_WIDTH, QUERY_HEADS * HEAD_SIZE), MODEL_WIDTH ** -0.5, 0.125, ((0, 32), (1, 2))),
        "key_projection_weight": centred(splits[4], (MODEL_WIDTH, KEY_VALUE_HEADS * HEAD_SIZE), MODEL_WIDTH ** -0.5, 0.125, ((0, 32), (1, 2))),
        "value_projection_weight": centred(splits[5], (MODEL_WIDTH, KEY_VALUE_HEADS * HEAD_SIZE), MODEL_WIDTH ** -0.5, 0.125, ((0, 32), (1, 2))),
        "w_output": centred(splits[6], (QUERY_HEADS * HEAD_SIZE, MODEL_WIDTH), (QUERY_HEADS * HEAD_SIZE // 32) ** -0.5, 0.75, ((0, 2), (1, 32))),
        "q_gain": jnp.clip(1.0 + 0.1 * jax.random.normal(splits[7], (HEAD_SIZE,), jnp.float32), 0.5, 1.5).astype(jnp.bfloat16),
        "k_gain": jnp.clip(1.0 + 0.1 * jax.random.normal(splits[8], (HEAD_SIZE,), jnp.float32), 0.5, 1.5).astype(jnp.bfloat16),
        "mlp_norm": jnp.clip(1.0 + 0.1 * jax.random.normal(splits[9], (MODEL_WIDTH,), jnp.float32), 0.5, 1.5).astype(jnp.bfloat16),
        "w_gate": centred(splits[10], (MODEL_WIDTH, FF), MODEL_WIDTH ** -0.5, 0.125, ((0, 32), (1, 2))),
        "w_up": centred(splits[11], (MODEL_WIDTH, FF), MODEL_WIDTH ** -0.5, 0.125, ((0, 32), (1, 2))),
        "w_down": centred(splits[12], (FF, MODEL_WIDTH), (FF // 3) ** -0.5, 0.125, ((0, 2), (1, 32))),
        "cotangent": centred(splits[13], (TOKEN_TOTAL, MODEL_WIDTH), 1.0, 6.0, ((0, 64),)),
    }


EPS = 1e-06
THETA = 1000000.0

@jax.custom_vjp
def reduced_copy(v):
    return lax.optimization_barrier(v.astype(jnp.bfloat16)).astype(jnp.float32)

@jax.custom_vjp
def reduced_backward(v):
    return v

def low_keep(v):
    return (reduced_copy(v), None)

def low_pass(kept, grad):
    return (grad,)

def back_keep(v):
    return (v, None)

def back_low(kept, grad):
    return (reduced_copy(grad),)
reduced_copy.defvjp(low_keep, low_pass)
reduced_backward.defvjp(back_keep, back_low)

def segments_of(lengths, count):
    steps = jnp.arange(count, dtype=jnp.int32)
    ends = jnp.cumsum(lengths, axis=-1).astype(jnp.int32)
    after = steps[None, :, None] >= ends[:, None, :]
    segment_ids = lax.optimization_barrier(jnp.sum(after.astype(jnp.int32), axis=-1)).astype(jnp.int32)
    start = lax.optimization_barrier(jnp.sum(jnp.where(after, lengths[:, None, :], 0), axis=-1)).astype(jnp.int32)
    return (segment_ids, (steps[None, :] - start).astype(jnp.int32))

def rms(value_rows):
    return value_rows * lax.rsqrt(lax.optimization_barrier(jnp.mean(value_rows * value_rows, axis=-1, keepdims=True)) + EPS)

def rotate(value_rows, cosine, sine):
    half = value_rows.shape[-1] // 2
    turned = jnp.concatenate([-value_rows[..., half:], value_rows[..., :half]], axis=-1)
    return value_rows * cosine + turned * sine

def matrix_product(left, right):
    return jnp.dot(left, right, precision=lax.Precision.HIGHEST)

def attend(pieces):
    query_rows, key_rows, value_rows, segment_ids = pieces
    rows = query_rows.shape[0]
    repeat_heads = query_rows.shape[1]
    q_rows = min(4096, rows)
    count = rows // q_rows
    key_steps = jnp.arange(rows, dtype=jnp.int32)
    starts = (jnp.arange(count, dtype=jnp.int32) * q_rows).astype(jnp.int32)
    q_blocks = query_rows.reshape(count, q_rows, repeat_heads, HEAD_SIZE)

    def one_block(item):
        q_block, start = item
        scores = jnp.einsum('qrd,kd->rqk', q_block, key_rows, precision=lax.Precision.HIGHEST) * HEAD_SIZE ** (-0.5)
        scores = reduced_backward(scores)
        q_steps = start + jnp.arange(q_rows, dtype=jnp.int32)
        q_seg = lax.dynamic_slice_in_dim(segment_ids, start, q_rows, 0)
        valid = (q_seg[:, None] == segment_ids[None, :]) & (q_steps[:, None] >= key_steps[None, :])
        scores = jnp.where(valid, scores, -1e+30)
        probs = reduced_copy(jax.nn.softmax(scores, axis=-1))
        return jnp.einsum('rqk,kd->qrd', probs, value_rows, precision=lax.Precision.HIGHEST)
    out = lax.map(jax.checkpoint(one_block), (q_blocks, starts))
    return out.reshape(rows, repeat_heads, HEAD_SIZE)

def forward(tokens, attn_norm, w_query, key_projection_weight, value_projection_weight, w_output, q_gain, k_gain, mlp_norm, w_gate, w_up, w_down, segment_ids, position):
    repeat_heads = QUERY_HEADS // KEY_VALUE_HEADS
    first_normed = reduced_copy(rms(tokens) * attn_norm)
    q_raw = reduced_backward(matrix_product(first_normed, w_query)).reshape(TOKEN_TOTAL, QUERY_HEADS, HEAD_SIZE)
    key_unnormed = reduced_backward(matrix_product(first_normed, key_projection_weight)).reshape(TOKEN_TOTAL, KEY_VALUE_HEADS, HEAD_SIZE)
    value_unnormed = reduced_copy(reduced_backward(matrix_product(first_normed, value_projection_weight))).reshape(TOKEN_TOTAL, KEY_VALUE_HEADS, HEAD_SIZE)
    freq = THETA ** (-jnp.arange(0, HEAD_SIZE, 2).astype(jnp.float32) / HEAD_SIZE)
    angles = position.reshape(TOKEN_TOTAL).astype(jnp.float32)[:, None] * freq[None, :]
    angles = jnp.concatenate([angles, angles], axis=-1)
    cosine = jnp.cos(angles)[:, None, :]
    sine = jnp.sin(angles)[:, None, :]
    query_rows = reduced_copy(rotate(rms(q_raw) * q_gain, cosine, sine))
    key_rows = reduced_copy(rotate(rms(key_unnormed) * k_gain, cosine, sine))
    query_rows = query_rows.reshape(PACK_TOTAL, PACK_TOKENS, KEY_VALUE_HEADS, repeat_heads, HEAD_SIZE).transpose(0, 2, 1, 3, 4).reshape(PACK_TOTAL * KEY_VALUE_HEADS, PACK_TOKENS, repeat_heads, HEAD_SIZE)
    key_rows = key_rows.reshape(PACK_TOTAL, PACK_TOKENS, KEY_VALUE_HEADS, HEAD_SIZE).transpose(0, 2, 1, 3).reshape(PACK_TOTAL * KEY_VALUE_HEADS, PACK_TOKENS, HEAD_SIZE)
    value_rows = value_unnormed.reshape(PACK_TOTAL, PACK_TOKENS, KEY_VALUE_HEADS, HEAD_SIZE).transpose(0, 2, 1, 3).reshape(PACK_TOTAL * KEY_VALUE_HEADS, PACK_TOKENS, HEAD_SIZE)
    segment_heads = jnp.repeat(segment_ids, KEY_VALUE_HEADS, axis=0)
    attention_output = lax.map(attend, (query_rows, key_rows, value_rows, segment_heads))
    attention_output = attention_output.reshape(PACK_TOTAL, KEY_VALUE_HEADS, PACK_TOKENS, repeat_heads, HEAD_SIZE).transpose(0, 2, 1, 3, 4)
    attention_output = reduced_copy(reduced_backward(attention_output.reshape(TOKEN_TOTAL, QUERY_HEADS * HEAD_SIZE)))
    branch = reduced_backward(matrix_product(attention_output, w_output))
    middle = tokens + branch
    normed2 = reduced_copy(rms(middle) * mlp_norm)
    gate = reduced_backward(matrix_product(normed2, w_gate))
    up = reduced_backward(matrix_product(normed2, w_up))
    hidden = reduced_copy(jax.nn.silu(gate) * up)
    return middle + matrix_product(hidden, w_down)

def reference(tokens, lengths, attn_norm, w_query, key_projection_weight, value_projection_weight, w_output, q_gain, k_gain, mlp_norm, w_gate, w_up, w_down, cotangent):
    segment_ids, position = segments_of(lengths, PACK_TOKENS)
    floats = [a.astype(jnp.float32) for a in (tokens, attn_norm, w_query, key_projection_weight, value_projection_weight, w_output, q_gain, k_gain, mlp_norm, w_gate, w_up, w_down)]

    def apply(*arrays):
        return forward(*arrays, segment_ids, position)
    output, pullback = jax.vjp(apply, *floats)
    grads = pullback(cotangent.astype(jnp.float32))
    return (output.astype(jnp.bfloat16), grads[0], grads[1], grads[2], grads[3], grads[4], grads[5], grads[6], grads[7], grads[8], grads[9], grads[10], grads[11])
```

```python
import functools

import jax
import jax.numpy as jnp
from jax import lax
from jax.experimental import pallas as pl
from jax.experimental.pallas import tpu as pltpu
from jax.sharding import PartitionSpec as P

HEAD = 128
EPS = 1e-06
THETA = 1000000.0
SCALE = HEAD ** (-0.5)
WIDTH = 2048
COLUMN = 1024
MESH = pl.DeviceIdType.MESH
BF = jnp.bfloat16
F32 = jnp.float32
HBM = pl.BlockSpec(memory_space=pl.ANY)
VMEM = pl.BlockSpec(memory_space=pltpu.VMEM)
LIMIT = 56 * 2**20


class Spot:
    def __init__(self):
        shard = lax.axis_index("shard")
        self.lo = lax.axis_index("dp")
        self.hi = lax.axis_index("tensor")
        self.x = self.hi * 2 + self.lo
        self.y = shard // 8
        self.z = (shard // 2) % 4
        self.c = shard % 2

    def dev(self, dx=0, dy=0, dz=0, other=False):
        x = (self.x + dx) % 4
        y = (self.y + dy) % 4
        z = (self.z + dz) % 4
        c = 1 - self.c if other else self.c
        return ((y * 4 + z) * 2 + c, x % 2, x // 2)

    def dp_mate(self):
        return ((self.y * 4 + self.z) * 2 + self.c, 1 - self.lo, self.hi)

    def column(self, step):
        flat = (self.y * 4 + self.z + step + 16) % 16
        return (flat * 2 + self.c, self.lo, self.hi)


def greet(devices):
    barrier = pltpu.get_barrier_semaphore()
    for device in devices:
        pl.semaphore_signal(barrier, inc=1, device_id=device, device_id_type=MESH)
    pl.semaphore_wait(barrier, len(devices))


class Wires:
    def __init__(self, send, recv, local):
        self.send, self.recv, self.here = send, recv, local
        self.count, self.near = 0, 0
        self.sent = []

    def push(self, src, dst, device):
        i = self.count
        self.count += 1
        copy = pltpu.make_async_remote_copy(
            src_ref=src,
            dst_ref=dst,
            send_sem=self.send.at[i],
            recv_sem=self.recv.at[i],
            device_id=device,
            device_id_type=MESH,
        )
        copy.start()
        self.sent.append(copy)
        return copy

    def local(self, src, dst):
        copy = pltpu.make_async_copy(src, dst, self.here.at[self.near])
        self.near += 1
        copy.start()
        return copy

    def sent_now(self, copy):
        copy.wait_send()
        self.sent = [other for other in self.sent if other is not copy]

    def drain(self):
        for copy in self.sent:
            copy.wait_send()


def wires_scratch(remote, local):
    return [
        pltpu.SemaphoreType.DMA((remote,)),
        pltpu.SemaphoreType.DMA((remote,)),
        pltpu.SemaphoreType.DMA((max(local, 1),)),
    ]


def by_rows(count, step, body):
    def run(i, _):
        body(pl.ds(pl.multiple_of(i * step, step), step))
        return 0

    lax.fori_loop(0, count // step, run, 0)


def add_into(dst, *sources):
    def body(rows):
        total = dst[rows, :].astype(F32)
        for source in sources:
            total = total + source[rows, :].astype(F32)
        dst[rows, :] = total.astype(dst.dtype)

    by_rows(dst.shape[0], 16, body)


def run_all(*parts):
    parts = list(parts)
    while parts:
        for part in list(parts):
            if next(part, StopIteration) is StopIteration:
                parts.remove(part)


def plane_gather(w, spot, pack, out):
    y, z, c = spot.y, spot.z, spot.c
    rows = pl.ds(pl.multiple_of(c * 64, 64), 64)
    swap = w.push(pack.at[1 - c], out.at[y, z, rows], spot.dev(other=True))
    own = w.local(pack.at[c], out.at[y, z, rows])
    yield
    swap.wait_recv()
    own.wait()
    ym, yp, zm, zp = (y + 3) % 4, (y + 1) % 4, (z + 3) % 4, (z + 1) % 4
    to_zp, to_zm = spot.dev(dz=1), spot.dev(dz=-1)
    to_yp, to_ym = spot.dev(dy=1), spot.dev(dy=-1)
    a, b = pl.ds(0, 64), pl.ds(64, 64)
    mine_a, mine_b = out.at[y, z, a], out.at[y, z, b]
    a1 = w.push(mine_a, mine_a, to_zp)
    a2 = w.push(mine_a, mine_a, to_zm)
    b1 = w.push(mine_b, mine_b, to_yp)
    b2 = w.push(mine_b, mine_b, to_ym)
    yield
    a1.wait_recv()
    part = out.at[y, zm, pl.ds(0, 32)]
    a3 = w.push(part, part, to_zp)
    b1.wait_recv()
    part = out.at[ym, z, pl.ds(64, 32)]
    b3 = w.push(part, part, to_yp)
    a2.wait_recv()
    part = out.at[y, zp, pl.ds(32, 32)]
    a4 = w.push(part, part, to_zm)
    b2.wait_recv()
    part = out.at[yp, z, pl.ds(96, 32)]
    b4 = w.push(part, part, to_ym)
    yield
    a3.wait_recv()
    a4.wait_recv()
    part = out.at[y, :, a]
    a5 = w.push(part, part, to_yp)
    a6 = w.push(part, part, to_ym)
    b3.wait_recv()
    b4.wait_recv()
    part = out.at[:, z, b]
    b5 = w.push(part, part, to_zp)
    b6 = w.push(part, part, to_zm)
    yield
    a5.wait_recv()
    part = out.at[ym, pl.ds(0, 2), a]
    a7 = w.push(part, part, to_yp)
    b5.wait_recv()
    part = out.at[pl.ds(0, 2), zm, b]
    b7 = w.push(part, part, to_zp)
    a6.wait_recv()
    part = out.at[yp, pl.ds(2, 2), a]
    a8 = w.push(part, part, to_ym)
    b6.wait_recv()
    part = out.at[pl.ds(2, 2), zp, b]
    b8 = w.push(part, part, to_zm)
    yield
    for copy in (a7, b7, a8, b8):
        copy.wait_recv()


def plane_sum_scratch(columns):
    return [
        pltpu.VMEM((2, 2, 64, columns), BF),
        pltpu.VMEM((2, 2, 64, columns), BF),
        pltpu.VMEM((2, 4, 64, columns), BF),
        pltpu.VMEM((2, 2, 2, 64, columns), BF),
        pltpu.VMEM((2, 2, 4, 64, columns), BF),
        pltpu.VMEM((2, 2, 32, columns), BF),
        pltpu.VMEM((2, 2, 64, columns), BF),
        pltpu.VMEM((128, columns), BF),
        pltpu.VMEM((2, 64, columns), BF),
    ]


def plane_sum(w, spot, part, scratch):
    plus, minus, held, in1, in2, in3, in4, full, both = scratch
    c = spot.c
    rows = (pl.ds(0, 64), pl.ds(64, 64))
    lanes = ((spot.y, spot.z), (spot.z, spot.y))
    steps = (("dy", "dz"), ("dz", "dy"))

    def view(h, k, low, size):
        at = (lanes[h][0] + k) % 4
        if h == 0:
            return part.at[at, pl.ds(low, size), rows[h]]
        return part.at[pl.ds(low, size), at, rows[h]]

    def to(h, stage, step):
        return spot.dev(**{steps[h][stage]: step})

    loads, first, second = [], [], []
    for h in range(2):
        first.append(
            (
                w.push(view(h, 2, 0, 2), in1.at[h, 0], to(h, 0, 1)),
                w.push(view(h, 2, 2, 2), in1.at[h, 1], to(h, 0, -1)),
            )
        )
    for h in range(2):
        loads.append(
            (
                w.local(view(h, 1, 0, 2), plus.at[h]),
                w.local(view(h, 3, 2, 2), minus.at[h]),
                w.local(view(h, 0, 0, 4), held.at[h]),
            )
        )
    early = []
    for h in range(2):
        early.append(
            (
                w.push(view(h, 1, 2, 2), in2.at[h, 0, pl.ds(2, 2)], to(h, 0, 1)),
                w.push(view(h, 3, 0, 2), in2.at[h, 1, pl.ds(0, 2)], to(h, 0, -1)),
            )
        )
    yield
    for h in range(2):
        loads[h][0].wait()
        first[h][0].wait_recv()
        for j in range(2):
            add_into(plus.at[h, j], in1.at[h, 0, j])
        one = w.push(plus.at[h], in2.at[h, 0, pl.ds(0, 2)], to(h, 0, 1))
        loads[h][1].wait()
        first[h][1].wait_recv()
        for j in range(2):
            add_into(minus.at[h, j], in1.at[h, 1, j])
        two = w.push(minus.at[h], in2.at[h, 1, pl.ds(2, 2)], to(h, 0, -1))
        second.append((one, two))
    yield
    third, early3 = [], []
    for h in range(2):
        loads[h][2].wait()
        for copy in early[h] + second[h]:
            copy.wait_recv()
        at = [(lanes[h][1] + k) % 4 for k in range(4)]
        add_into(held.at[h, at[2]], in2.at[h, 0, at[2]], in2.at[h, 1, at[2]])
        far = held.at[h, at[2]]
        third.append(
            (
                w.push(far.at[pl.ds(0, 32)], in3.at[h, 0], to(h, 1, 1)),
                w.push(far.at[pl.ds(32, 32)], in3.at[h, 1], to(h, 1, -1)),
            )
        )
        add_into(held.at[h, at[1]], in2.at[h, 0, at[1]], in2.at[h, 1, at[1]])
        one = w.push(held.at[h, at[1], pl.ds(32, 32)], in4.at[h, 0, pl.ds(32, 32)], to(h, 1, 1))
        add_into(held.at[h, at[3]], in2.at[h, 0, at[3]], in2.at[h, 1, at[3]])
        two = w.push(held.at[h, at[3], pl.ds(0, 32)], in4.at[h, 1, pl.ds(0, 32)], to(h, 1, -1))
        early3.append((one, two))
        add_into(held.at[h, at[0]], in2.at[h, 0, at[0]], in2.at[h, 1, at[0]])
    yield
    fourth = []
    for h in range(2):
        at = [(lanes[h][1] + k) % 4 for k in range(4)]
        third[h][0].wait_recv()
        piece = held.at[h, at[1], pl.ds(0, 32)]
        add_into(piece, in3.at[h, 0])
        one = w.push(piece, in4.at[h, 0, pl.ds(0, 32)], to(h, 1, 1))
        third[h][1].wait_recv()
        piece = held.at[h, at[3], pl.ds(32, 32)]
        add_into(piece, in3.at[h, 1])
        two = w.push(piece, in4.at[h, 1, pl.ds(32, 32)], to(h, 1, -1))
        fourth.append((one, two))
    yield
    for h in range(2):
        for copy in early3[h] + fourth[h]:
            copy.wait_recv()
        mine = held.at[h, lanes[h][1]]
        target = full.at[rows[h]]

        def body(r):
            total = mine[r, :].astype(F32) + in4[h, 0, r, :].astype(F32)
            target[r, :] = (total + in4[h, 1, r, :].astype(F32)).astype(BF)

        by_rows(64, 16, body)
    theirs = full.at[pl.ds(pl.multiple_of((1 - c) * 64, 64), 64)]
    mine = full.at[pl.ds(pl.multiple_of(c * 64, 64), 64)]
    swap = w.push(theirs, both.at[c], spot.dev(other=True))

    def keep(r):
        both[c, r, :] = mine[r, :]

    by_rows(64, 16, keep)
    swap.wait_recv()


def column_sum_scratch():
    return [
        pltpu.VMEM((4, 128, WIDTH), BF),
        pltpu.VMEM((4, 128, WIDTH), BF),
        pltpu.VMEM((2, 64, WIDTH), BF),
        pltpu.VMEM((2, 128, WIDTH), BF),
    ]


def column_sum(w, spot, part, scratch, finish):
    own, got, in1, in2 = scratch
    x, c = spot.x, spot.c
    loads, swaps = {}, {}
    right, left = spot.dev(dx=1), spot.dev(dx=-1)
    for k in (2, 1, 3, 0):
        at = (x + k) % 4
        swaps[k] = w.push(part.at[1 - c, at % 2, at // 2], got.at[k], spot.dev(other=True))
        loads[k] = w.local(part.at[c, at % 2, at // 2], own.at[k])
    yield

    def merge(k):
        loads[k].wait()
        swaps[k].wait_recv()
        add_into(own.at[k], got.at[k])

    low, high = pl.ds(0, 64), pl.ds(64, 64)
    merge(2)
    far1 = w.push(own.at[2, low], in1.at[0], right)
    far2 = w.push(own.at[2, high], in1.at[1], left)
    merge(1)
    one = w.push(own.at[1, high], in2.at[0, high], right)
    merge(3)
    two = w.push(own.at[3, low], in2.at[1, low], left)
    merge(0)
    yield
    far1.wait_recv()
    add_into(own.at[1, low], in1.at[0])
    three = w.push(own.at[1, low], in2.at[0, low], right)
    far2.wait_recv()
    add_into(own.at[3, high], in1.at[1])
    four = w.push(own.at[3, high], in2.at[1, high], left)
    yield
    for copy in (one, two, three, four):
        copy.wait_recv()

    def total(rows):
        return own[0, rows, :].astype(F32) + in2[0, rows, :].astype(F32) + in2[1, rows, :].astype(F32)

    finish(total)


def column_share(w, spot, mine, out):
    x, c = spot.x, spot.c
    right, left, mate = spot.dev(dx=1), spot.dev(dx=-1), spot.dev(other=True)

    def slot(k):
        at = (x + k + 4) % 4
        return out.at[c, at % 2, at // 2]

    low, high = pl.ds(0, 64), pl.ds(64, 64)
    own = w.local(mine, slot(0))
    a = w.push(mine, slot(0), right)
    b = w.push(mine, slot(0), left)
    d = w.push(mine, slot(0), mate)
    yield
    a.wait_recv()
    e = w.push(slot(-1).at[low], slot(-1).at[low], right)
    f = w.push(slot(-1), slot(-1), mate)
    b.wait_recv()
    g = w.push(slot(1).at[high], slot(1).at[high], left)
    h = w.push(slot(1), slot(1), mate)
    yield
    e.wait_recv()
    i = w.push(slot(2).at[low], slot(2).at[low], mate)
    g.wait_recv()
    j = w.push(slot(2).at[high], slot(2).at[high], mate)
    yield
    own.wait()
    for copy in (d, f, h, i, j):
        copy.wait_recv()


def token_share(w, spot, block, out):
    c, lo = spot.c, spot.lo
    right, left, mate = spot.dev(dx=1), spot.dev(dx=-1), spot.dev(other=True)
    low, high = pl.ds(0, 128), pl.ds(128, 128)
    own = w.local(block, out.at[c, lo])
    a = w.push(block.at[low], out.at[c, lo, low], right)
    b = w.push(block.at[high], out.at[c, lo, high], left)
    d = w.push(block, out.at[c, lo], mate)
    yield
    a.wait_recv()
    part = out.at[c, 1 - lo, low]
    e = w.push(part, part, mate)
    b.wait_recv()
    part = out.at[c, 1 - lo, high]
    f = w.push(part, part, mate)
    yield
    own.wait()
    for copy in (d, e, f):
        copy.wait_recv()


def pair_share(w, spot, mine, out):
    own = w.local(mine, out.at[spot.hi])
    a = w.push(mine, out.at[spot.hi], spot.dev(dx=2))
    yield
    own.wait()
    a.wait_recv()


def neighbours(spot, x=False, yz=False, core=False, pair=False, far=False):
    found = []
    if x:
        found += [spot.dev(dx=1), spot.dev(dx=-1)]
    if yz:
        found += [spot.dev(dy=1), spot.dev(dy=-1), spot.dev(dz=1), spot.dev(dz=-1)]
    if core:
        found += [spot.dev(other=True)]
    if pair:
        found += [spot.dev(dx=2)]
    if far:
        found += [spot.dev(dy=2), spot.dev(dz=2)]
    return found


def params(collective_id):
    return pltpu.CompilerParams(
        collective_id=collective_id, has_side_effects=True, vmem_limit_bytes=LIMIT
    )


def own_block(ref, spot):
    return ref.at[spot.c, spot.lo, spot.hi]


def open_kernel(tok, cot, pack, tok_out, cot_out, weights, send, recv, here):
    spot = Spot()
    greet(neighbours(spot, x=True, yz=True, core=True))
    w = Wires(send, recv, here)
    run_all(
        plane_gather(w, spot, pack, weights),
        token_share(w, spot, tok, tok_out),
        token_share(w, spot, cot, cot_out),
    )
    w.drain()


def open_call(tok, cot, pack):
    blocks = jax.ShapeDtypeStruct((2, 2, 256, WIDTH), BF)
    return pl.pallas_call(
        open_kernel,
        out_shape=(blocks, blocks, jax.ShapeDtypeStruct((4, 4, 128, pack.shape[-1]), BF)),
        in_specs=[HBM] * 3,
        out_specs=(HBM,) * 3,
        scratch_shapes=wires_scratch(40, 4),
        compiler_params=params(1),
        name="open",
    )(tok, cot, pack)


def next_column_kernel(block, out, send, recv, here):
    spot = Spot()
    greet([spot.column(1), spot.column(-1)])
    w = Wires(send, recv, here)
    w.push(block, out, spot.column(1)).wait_recv()
    w.drain()


def next_column_call(block):
    return pl.pallas_call(
        next_column_kernel,
        out_shape=jax.ShapeDtypeStruct(block.shape, block.dtype),
        in_specs=[HBM],
        out_specs=HBM,
        scratch_shapes=wires_scratch(1, 1),
        compiler_params=params(2),
        name="next_column",
    )(block)


def middle_kernel(part, tok, gain, pack, mid, normed, weights, s0, s1, s2, s3, base, low, send, recv, here):
    spot = Spot()
    greet(neighbours(spot, x=True, yz=True, core=True))
    w = Wires(send, recv, here)
    load = w.local(own_block(tok, spot), base)

    def finish(total):
        load.wait()

        def body(rows):
            middle = base[rows, :].astype(F32) + total(rows)
            mid[rows, :] = middle
            inverse = lax.rsqrt(jnp.mean(middle * middle, axis=-1, keepdims=True) + EPS)
            low[rows, :] = (middle * inverse * gain[...]).astype(BF)

        by_rows(128, 16, body)

    def branch():
        yield from column_sum(w, spot, part, (s0, s1, s2, s3), finish)
        yield from column_share(w, spot, low, normed)

    run_all(branch(), plane_gather(w, spot, pack, weights))
    w.drain()


def middle_call(part, tok, gain, pack):
    blocks = jax.ShapeDtypeStruct((2, 2, 2, 128, WIDTH), BF)
    return pl.pallas_call(
        middle_kernel,
        out_shape=(
            jax.ShapeDtypeStruct((128, WIDTH), F32),
            blocks,
            jax.ShapeDtypeStruct((4, 4, 128, pack.shape[-1]), BF),
        ),
        in_specs=[HBM, HBM, VMEM, HBM],
        out_specs=(VMEM, HBM, HBM),
        scratch_shapes=column_sum_scratch()
        + [pltpu.VMEM((128, WIDTH), BF), pltpu.VMEM((128, WIDTH), BF)]
        + wires_scratch(48, 8),
        compiler_params=params(3),
        name="middle",
    )(part, tok, gain, pack)


def rms_back(total, base, gain, rows, extra, out, gain_grad):
    values = base[rows, :].astype(F32)
    inverse = lax.rsqrt(jnp.mean(values * values, axis=-1, keepdims=True) + EPS)
    normed = values * inverse
    grad = total(rows)
    scaled = grad * gain[...]
    back = inverse * (scaled - normed * jnp.mean(scaled * normed, axis=-1, keepdims=True))
    gain_grad[...] += jnp.sum(grad * normed, axis=0, keepdims=True)
    out[rows, :] = extra[rows, :].astype(F32) + back


def turn_kernel(
    dnorm, mixed, mid, cot, gain, grads, dmid, dbranch, out, gain_grad, both,
    s0, s1, s2, s3, t0, t1, t2, t3, top, low, result, p0, p1, p2, p3, p4, p5, p6, p7, p8, send, recv, here,
):
    spot = Spot()
    greet(neighbours(spot, x=True, yz=True, core=True))
    w = Wires(send, recv, here)
    load = w.local(own_block(cot, spot), top)
    gain_grad[...] = jnp.zeros_like(gain_grad)

    def finish_norm(total):
        load.wait()

        def body(rows):
            rms_back(total, mid, gain, rows, top, dmid, gain_grad)
            low[rows, :] = dmid[rows, :].astype(BF)

        by_rows(128, 16, body)

    def finish_out(total):
        def body(rows):
            result[rows, :] = (mid[rows, :] + total(rows)).astype(BF)

        by_rows(128, 16, body)

    def back():
        yield from column_sum(w, spot, dnorm, (s0, s1, s2, s3), finish_norm)
        yield from column_share(w, spot, low, dbranch)

    def forth():
        yield
        yield
        yield from column_sum(w, spot, mixed, (t0, t1, t2, t3), finish_out)

    scratch = (p0, p1, p2, p3, p4, p5, p6, p7, p8)
    run_all(back(), plane_sum(w, spot, grads, scratch), forth())
    first = w.local(result, out)
    second = w.local(p8, both)
    first.wait()
    second.wait()
    w.drain()


def turn_call(dnorm, mixed, mid, cot, gain, grads):
    blocks = jax.ShapeDtypeStruct((2, 2, 2, 128, WIDTH), BF)
    columns = grads.shape[-1]
    return pl.pallas_call(
        turn_kernel,
        out_shape=(
            jax.ShapeDtypeStruct((128, WIDTH), F32),
            blocks,
            jax.ShapeDtypeStruct((128, WIDTH), BF),
            jax.ShapeDtypeStruct((1, WIDTH), F32),
            jax.ShapeDtypeStruct((2, 64, columns), BF),
        ),
        in_specs=[HBM, HBM, VMEM, HBM, VMEM, HBM],
        out_specs=(VMEM, HBM, HBM, VMEM, HBM),
        scratch_shapes=column_sum_scratch()
        + column_sum_scratch()
        + [pltpu.VMEM((128, WIDTH), BF)] * 3
        + plane_sum_scratch(columns)
        + wires_scratch(64, 24),
        compiler_params=params(4),
        name="turn",
    )(dnorm, mixed, mid, cot, gain, grads)


def back_column_kernel(block, result, both, came, out, whole, send, recv, here):
    spot = Spot()
    greet([spot.column(1), spot.column(-1), spot.dev(dx=2), spot.dp_mate()])
    w = Wires(send, recv, here)
    a = w.push(block, came, spot.column(-1))
    own = w.local(both, whole.at[spot.lo])
    b = w.push(both, whole.at[spot.lo], spot.dp_mate())
    run_all(pair_share(w, spot, result, out))
    own.wait()
    a.wait_recv()
    b.wait_recv()
    w.drain()


def back_column_call(block, result, both):
    return pl.pallas_call(
        back_column_kernel,
        out_shape=(
            jax.ShapeDtypeStruct(block.shape, block.dtype),
            jax.ShapeDtypeStruct((2, 128, WIDTH), BF),
            jax.ShapeDtypeStruct((2,) + both.shape, BF),
        ),
        in_specs=[HBM] * 3,
        out_specs=(HBM,) * 3,
        scratch_shapes=wires_scratch(4, 4),
        compiler_params=params(5),
        name="back_column",
    )(block, result, both)


def sum_everywhere(w, spot, vector, pair, lines):
    a = w.push(vector, pair, spot.dev(other=True))
    yield
    a.wait_recv()
    w.sent_now(a)
    vector[...] = vector[...] + pair[...]
    yield
    for stage, (axis, at) in enumerate((("dx", spot.x), ("dy", spot.y), ("dz", spot.z))):
        slots = lines.at[stage]
        slots[at] = vector[...]
        copies = [w.push(vector, slots.at[at], spot.dev(**{axis: k})) for k in (1, 2, 3)]
        yield
        for copy in copies:
            copy.wait_recv()
            w.sent_now(copy)
        vector[...] = slots[0] + slots[1] + slots[2] + slots[3]
        yield


def close_kernel(
    dnorm, tok, gain, dmid, grads, small, gtok, whole, vector,
    s0, s1, s2, s3, base, final, gain_grad, low, theirs, p0, p1, p2, p3, p4, p5, p6, p7, p8, pair, lines,
    send, recv, here,
):
    spot = Spot()
    mates = neighbours(spot, x=True, yz=True, core=True, pair=True, far=True)
    greet(mates)
    w = Wires(send, recv, here)
    load = w.local(own_block(tok, spot), base)
    gain_grad[...] = jnp.zeros_like(gain_grad)

    def finish(total):
        load.wait()

        def body(rows):
            rms_back(total, base, gain, rows, dmid, final, gain_grad)
            low[rows, :] = final[rows, :].astype(BF)

        by_rows(128, 16, body)

    def back():
        yield from column_sum(w, spot, dnorm, (s0, s1, s2, s3), finish)
        sent = w.push(low, theirs, spot.dev(dx=2))
        vector[...] = small[...]
        for i in range(16):
            vector[i : i + 1, :] = gain_grad[:, i * 128 : (i + 1) * 128]
        yield from sum_everywhere(w, spot, vector, pair, lines)
        by_rows(128, 16, lambda rows: final.__setitem__((rows, slice(None)), low[rows, :].astype(F32)))
        one = w.local(final, gtok.at[spot.hi])
        sent.wait_recv()
        one.wait()
        by_rows(128, 16, lambda rows: final.__setitem__((rows, slice(None)), theirs[rows, :].astype(F32)))
        two = w.local(final, gtok.at[1 - spot.hi])
        two.wait()

    def weights():
        yield from plane_sum(w, spot, grads, (p0, p1, p2, p3, p4, p5, p6, p7, p8))
        own = w.local(p8, whole.at[spot.lo])
        a = w.push(p8, whole.at[spot.lo], spot.dp_mate())
        yield
        own.wait()
        a.wait_recv()

    run_all(back(), weights())
    w.drain()


def close_call(dnorm, tok, gain, dmid, grads, small):
    columns = grads.shape[-1]
    rows = small.shape[0]
    return pl.pallas_call(
        close_kernel,
        out_shape=(
            jax.ShapeDtypeStruct((2, 128, WIDTH), F32),
            jax.ShapeDtypeStruct((2, 2, 64, columns), BF),
            jax.ShapeDtypeStruct((rows, 128), F32),
        ),
        in_specs=[HBM, HBM, VMEM, VMEM, HBM, VMEM],
        out_specs=(HBM, HBM, VMEM),
        scratch_shapes=column_sum_scratch()
        + [
            pltpu.VMEM((128, WIDTH), BF),
            pltpu.VMEM((128, WIDTH), F32),
            pltpu.VMEM((1, WIDTH), F32),
            pltpu.VMEM((128, WIDTH), BF),
            pltpu.VMEM((128, WIDTH), BF),
        ]
        + plane_sum_scratch(columns)
        + [pltpu.VMEM((rows, 128), F32), pltpu.VMEM((3, 4, rows, 128), F32)]
        + wires_scratch(64, 24),
        compiler_params=params(6),
        name="close",
    )(dnorm, tok, gain, dmid, grads, small)


BLOCK = 256
SPAN = COLUMN + BLOCK
NT = (((1,), (1,)), ((), ()))
TN = (((0,), (0,)), ((), ()))
NN = (((1,), (0,)), ((), ()))


def dot(a, b, dims):
    return lax.dot_general(a, b, dims, preferred_element_type=F32)


def attend_kernel(q, kv, doc_q, doc_k, out, inverse):
    start = pl.multiple_of(pl.program_id(0) * BLOCK, BLOCK)
    keys = kv[pl.ds(start, SPAN), 0:HEAD]
    values = kv[pl.ds(start, SPAN), HEAD:]
    row = lax.broadcasted_iota(jnp.int32, (BLOCK, SPAN), 0)
    col = lax.broadcasted_iota(jnp.int32, (BLOCK, SPAN), 1)
    valid = (doc_q[...] == doc_k[:, pl.ds(start, SPAN)]) & (col <= row + COLUMN)
    for h in range(2):
        scores = dot(q[:, h * HEAD : (h + 1) * HEAD], keys, NT) * SCALE
        weights = jnp.where(valid, jnp.exp(scores), 0.0)
        back = 1.0 / jnp.sum(weights, axis=-1, keepdims=True)
        probs = (weights * back).astype(BF)
        out[:, h * HEAD : (h + 1) * HEAD] = dot(probs, values, NN).astype(BF)
        inverse[:, h : h + 1] = back


def attend_call(q, kv, doc_q, doc_k):
    return pl.pallas_call(
        attend_kernel,
        grid=(COLUMN // BLOCK,),
        out_shape=(
            jax.ShapeDtypeStruct((COLUMN, 2 * HEAD), BF),
            jax.ShapeDtypeStruct((COLUMN, 2), F32),
        ),
        in_specs=[
            pl.BlockSpec((BLOCK, 2 * HEAD), lambda i: (i, 0)),
            VMEM,
            pl.BlockSpec((BLOCK, 1), lambda i: (i, 0)),
            VMEM,
        ],
        out_specs=(
            pl.BlockSpec((BLOCK, 2 * HEAD), lambda i: (i, 0)),
            pl.BlockSpec((BLOCK, 2), lambda i: (i, 0)),
        ),
        compiler_params=pltpu.CompilerParams(vmem_limit_bytes=LIMIT),
        name="attend",
    )(q, kv, doc_q, doc_k)


def attend_back_kernel(q, kv, do, doc_q, doc_k, inverse, delta, dq, dkv):
    @pl.when(pl.program_id(0) == 0)
    def _():
        dkv[...] = jnp.zeros_like(dkv)

    start = pl.multiple_of(pl.program_id(0) * BLOCK, BLOCK)
    keys = kv[pl.ds(start, SPAN), 0:HEAD]
    values = kv[pl.ds(start, SPAN), HEAD:]
    row = lax.broadcasted_iota(jnp.int32, (SPAN, BLOCK), 0)
    col = lax.broadcasted_iota(jnp.int32, (SPAN, BLOCK), 1)
    valid = (doc_k[pl.ds(start, SPAN), :] == doc_q[...]) & (row <= col + COLUMN)
    for h in range(2):
        span = slice(h * HEAD, (h + 1) * HEAD)
        query = q[:, span]
        upstream = do[:, span]
        scores = dot(keys, query, NT) * SCALE
        probs = jnp.where(valid, jnp.exp(scores), 0.0) * inverse[h : h + 1, :]
        d_probs = dot(values, upstream, NT)
        d_scores = (probs * (d_probs - delta[h : h + 1, :])).astype(BF)
        dkv[pl.ds(start, SPAN), 0:HEAD] += dot(d_scores, query, NN) * SCALE
        dkv[pl.ds(start, SPAN), HEAD:] += dot(probs.astype(BF), upstream, NN)
        dq[:, span] = dot(d_scores, keys, TN) * SCALE


def attend_back_call(q, kv, do, doc_q, doc_k, inverse, delta):
    return pl.pallas_call(
        attend_back_kernel,
        grid=(COLUMN // BLOCK,),
        out_shape=(
            jax.ShapeDtypeStruct((COLUMN, 2 * HEAD), F32),
            jax.ShapeDtypeStruct((2 * COLUMN, 2 * HEAD), F32),
        ),
        in_specs=[
            pl.BlockSpec((BLOCK, 2 * HEAD), lambda i: (i, 0)),
            VMEM,
            pl.BlockSpec((BLOCK, 2 * HEAD), lambda i: (i, 0)),
            pl.BlockSpec((1, BLOCK), lambda i: (0, i)),
            VMEM,
            pl.BlockSpec((2, BLOCK), lambda i: (0, i)),
            pl.BlockSpec((2, BLOCK), lambda i: (0, i)),
        ],
        out_specs=(pl.BlockSpec((BLOCK, 2 * HEAD), lambda i: (i, 0)), VMEM),
        compiler_params=pltpu.CompilerParams(vmem_limit_bytes=LIMIT),
        name="attend_back",
    )(q, kv, do, doc_q, doc_k, inverse, delta)


def documents_of(lengths, first_row, count):
    rows = first_row + jnp.arange(count, dtype=jnp.int32)
    bounds = jnp.cumsum(lengths[0])
    passed = rows[:, None] >= bounds[None, :]
    document = jnp.sum(passed.astype(jnp.int32), axis=-1)
    start = jnp.sum(jnp.where(passed, lengths[0][None, :], 0), axis=-1)
    return (jnp.where(rows >= 0, document, -1), rows - start)


def rms_forward(rows):
    inverse = lax.rsqrt(jnp.mean(rows * rows, axis=-1, keepdims=True) + EPS)
    return (rows * inverse, inverse)


def rms_backward(grad, gain, normed, inverse):
    scaled = grad * gain
    back = inverse * (scaled - normed * jnp.mean(scaled * normed, axis=-1, keepdims=True))
    return (back, jnp.sum(grad * normed, axis=0))


def rotate(rows, cosine, sine):
    half = rows.shape[-1] // 2
    turned = jnp.concatenate([-rows[..., half:], rows[..., :half]], axis=-1)
    return rows * cosine + turned * sine


def mine_of(weight, dp):
    rows, columns = weight.shape
    quarter = lax.dynamic_slice_in_dim(weight, dp * (columns // 2), columns // 2, 1)
    return quarter.reshape(rows, 2, columns // 4).transpose(1, 0, 2)


def on_device(
    tokens, lengths, attn_norm, w_query, w_key, w_value, w_output, q_gain, k_gain, mlp_norm, w_gate, w_up, w_down, cotangent,
):
    shard = lax.axis_index("shard")
    dp = lax.axis_index("dp")
    first_row = (shard // 2) * COLUMN
    documents, places = documents_of(lengths, first_row - COLUMN, 2 * COLUMN)
    freq = THETA ** (-jnp.arange(0, HEAD, 2).astype(F32) / HEAD)
    angles = places[COLUMN:].astype(F32)[:, None] * freq[None, :]
    angles = jnp.concatenate([angles, angles], axis=-1)
    cosine, sine = jnp.cos(angles), jnp.sin(angles)
    doc_row, doc_col = documents[None, :], documents[:, None]

    gains = jnp.pad(jnp.stack([attn_norm, mlp_norm], axis=1), ((0, 0), (0, 126)))
    pack1 = jnp.concatenate(
        [
            mine_of(w_query, dp),
            mine_of(w_key, dp),
            mine_of(w_value, dp),
            mine_of(w_output.T, dp),
            jnp.stack([gains, gains]),
        ],
        axis=-1,
    )
    pack2 = jnp.concatenate([mine_of(w_gate, dp), mine_of(w_up, dp), mine_of(w_down.T, dp)], axis=-1)
    tok, cot, weights1 = open_call(tokens, cotangent, pack1)
    weights1 = weights1.reshape(WIDTH, 896)
    w_qkv, w_out = weights1[:, :512], weights1[:, 512:768]
    both_gains = weights1[:, 768:770].astype(F32).T
    attn_gain, mlp_gain = both_gains[0:1], both_gains[1:2]
    q_scale, k_scale = q_gain.astype(F32), k_gain.astype(F32)

    inputs = tok.reshape(COLUMN, WIDTH).astype(F32)
    normed1 = (rms_forward(inputs)[0] * attn_gain).astype(BF)
    raw = jnp.dot(normed1, w_qkv, preferred_element_type=F32)
    heads = [rms_forward(raw[:, i * HEAD : (i + 1) * HEAD]) for i in range(3)]
    scales = [q_scale, q_scale, k_scale]
    turned = [rotate(n * s, cosine, sine).astype(BF) for (n, _), s in zip(heads, scales)]
    query = jnp.concatenate(turned[:2], axis=-1)
    kv = jnp.concatenate([turned[2], raw[:, 3 * HEAD :].astype(BF)], axis=-1)
    kv_all = jnp.concatenate([next_column_call(kv), kv], axis=0)
    attended, inverse = attend_call(query, kv_all, doc_col[COLUMN:], doc_row)
    branch = lax.dot_general(attended, w_out, NT, preferred_element_type=F32).astype(BF)
    blocks = (2, 2, 2, 128, WIDTH)
    middle, normed2, weights2 = middle_call(
        branch.reshape(blocks), tok.reshape(blocks), mlp_gain, pack2
    )
    normed2 = normed2.reshape(COLUMN, WIDTH)
    weights2 = weights2.reshape(WIDTH, 2304)
    w_in, w_dn = weights2[:, :1536], weights2[:, 1536:]
    cot_rows = cot.reshape(COLUMN, WIDTH)
    gate_up = jnp.dot(normed2, w_in, preferred_element_type=F32)
    gate, up = gate_up[:, :768], gate_up[:, 768:]
    sigma = jax.nn.sigmoid(gate)
    active = gate * sigma
    hidden = (active * up).astype(BF)
    mixed = lax.dot_general(hidden, w_dn, NT, preferred_element_type=F32).astype(BF)
    d_hidden = jnp.dot(cot_rows, w_dn, preferred_element_type=F32)
    d_gate = (d_hidden * up * sigma * (1.0 + gate * (1.0 - sigma))).astype(BF)
    d_up = (d_hidden * active).astype(BF)
    d_both = jnp.concatenate([d_gate, d_up], axis=-1)
    d_norm2 = lax.dot_general(d_both, w_in, NT, preferred_element_type=F32).astype(BF)
    g_in = lax.dot_general(normed2, d_both, TN, preferred_element_type=F32).astype(BF)
    g_down = lax.dot_general(cot_rows, hidden, TN, preferred_element_type=F32).astype(BF)
    grads2 = jnp.concatenate([g_in, g_down], axis=-1).reshape(4, 4, 128, 2304)
    d_middle, d_branch, result, g_mlp, both2 = turn_call(
        d_norm2.reshape(blocks), mixed.reshape(blocks), middle, cot.reshape(blocks), mlp_gain, grads2
    )
    d_branch = d_branch.reshape(COLUMN, WIDTH)
    d_attended = jnp.dot(d_branch, w_out, preferred_element_type=F32).astype(BF)
    g_out = lax.dot_general(d_branch, attended, TN, preferred_element_type=F32).astype(BF)
    product = attended.astype(F32) * d_attended.astype(F32)
    delta = jnp.sum(product.reshape(COLUMN, 2, HEAD), axis=-1).T
    d_query, d_kv = attend_back_call(
        query, kv_all, d_attended, doc_row[:, COLUMN:], doc_col, inverse.T, delta
    )
    came, out, whole2 = back_column_call(d_kv[:COLUMN].astype(BF), result, both2)
    last = shard // 2 == 15
    d_kv = d_kv[COLUMN:] + jnp.where(last, 0.0, came.astype(F32))
    incoming = [d_query[:, :HEAD], d_query[:, HEAD:], d_kv[:, :HEAD]]
    d_raw, g_gain = [], []
    for grad, s, (n, i) in zip(incoming, scales, heads):
        back, gain_grad = rms_backward(rotate(grad, cosine, -sine), s, n, i)
        d_raw.append(back.astype(BF))
        g_gain.append(gain_grad)
    d_qkv = jnp.concatenate(d_raw + [d_kv[:, HEAD:].astype(BF)], axis=-1)
    d_norm1 = lax.dot_general(d_qkv, w_qkv, NT, preferred_element_type=F32).astype(BF)
    g_qkv = lax.dot_general(normed1, d_qkv, TN, preferred_element_type=F32).astype(BF)
    grads1 = jnp.concatenate([g_qkv, g_out], axis=-1).reshape(4, 4, 128, 768)
    small = jnp.concatenate(
        [
            jnp.zeros((16, 128), F32),
            g_mlp.reshape(16, 128),
            (g_gain[0] + g_gain[1])[None],
            g_gain[2][None],
            jnp.zeros((6, 128), F32),
        ],
        axis=0,
    )
    g_tokens, whole1, sums = close_call(
        d_norm1.reshape(blocks), tok.reshape(blocks), attn_gain, d_middle, grads1, small
    )

    def spread(whole, low, size):
        piece = whole[..., low : low + size].astype(F32)
        return piece.transpose(2, 0, 1, 3).reshape(64, 4 * size)

    def rows_of(block):
        return lax.dynamic_slice_in_dim(block.reshape(WIDTH), shard * 64, 64)

    return (
        out.reshape(256, WIDTH),
        g_tokens.reshape(256, WIDTH),
        rows_of(sums[0:16]),
        spread(whole1, 0, 256),
        spread(whole1, 256, 128),
        spread(whole1, 384, 128),
        spread(whole1, 512, 256).T,
        sums[32],
        sums[33],
        rows_of(sums[16:32]),
        spread(whole2, 0, 768),
        spread(whole2, 768, 768),
        spread(whole2, 1536, 768).T,
    )


def solution(mesh):
    rows = P(("shard", "dp"), None)
    down = P("shard", "tensor")
    across = P("tensor", "shard")
    one = P("shard")
    return jax.shard_map(
        on_device,
        mesh=mesh,
        in_specs=(rows, P(), one, down, down, down, across, P(), P(), one, down, down, across, rows),
        out_specs=(rows, rows, one, down, down, down, across, P(), P(), one, down, down, across),
        check_vma=False,
    )
```

```python
import functools

import jax
import jax.numpy as jnp
from jax import lax
from jax.experimental import pallas as pl
from jax.experimental.pallas import tpu as pltpu
from jax.sharding import PartitionSpec as P

HEAD = 128
EPS = 1e-06
THETA = 1000000.0
SCALE = HEAD ** (-0.5)
WIDTH = 2048
COLUMN = 1024
MESH = pl.DeviceIdType.MESH
BF = jnp.bfloat16
F32 = jnp.float32
HBM = pl.BlockSpec(memory_space=pl.ANY)
VMEM = pl.BlockSpec(memory_space=pltpu.VMEM)
LIMIT = 56 * 2**20


class Spot:
    def __init__(self):
        shard = lax.axis_index("shard")
        self.lo = lax.axis_index("dp")
        self.hi = lax.axis_index("tensor")
        self.x = self.hi * 2 + self.lo
        self.y = shard // 8
        self.z = (shard // 2) % 4
        self.c = shard % 2

    def dev(self, dx=0, dy=0, dz=0, other=False):
        x = (self.x + dx) % 4
        y = (self.y + dy) % 4
        z = (self.z + dz) % 4
        c = 1 - self.c if other else self.c
        return ((y * 4 + z) * 2 + c, x % 2, x // 2)

    def dp_mate(self):
        return ((self.y * 4 + self.z) * 2 + self.c, 1 - self.lo, self.hi)

    def column(self, step):
        flat = (self.y * 4 + self.z + step + 16) % 16
        return (flat * 2 + self.c, self.lo, self.hi)


def greet(devices):
    barrier = pltpu.get_barrier_semaphore()
    for device in devices:
        pl.semaphore_signal(barrier, inc=1, device_id=device, device_id_type=MESH)
    pl.semaphore_wait(barrier, len(devices))


class Wires:
    def __init__(self, send, recv, local):
        self.send, self.recv, self.here = send, recv, local
        self.count, self.near = 0, 0
        self.sent = []

    def push(self, src, dst, device):
        i = self.count
        self.count += 1
        copy = pltpu.make_async_remote_copy(
            src_ref=src,
            dst_ref=dst,
            send_sem=self.send.at[i],
            recv_sem=self.recv.at[i],
            device_id=device,
            device_id_type=MESH,
        )
        copy.start()
        self.sent.append(copy)
        return copy

    def local(self, src, dst):
        copy = pltpu.make_async_copy(src, dst, self.here.at[self.near])
        self.near += 1
        copy.start()
        return copy

    def sent_now(self, copy):
        copy.wait_send()
        self.sent = [other for other in self.sent if other is not copy]

    def drain(self):
        for copy in self.sent:
            copy.wait_send()


def wires_scratch(remote, local):
    return [
        pltpu.SemaphoreType.DMA((remote,)),
        pltpu.SemaphoreType.DMA((remote,)),
        pltpu.SemaphoreType.DMA((max(local, 1),)),
    ]


def by_rows(count, step, body):
    def run(i, _):
        body(pl.ds(pl.multiple_of(i * step, step), step))
        return 0

    lax.fori_loop(0, count // step, run, 0)


def add_into(dst, *sources):
    def body(rows):
        total = dst[rows, :].astype(F32)
        for source in sources:
            total = total + source[rows, :].astype(F32)
        dst[rows, :] = total.astype(dst.dtype)

    by_rows(dst.shape[0], 16, body)


def run_all(*parts):
    parts = list(parts)
    while parts:
        for part in list(parts):
            if next(part, StopIteration) is StopIteration:
                parts.remove(part)


def plane_gather(w, spot, pack, out):
    y, z, c = spot.y, spot.z, spot.c
    rows = pl.ds(pl.multiple_of(c * 64, 64), 64)
    swap = w.push(pack.at[1 - c], out.at[y, z, rows], spot.dev(other=True))
    own = w.local(pack.at[c], out.at[y, z, rows])
    yield
    swap.wait_recv()
    own.wait()
    ym, yp, zm, zp = (y + 3) % 4, (y + 1) % 4, (z + 3) % 4, (z + 1) % 4
    to_zp, to_zm = spot.dev(dz=1), spot.dev(dz=-1)
    to_yp, to_ym = spot.dev(dy=1), spot.dev(dy=-1)
    a, b = pl.ds(0, 64), pl.ds(64, 64)
    mine_a, mine_b = out.at[y, z, a], out.at[y, z, b]
    a1 = w.push(mine_a, mine_a, to_zp)
    a2 = w.push(mine_a, mine_a, to_zm)
    b1 = w.push(mine_b, mine_b, to_yp)
    b2 = w.push(mine_b, mine_b, to_ym)
    yield
    a1.wait_recv()
    part = out.at[y, zm, pl.ds(0, 32)]
    a3 = w.push(part, part, to_zp)
    b1.wait_recv()
    part = out.at[ym, z, pl.ds(64, 32)]
    b3 = w.push(part, part, to_yp)
    a2.wait_recv()
    part = out.at[y, zp, pl.ds(32, 32)]
    a4 = w.push(part, part, to_zm)
    b2.wait_recv()
    part = out.at[yp, z, pl.ds(96, 32)]
    b4 = w.push(part, part, to_ym)
    yield
    a3.wait_recv()
    a4.wait_recv()
    part = out.at[y, :, a]
    a5 = w.push(part, part, to_yp)
    a6 = w.push(part, part, to_ym)
    b3.wait_recv()
    b4.wait_recv()
    part = out.at[:, z, b]
    b5 = w.push(part, part, to_zp)
    b6 = w.push(part, part, to_zm)
    yield
    a5.wait_recv()
    part = out.at[ym, pl.ds(0, 2), a]
    a7 = w.push(part, part, to_yp)
    b5.wait_recv()
    part = out.at[pl.ds(0, 2), zm, b]
    b7 = w.push(part, part, to_zp)
    a6.wait_recv()
    part = out.at[yp, pl.ds(2, 2), a]
    a8 = w.push(part, part, to_ym)
    b6.wait_recv()
    part = out.at[pl.ds(2, 2), zp, b]
    b8 = w.push(part, part, to_zm)
    yield
    for copy in (a7, b7, a8, b8):
        copy.wait_recv()


def plane_sum_scratch(columns):
    return [
        pltpu.VMEM((2, 2, 64, columns), BF),
        pltpu.VMEM((2, 2, 64, columns), BF),
        pltpu.VMEM((2, 4, 64, columns), BF),
        pltpu.VMEM((2, 2, 2, 64, columns), BF),
        pltpu.VMEM((2, 2, 4, 64, columns), BF),
        pltpu.VMEM((2, 2, 32, columns), BF),
        pltpu.VMEM((2, 2, 64, columns), BF),
        pltpu.VMEM((128, columns), BF),
        pltpu.VMEM((2, 64, columns), BF),
    ]


def plane_sum(w, spot, part, scratch):
    plus, minus, held, in1, in2, in3, in4, full, both = scratch
    c = spot.c
    rows = (pl.ds(0, 64), pl.ds(64, 64))
    lanes = ((spot.y, spot.z), (spot.z, spot.y))
    steps = (("dy", "dz"), ("dz", "dy"))

    def view(h, k, low, size):
        at = (lanes[h][0] + k) % 4
        if h == 0:
            return part.at[at, pl.ds(low, size), rows[h]]
        return part.at[pl.ds(low, size), at, rows[h]]

    def to(h, stage, step):
        return spot.dev(**{steps[h][stage]: step})

    loads, first, second = [], [], []
    for h in range(2):
        first.append(
            (
                w.push(view(h, 2, 0, 2), in1.at[h, 0], to(h, 0, 1)),
                w.push(view(h, 2, 2, 2), in1.at[h, 1], to(h, 0, -1)),
            )
        )
    for h in range(2):
        loads.append(
            (
                w.local(view(h, 1, 0, 2), plus.at[h]),
                w.local(view(h, 3, 2, 2), minus.at[h]),
                w.local(view(h, 0, 0, 4), held.at[h]),
            )
        )
    early = []
    for h in range(2):
        early.append(
            (
                w.push(view(h, 1, 2, 2), in2.at[h, 0, pl.ds(2, 2)], to(h, 0, 1)),
                w.push(view(h, 3, 0, 2), in2.at[h, 1, pl.ds(0, 2)], to(h, 0, -1)),
            )
        )
    yield
    for h in range(2):
        loads[h][0].wait()
        first[h][0].wait_recv()
        for j in range(2):
            add_into(plus.at[h, j], in1.at[h, 0, j])
        one = w.push(plus.at[h], in2.at[h, 0, pl.ds(0, 2)], to(h, 0, 1))
        loads[h][1].wait()
        first[h][1].wait_recv()
        for j in range(2):
            add_into(minus.at[h, j], in1.at[h, 1, j])
        two = w.push(minus.at[h], in2.at[h, 1, pl.ds(2, 2)], to(h, 0, -1))
        second.append((one, two))
    yield
    third, early3 = [], []
    for h in range(2):
        loads[h][2].wait()
        for copy in early[h] + second[h]:
            copy.wait_recv()
        at = [(lanes[h][1] + k) % 4 for k in range(4)]
        add_into(held.at[h, at[2]], in2.at[h, 0, at[2]], in2.at[h, 1, at[2]])
        far = held.at[h, at[2]]
        third.append(
            (
                w.push(far.at[pl.ds(0, 32)], in3.at[h, 0], to(h, 1, 1)),
                w.push(far.at[pl.ds(32, 32)], in3.at[h, 1], to(h, 1, -1)),
            )
        )
        add_into(held.at[h, at[1]], in2.at[h, 0, at[1]], in2.at[h, 1, at[1]])
        one = w.push(held.at[h, at[1], pl.ds(32, 32)], in4.at[h, 0, pl.ds(32, 32)], to(h, 1, 1))
        add_into(held.at[h, at[3]], in2.at[h, 0, at[3]], in2.at[h, 1, at[3]])
        two = w.push(held.at[h, at[3], pl.ds(0, 32)], in4.at[h, 1, pl.ds(0, 32)], to(h, 1, -1))
        early3.append((one, two))
        add_into(held.at[h, at[0]], in2.at[h, 0, at[0]], in2.at[h, 1, at[0]])
    yield
    fourth = []
    for h in range(2):
        at = [(lanes[h][1] + k) % 4 for k in range(4)]
        third[h][0].wait_recv()
        piece = held.at[h, at[1], pl.ds(0, 32)]
        add_into(piece, in3.at[h, 0])
        one = w.push(piece, in4.at[h, 0, pl.ds(0, 32)], to(h, 1, 1))
        third[h][1].wait_recv()
        piece = held.at[h, at[3], pl.ds(32, 32)]
        add_into(piece, in3.at[h, 1])
        two = w.push(piece, in4.at[h, 1, pl.ds(32, 32)], to(h, 1, -1))
        fourth.append((one, two))
    yield
    for h in range(2):
        for copy in early3[h] + fourth[h]:
            copy.wait_recv()
        mine = held.at[h, lanes[h][1]]
        target = full.at[rows[h]]

        def body(r):
            total = mine[r, :].astype(F32) + in4[h, 0, r, :].astype(F32)
            target[r, :] = (total + in4[h, 1, r, :].astype(F32)).astype(BF)

        by_rows(64, 16, body)
    theirs = full.at[pl.ds(pl.multiple_of((1 - c) * 64, 64), 64)]
    mine = full.at[pl.ds(pl.multiple_of(c * 64, 64), 64)]
    swap = w.push(theirs, both.at[c], spot.dev(other=True))

    def keep(r):
        both[c, r, :] = mine[r, :]

    by_rows(64, 16, keep)
    swap.wait_recv()


def column_sum_scratch():
    return [
        pltpu.VMEM((4, 128, WIDTH), BF),
        pltpu.VMEM((4, 128, WIDTH), BF),
        pltpu.VMEM((2, 64, WIDTH), BF),
        pltpu.VMEM((2, 128, WIDTH), BF),
    ]


def column_sum(w, spot, part, scratch, finish, resident=False):
    own, got, in1, in2 = scratch
    x, c = spot.x, spot.c
    right, left = spot.dev(dx=1), spot.dev(dx=-1)
    places = [((x + k) % 4 % 2, (x + k) % 4 // 2) for k in range(4)]
    swaps, loads = {}, {}
    for k in (2, 1, 3, 0):
        swaps[k] = w.push(part.at[1 - c, places[k][0], places[k][1]], got.at[k], spot.dev(other=True))
    if resident:
        own = [part.at[c, lo, hi] for lo, hi in places]
    else:
        for k in (2, 1, 3, 0):
            loads[k] = w.local(part.at[c, places[k][0], places[k][1]], own.at[k])
        own = [own.at[k] for k in range(4)]
    yield

    def merge(k):
        if not resident:
            loads[k].wait()
        swaps[k].wait_recv()
        add_into(own[k], got.at[k])

    low, high = pl.ds(0, 64), pl.ds(64, 64)
    merge(2)
    far1 = w.push(own[2].at[low], in1.at[0], right)
    far2 = w.push(own[2].at[high], in1.at[1], left)
    merge(1)
    one = w.push(own[1].at[high], in2.at[0, high], right)
    merge(3)
    two = w.push(own[3].at[low], in2.at[1, low], left)
    merge(0)
    yield
    far1.wait_recv()
    add_into(own[1].at[low], in1.at[0])
    three = w.push(own[1].at[low], in2.at[0, low], right)
    far2.wait_recv()
    add_into(own[3].at[high], in1.at[1])
    four = w.push(own[3].at[high], in2.at[1, high], left)
    yield
    for copy in (one, two, three, four):
        copy.wait_recv()

    def total(rows):
        return own[0][rows, :].astype(F32) + in2[0, rows, :].astype(F32) + in2[1, rows, :].astype(F32)

    finish(total)


def column_share(w, spot, mine, out):
    x, c = spot.x, spot.c
    right, left, mate = spot.dev(dx=1), spot.dev(dx=-1), spot.dev(other=True)

    def slot(k):
        at = (x + k + 4) % 4
        return out.at[c, at % 2, at // 2]

    low, high = pl.ds(0, 64), pl.ds(64, 64)
    own = w.local(mine, slot(0))
    a = w.push(mine, slot(0), right)
    b = w.push(mine, slot(0), left)
    d = w.push(mine, slot(0), mate)
    yield
    a.wait_recv()
    e = w.push(slot(-1).at[low], slot(-1).at[low], right)
    f = w.push(slot(-1), slot(-1), mate)
    b.wait_recv()
    g = w.push(slot(1).at[high], slot(1).at[high], left)
    h = w.push(slot(1), slot(1), mate)
    yield
    e.wait_recv()
    i = w.push(slot(2).at[low], slot(2).at[low], mate)
    g.wait_recv()
    j = w.push(slot(2).at[high], slot(2).at[high], mate)
    yield
    own.wait()
    for copy in (d, f, h, i, j):
        copy.wait_recv()


def token_share(w, spot, block, out):
    own_at, far_at = spot.c * 2 + spot.lo, spot.c * 2 + 1 - spot.lo
    right, left, mate = spot.dev(dx=1), spot.dev(dx=-1), spot.dev(other=True)
    low, high = pl.ds(0, 128), pl.ds(128, 128)
    own = w.local(block, out.at[own_at])
    a = w.push(block.at[low], out.at[own_at, low], right)
    b = w.push(block.at[high], out.at[own_at, high], left)
    d = w.push(block, out.at[own_at], mate)
    yield
    a.wait_recv()
    part = out.at[far_at, low]
    e = w.push(part, part, mate)
    b.wait_recv()
    part = out.at[far_at, high]
    f = w.push(part, part, mate)
    yield
    own.wait()
    for copy in (d, e, f):
        copy.wait_recv()


def pair_share(w, spot, mine, out):
    own = w.local(mine, out.at[spot.hi])
    a = w.push(mine, out.at[spot.hi], spot.dev(dx=2))
    yield
    own.wait()
    a.wait_recv()


def neighbours(spot, x=False, yz=False, core=False, pair=False, far=False):
    found = []
    if x:
        found += [spot.dev(dx=1), spot.dev(dx=-1)]
    if yz:
        found += [spot.dev(dy=1), spot.dev(dy=-1), spot.dev(dz=1), spot.dev(dz=-1)]
    if core:
        found += [spot.dev(other=True)]
    if pair:
        found += [spot.dev(dx=2)]
    if far:
        found += [spot.dev(dy=2), spot.dev(dz=2)]
    return found


BLOCK = 256
SPAN = COLUMN + BLOCK
NT = (((1,), (1,)), ((), ()))
TN = (((0,), (0,)), ((), ()))
NN = (((1,), (0,)), ((), ()))


def dot(a, b, dims):
    return lax.dot_general(a, b, dims, preferred_element_type=F32)


def rms_of(rows):
    inverse = lax.rsqrt(jnp.mean(rows * rows, axis=-1, keepdims=True) + EPS)
    return rows * inverse, inverse


def turn_half(rows):
    half = HEAD // 2
    return jnp.concatenate([-rows[:, half:], rows[:, :half]], axis=-1)


def params(collective_id):
    return pltpu.CompilerParams(
        collective_id=collective_id, has_side_effects=True, vmem_limit_bytes=LIMIT
    )


def own_block(ref, spot):
    return ref.at[spot.c, spot.lo, spot.hi]


def place_rows(spot, lengths, freq, doc_row, doc_col, cosine, sine):
    first = (spot.y * 4 + spot.z - 1) * COLUMN
    rows = lax.broadcasted_iota(jnp.int32, (16, 128), 0) * 128 + first
    rows = rows + lax.broadcasted_iota(jnp.int32, (16, 128), 1)
    document = jnp.zeros((16, 128), jnp.int32)
    start = jnp.zeros((16, 128), jnp.int32)
    bound = jnp.int32(0)
    for d in range(lengths.shape[1]):
        bound = bound + lengths[0, d]
        passed = rows >= bound
        document = document + passed.astype(jnp.int32)
        start = jnp.where(passed, bound, start)
    document = jnp.where(rows >= 0, document, -1).astype(F32)
    place = (rows - start).astype(F32)
    for g in range(16):
        line = document[g : g + 1, :]
        at = slice(g * 128, (g + 1) * 128)
        doc_row[:, at] = line
        doc_col[at, :] = jnp.transpose(jnp.broadcast_to(line, (128, 128)))
        if g >= 8:
            down = jnp.transpose(jnp.broadcast_to(place[g : g + 1, :], (128, 128)))
            angles = down * freq[...]
            at = slice((g - 8) * 128, (g - 7) * 128)
            cosine[at, :] = jnp.cos(angles)
            sine[at, :] = jnp.sin(angles)


def turned_head(raw, scale, cosine, sine):
    unit = rms_of(raw)[0] * scale
    return (unit * cosine + turn_half(unit) * sine).astype(BF)


def forward_kernel(
    tok, cot, pack_a, pack_w, pack_b, lengths, freq, q_gain, k_gain,
    normed1, w_a, w_w, w_b, cot_all, raw, query, kv, before, attended, inverse, mid, normed2, cosine, sine, gains, doc_row, doc_col,
    tok_all, low1, roots, top, total, branch, got, in1, in2, low, send, recv, here,
):
    spot = Spot()
    greet(neighbours(spot, x=True, yz=True, core=True) + [spot.column(1), spot.column(-1)])
    w = Wires(send, recv, here)
    take_a = plane_gather(w, spot, pack_a, w_a)
    take_w = plane_gather(w, spot, pack_w, w_w)
    take_b = plane_gather(w, spot, pack_b, w_b)
    take_tok = token_share(w, spot, tok, tok_all)
    take_cot = token_share(w, spot, cot, cot_all)

    def go(*parts):
        for part in parts:
            next(part, None)

    go(take_a, take_tok, take_w, take_b, take_a)
    place_rows(spot, lengths, freq, doc_row, doc_col, cosine, sine)
    go(take_a, take_tok, take_a, take_tok)

    def roots_of(i, _):
        rows = pl.ds(pl.multiple_of(i * 32, 32), 32)
        values = tok_all[i // 8, pl.ds(pl.multiple_of(i % 8 * 32, 32), 32), :].astype(F32)
        roots[rows, :] = lax.rsqrt(jnp.mean(values * values, axis=-1, keepdims=True) + EPS)
        return 0

    lax.fori_loop(0, 32, roots_of, 0)
    go(take_a, take_w, take_a)
    go(take_cot, take_b)
    for i in range(16):
        block = jnp.transpose(w_a[i // 4, i % 4, :, 512:640].astype(F32))
        gains[:, i * 128 : (i + 1) * 128] = block[0:2, :]

    def norm_rows(i, _):
        rows = pl.ds(pl.multiple_of(i * 32, 32), 32)
        values = tok_all[i // 8, pl.ds(pl.multiple_of(i % 8 * 32, 32), 32), :].astype(F32)
        low1[rows, :] = (values * roots[rows, :] * gains[0:1, :]).astype(BF)
        return 0

    lax.fori_loop(0, 32, norm_rows, 0)
    keep = w.local(low1, normed1)

    def project_kv(i, _):
        rows = pl.ds(pl.multiple_of(i * BLOCK, BLOCK), BLOCK)
        out = dot(low1[rows, :], w_a[:, :, :, 256:512].reshape(WIDTH, 256), NN)
        raw[rows, 256:512] = out
        kv[rows, :HEAD] = turned_head(out[:, :HEAD], k_gain[...].astype(F32), cosine[rows, :], sine[rows, :])
        kv[rows, HEAD:] = out[:, HEAD:].astype(BF)
        return 0

    def project_q(i, _):
        rows = pl.ds(pl.multiple_of(i * BLOCK, BLOCK), BLOCK)
        out = dot(low1[rows, :], w_a[:, :, :, 0:256].reshape(WIDTH, 256), NN)
        raw[rows, 0:256] = out
        for h in range(2):
            span = slice(h * HEAD, (h + 1) * HEAD)
            query[rows, span] = turned_head(out[:, span], q_gain[...].astype(F32), cosine[rows, :], sine[rows, :])
        return 0

    lax.fori_loop(0, 4, project_kv, 0)
    pass_kv = w.push(kv, before, spot.column(1))
    go(take_w, take_b)
    lax.fori_loop(0, 4, project_q, 0)
    go(take_cot)

    def weights_of(i, h, keys, docs, causal):
        rows = slice(i * BLOCK, (i + 1) * BLOCK)
        scores = dot(query[rows, h * HEAD : (h + 1) * HEAD], keys, NT) * SCALE
        valid = doc_col[COLUMN + i * BLOCK : COLUMN + (i + 1) * BLOCK, 0:1] == docs
        if causal:
            row = lax.broadcasted_iota(jnp.int32, scores.shape, 0) + i * BLOCK
            valid = valid & (lax.broadcasted_iota(jnp.int32, scores.shape, 1) <= row)
        return jnp.where(valid, jnp.exp(scores), 0.0)

    for i in range(4):
        rows, end = slice(i * BLOCK, (i + 1) * BLOCK), (i + 1) * BLOCK
        for h in range(2):
            weight = weights_of(i, h, kv[0:end, :HEAD], doc_row[:, COLUMN : COLUMN + end], True)
            total[rows, h : h + 1] = jnp.sum(weight, axis=-1, keepdims=True)
            top[rows, h * HEAD : (h + 1) * HEAD] = dot(weight.astype(BF), kv[0:end, HEAD:], NN)
        if i == 1:
            go(take_w)
    pass_kv.wait_recv()
    go(take_w, take_b)
    for i in range(4):
        rows, low_key = slice(i * BLOCK, (i + 1) * BLOCK), i * BLOCK
        for h in range(2):
            span = slice(h * HEAD, (h + 1) * HEAD)
            weight = weights_of(i, h, before[low_key:, :HEAD], doc_row[:, low_key:COLUMN], False)
            back = 1.0 / (total[rows, h : h + 1] + jnp.sum(weight, axis=-1, keepdims=True))
            inverse[rows, h : h + 1] = back
            attended[rows, span] = ((top[rows, span] + dot(weight.astype(BF), before[low_key:, HEAD:], NN)) * back).astype(BF)
    go(take_w)

    def branch_of(core):
        def one(lo, _):
            rows = pl.ds(pl.multiple_of((core * 2 + lo) * BLOCK, BLOCK), BLOCK)
            out = dot(attended[rows, :], w_w[...].reshape(WIDTH, 256), NT)
            branch[core, lo] = out.astype(BF).reshape(2, 128, WIDTH)
            return 0

        lax.fori_loop(0, 2, one, 0)

    def finish(add):
        def body(rows):
            base = tok[pl.ds(pl.multiple_of(spot.hi * 128 + rows.start, 16), 16), :].astype(F32)
            middle = base + add(rows)
            mid[rows, :] = middle
            root = lax.rsqrt(jnp.mean(middle * middle, axis=-1, keepdims=True) + EPS)
            low[rows, :] = (middle * root * gains[1:2, :]).astype(BF)

        by_rows(128, 16, body)

    branch_of(1 - spot.c)
    fold = column_sum(w, spot, branch, (None, got, in1, in2), finish, resident=True)
    go(fold)
    branch_of(spot.c)
    go(fold, fold, fold, take_cot)
    share = column_share(w, spot, low, normed2)
    go(share, take_b, share, share, take_b, share)
    keep.wait()
    w.drain()


def forward_call(tok, cot, pack_a, pack_w, pack_b, lengths, freq, q_gain, k_gain):
    def gathered(pack):
        return jax.ShapeDtypeStruct((4, 4, 128, pack.shape[-1]), BF)

    def shape(*sizes, kind=BF):
        return jax.ShapeDtypeStruct(sizes, kind)

    outs = (
        (shape(COLUMN, WIDTH), HBM),
        (gathered(pack_a), VMEM),
        (gathered(pack_w), VMEM),
        (gathered(pack_b), HBM),
        (shape(4, 256, WIDTH), HBM),
        (shape(COLUMN, 512, kind=F32), VMEM),
        (shape(COLUMN, 256), VMEM),
        (shape(COLUMN, 256), VMEM),
        (shape(COLUMN, 256), VMEM),
        (shape(COLUMN, 256), VMEM),
        (shape(COLUMN, 2, kind=F32), VMEM),
        (shape(128, WIDTH, kind=F32), VMEM),
        (shape(2, 2, 2, 128, WIDTH), HBM),
        (shape(COLUMN, HEAD, kind=F32), VMEM),
        (shape(COLUMN, HEAD, kind=F32), VMEM),
        (shape(2, WIDTH, kind=F32), VMEM),
        (shape(1, 2 * COLUMN, kind=F32), VMEM),
        (shape(2 * COLUMN, 128, kind=F32), VMEM),
    )
    return pl.pallas_call(
        forward_kernel,
        out_shape=tuple(o[0] for o in outs),
        in_specs=[VMEM] * 5 + [pl.BlockSpec(memory_space=pltpu.SMEM)] + [VMEM] * 3,
        out_specs=tuple(o[1] for o in outs),
        scratch_shapes=[
            pltpu.VMEM((4, 256, WIDTH), BF),
            pltpu.VMEM((COLUMN, WIDTH), BF),
            pltpu.VMEM((COLUMN, 1), F32),
            pltpu.VMEM((COLUMN, 256), F32),
            pltpu.VMEM((COLUMN, 2), F32),
            pltpu.VMEM((2, 2, 2, 128, WIDTH), BF),
        ]
        + column_sum_scratch()[1:]
        + [pltpu.VMEM((128, WIDTH), BF)]
        + wires_scratch(96, 12),
        compiler_params=params(1),
        name="forward",
    )(tok, cot, pack_a, pack_w, pack_b, lengths, freq, q_gain, k_gain)


def rms_back(total, base, gain, rows, extra, out, gain_grad):
    values = base[rows, :].astype(F32)
    inverse = lax.rsqrt(jnp.mean(values * values, axis=-1, keepdims=True) + EPS)
    normed = values * inverse
    grad = total(rows)
    scaled = grad * gain[...]
    back = inverse * (scaled - normed * jnp.mean(scaled * normed, axis=-1, keepdims=True))
    gain_grad[...] += jnp.sum(grad * normed, axis=0, keepdims=True)
    out[rows, :] = extra[rows, :].astype(F32) + back


def turn_kernel(
    dnorm, mixed, mid, cot, gain, grads, dmid, dbranch, out, gain_grad, both,
    s0, s1, s2, s3, t0, t1, t2, t3, top, low, result, p0, p1, p2, p3, p4, p5, p6, p7, p8, send, recv, here,
):
    spot = Spot()
    greet(neighbours(spot, x=True, yz=True, core=True))
    w = Wires(send, recv, here)
    load = w.local(own_block(cot, spot), top)
    gain_grad[...] = jnp.zeros_like(gain_grad)

    def finish_norm(total):
        load.wait()

        def body(rows):
            rms_back(total, mid, gain, rows, top, dmid, gain_grad)
            low[rows, :] = dmid[rows, :].astype(BF)

        by_rows(128, 16, body)

    def finish_out(total):
        def body(rows):
            result[rows, :] = (mid[rows, :] + total(rows)).astype(BF)

        by_rows(128, 16, body)

    def back():
        yield from column_sum(w, spot, dnorm, (s0, s1, s2, s3), finish_norm)
        yield from column_share(w, spot, low, dbranch)

    def forth():
        yield
        yield
        yield from column_sum(w, spot, mixed, (t0, t1, t2, t3), finish_out)

    scratch = (p0, p1, p2, p3, p4, p5, p6, p7, p8)
    run_all(back(), plane_sum(w, spot, grads, scratch), forth())
    first = w.local(result, out)
    second = w.local(p8, both)
    first.wait()
    second.wait()
    w.drain()


def turn_call(dnorm, mixed, mid, cot, gain, grads):
    blocks = jax.ShapeDtypeStruct((2, 2, 2, 128, WIDTH), BF)
    columns = grads.shape[-1]
    return pl.pallas_call(
        turn_kernel,
        out_shape=(
            jax.ShapeDtypeStruct((128, WIDTH), F32),
            blocks,
            jax.ShapeDtypeStruct((128, WIDTH), BF),
            jax.ShapeDtypeStruct((1, WIDTH), F32),
            jax.ShapeDtypeStruct((2, 64, columns), BF),
        ),
        in_specs=[HBM, HBM, VMEM, HBM, VMEM, HBM],
        out_specs=(VMEM, HBM, HBM, VMEM, HBM),
        scratch_shapes=column_sum_scratch()
        + column_sum_scratch()
        + [pltpu.VMEM((128, WIDTH), BF)] * 3
        + plane_sum_scratch(columns)
        + wires_scratch(64, 24),
        compiler_params=params(4),
        name="turn",
    )(dnorm, mixed, mid, cot, gain, grads)


def back_column_kernel(block, result, both, came, out, whole, send, recv, here):
    spot = Spot()
    greet([spot.column(1), spot.column(-1), spot.dev(dx=2), spot.dp_mate()])
    w = Wires(send, recv, here)
    a = w.push(block, came, spot.column(-1))
    own = w.local(both, whole.at[spot.lo])
    b = w.push(both, whole.at[spot.lo], spot.dp_mate())
    run_all(pair_share(w, spot, result, out))
    own.wait()
    a.wait_recv()
    b.wait_recv()
    w.drain()


def back_column_call(block, result, both):
    return pl.pallas_call(
        back_column_kernel,
        out_shape=(
            jax.ShapeDtypeStruct(block.shape, block.dtype),
            jax.ShapeDtypeStruct((2, 128, WIDTH), BF),
            jax.ShapeDtypeStruct((2,) + both.shape, BF),
        ),
        in_specs=[HBM, VMEM, VMEM],
        out_specs=(HBM,) * 3,
        scratch_shapes=wires_scratch(4, 4),
        compiler_params=params(5),
        name="back_column",
    )(block, result, both)


def sum_everywhere(w, spot, vector, pair, lines):
    a = w.push(vector, pair, spot.dev(other=True))
    yield
    a.wait_recv()
    w.sent_now(a)
    vector[...] = vector[...] + pair[...]
    yield
    for stage, (axis, at) in enumerate((("dx", spot.x), ("dy", spot.y), ("dz", spot.z))):
        slots = lines.at[stage]
        slots[at] = vector[...]
        copies = [w.push(vector, slots.at[at], spot.dev(**{axis: k})) for k in (1, 2, 3)]
        yield
        for copy in copies:
            copy.wait_recv()
            w.sent_now(copy)
        vector[...] = slots[0] + slots[1] + slots[2] + slots[3]
        yield


def close_kernel(
    dnorm, tok, gain, dmid, grads, small, gtok, whole, vector,
    s0, s1, s2, s3, base, final, gain_grad, low, theirs, p0, p1, p2, p3, p4, p5, p6, p7, p8, pair, lines,
    send, recv, here,
):
    spot = Spot()
    mates = neighbours(spot, x=True, yz=True, core=True, pair=True, far=True)
    greet(mates)
    w = Wires(send, recv, here)
    load = w.local(tok.at[spot.hi], base)
    gain_grad[...] = jnp.zeros_like(gain_grad)

    def finish(total):
        load.wait()

        def body(rows):
            rms_back(total, base, gain, rows, dmid, final, gain_grad)
            low[rows, :] = final[rows, :].astype(BF)

        by_rows(128, 16, body)

    def back():
        yield from column_sum(w, spot, dnorm, (s0, s1, s2, s3), finish)
        sent = w.push(low, theirs, spot.dev(dx=2))
        vector[...] = small[...]
        for i in range(16):
            vector[i : i + 1, :] = gain_grad[:, i * 128 : (i + 1) * 128]
        yield from sum_everywhere(w, spot, vector, pair, lines)
        by_rows(128, 16, lambda rows: final.__setitem__((rows, slice(None)), low[rows, :].astype(F32)))
        one = w.local(final, gtok.at[spot.hi])
        sent.wait_recv()
        one.wait()
        by_rows(128, 16, lambda rows: final.__setitem__((rows, slice(None)), theirs[rows, :].astype(F32)))
        two = w.local(final, gtok.at[1 - spot.hi])
        two.wait()

    def weights():
        yield from plane_sum(w, spot, grads, (p0, p1, p2, p3, p4, p5, p6, p7, p8))
        own = w.local(p8, whole.at[spot.lo])
        a = w.push(p8, whole.at[spot.lo], spot.dp_mate())
        yield
        own.wait()
        a.wait_recv()

    run_all(back(), weights())
    w.drain()


def close_call(dnorm, tok, gain, dmid, grads, small):
    columns = grads.shape[-1]
    rows = small.shape[0]
    return pl.pallas_call(
        close_kernel,
        out_shape=(
            jax.ShapeDtypeStruct((2, 128, WIDTH), F32),
            jax.ShapeDtypeStruct((2, 2, 64, columns), BF),
            jax.ShapeDtypeStruct((rows, 128), F32),
        ),
        in_specs=[HBM, HBM, VMEM, VMEM, HBM, VMEM],
        out_specs=(HBM, HBM, VMEM),
        scratch_shapes=column_sum_scratch()
        + [
            pltpu.VMEM((128, WIDTH), BF),
            pltpu.VMEM((128, WIDTH), F32),
            pltpu.VMEM((1, WIDTH), F32),
            pltpu.VMEM((128, WIDTH), BF),
            pltpu.VMEM((128, WIDTH), BF),
        ]
        + plane_sum_scratch(columns)
        + [pltpu.VMEM((rows, 128), F32), pltpu.VMEM((3, 4, rows, 128), F32)]
        + wires_scratch(64, 24),
        compiler_params=params(6),
        name="close",
    )(dnorm, tok, gain, dmid, grads, small)


def local_params():
    return pltpu.CompilerParams(vmem_limit_bytes=LIMIT)


def rows_spec(columns):
    return pl.BlockSpec((BLOCK, columns), lambda i: (i, 0))


def as_row(column):
    return jnp.transpose(jnp.broadcast_to(column, (column.shape[0], HEAD)))[0:1, :]


def attend_back_kernel(
    d_branch, weights, attended, q, before, own, doc_q, doc_k, inverse, dq, dkv, kv
):
    @pl.when(pl.program_id(0) == 0)
    def _():
        kv[0:COLUMN, :] = before[...]
        kv[COLUMN:, :] = own[...]
        dkv[...] = jnp.zeros_like(dkv)

    do = dot(d_branch[...], weights[...], NN).astype(BF)
    product = attended[...].astype(F32) * do.astype(F32)
    start = pl.multiple_of(pl.program_id(0) * BLOCK, BLOCK)
    keys = kv[pl.ds(start, SPAN), 0:HEAD]
    values = kv[pl.ds(start, SPAN), HEAD:]
    row = lax.broadcasted_iota(jnp.int32, (SPAN, BLOCK), 0)
    col = lax.broadcasted_iota(jnp.int32, (SPAN, BLOCK), 1)
    valid = (doc_k[pl.ds(start, SPAN), 0:1] == doc_q[...]) & (row <= col + COLUMN)
    for h in range(2):
        span = slice(h * HEAD, (h + 1) * HEAD)
        query = q[:, span]
        upstream = do[:, span]
        back = as_row(inverse[:, h : h + 1])
        delta = as_row(jnp.sum(product[:, span], axis=-1, keepdims=True))
        scores = dot(keys, query, NT) * SCALE
        probs = jnp.where(valid, jnp.exp(scores), 0.0) * back
        d_probs = dot(values, upstream, NT)
        d_scores = (probs * (d_probs - delta)).astype(BF)
        dkv[pl.ds(start, SPAN), 0:HEAD] += dot(d_scores, query, NN) * SCALE
        dkv[pl.ds(start, SPAN), HEAD:] += dot(probs.astype(BF), upstream, NN)
        dq[:, span] = dot(d_scores, keys, TN) * SCALE


def attend_back_call(d_branch, weights, attended, q, before, own, doc_q, doc_k, inverse):
    return pl.pallas_call(
        attend_back_kernel,
        grid=(COLUMN // BLOCK,),
        out_shape=(
            jax.ShapeDtypeStruct((COLUMN, 2 * HEAD), F32),
            jax.ShapeDtypeStruct((2 * COLUMN, 2 * HEAD), F32),
        ),
        in_specs=[
            rows_spec(WIDTH),
            VMEM,
            rows_spec(2 * HEAD),
            rows_spec(2 * HEAD),
            VMEM,
            VMEM,
            pl.BlockSpec((1, BLOCK), lambda i: (0, i + COLUMN // BLOCK)),
            VMEM,
            rows_spec(2),
        ],
        out_specs=(rows_spec(2 * HEAD), VMEM),
        scratch_shapes=[pltpu.VMEM((2 * COLUMN, 2 * HEAD), BF)],
        compiler_params=local_params(),
        name="attend_back",
    )(d_branch, weights, attended, q, before, own, doc_q, doc_k, inverse)


def hidden_kernel(normed, cot, weights, mixed, d_norm, hidden, d_both):
    low, up_rows = normed[...], cot[...]
    for j in range(3):
        a = slice(j * 256, (j + 1) * 256)
        b = slice(768 + j * 256, 1024 + j * 256)
        d = slice(1536 + j * 256, 1792 + j * 256)
        gate = dot(low, weights[:, a], NN)
        up = dot(low, weights[:, b], NN)
        d_hidden = dot(up_rows, weights[:, d], NN)
        sigma = lax.logistic(gate)
        active = gate * sigma
        hidden[:, a] = (active * up).astype(BF)
        d_both[:, a] = (d_hidden * up * sigma * (1.0 + gate * (1.0 - sigma))).astype(BF)
        d_both[:, b] = (d_hidden * active).astype(BF)
    mixed[...] = dot(hidden[...], weights[:, 1536:], NT).astype(BF)
    d_norm[...] = dot(d_both[...], weights[:, :1536], NT).astype(BF)


def hidden_call(normed, cot, weights):
    return pl.pallas_call(
        hidden_kernel,
        grid=(COLUMN // BLOCK,),
        out_shape=(
            jax.ShapeDtypeStruct((COLUMN, WIDTH), BF),
            jax.ShapeDtypeStruct((COLUMN, WIDTH), BF),
            jax.ShapeDtypeStruct((COLUMN, 768), BF),
            jax.ShapeDtypeStruct((COLUMN, 1536), BF),
        ),
        in_specs=[rows_spec(WIDTH), rows_spec(WIDTH), VMEM],
        out_specs=(rows_spec(WIDTH), rows_spec(WIDTH), rows_spec(768), rows_spec(1536)),
        compiler_params=local_params(),
        name="hidden",
    )(normed, cot, weights)


def two_grads_kernel(left1, right1, left2, right2, out):
    n = right1.shape[1]
    out[:, :n] = dot(left1[...], right1[...], TN).astype(BF)
    out[:, n:] = dot(left2[...], right2[...], TN).astype(BF)


def two_grads_call(left1, right1, left2, right2):
    tile = pl.BlockSpec((COLUMN, BLOCK), lambda i: (0, i))
    columns = right1.shape[1] + right2.shape[1]
    return pl.pallas_call(
        two_grads_kernel,
        grid=(WIDTH // BLOCK,),
        out_shape=jax.ShapeDtypeStruct((WIDTH, columns), BF),
        in_specs=[tile, VMEM, tile, VMEM],
        out_specs=rows_spec(columns),
        compiler_params=local_params(),
        name="two_grads",
    )(left1, right1, left2, right2)


def project_back_kernel(
    dq, dkv, came, raw, weights, q_gain, k_gain, cosine, sine, d_raw, d_norm, gain_grads
):
    @pl.when(pl.program_id(0) == 0)
    def _():
        gain_grads[...] = jnp.zeros_like(gain_grads)

    for h, scale in enumerate((q_gain, q_gain, k_gain)):
        span = slice(h * HEAD, (h + 1) * HEAD)
        if h < 2:
            grad = dq[:, span]
        else:
            grad = dkv[:, :HEAD] + came[:, :HEAD].astype(F32)
        grad = grad * cosine[...] - turn_half(grad) * sine[...]
        unit, inverse = rms_of(raw[:, span])
        scaled = grad * scale[...]
        back = inverse * (scaled - unit * jnp.mean(scaled * unit, axis=-1, keepdims=True))
        d_raw[:, span] = back.astype(BF)
        at = h // 2
        gain_grads[at : at + 1, :] += jnp.sum(grad * unit, axis=0, keepdims=True)
    d_raw[:, 3 * HEAD :] = (dkv[:, HEAD:] + came[:, HEAD:].astype(F32)).astype(BF)
    d_norm[...] = dot(d_raw[...], weights[:, :512], NT).astype(BF)


def project_back_call(dq, dkv, came, raw, weights, q_gain, k_gain, cosine, sine):
    own = pl.BlockSpec((BLOCK, 2 * HEAD), lambda i: (i + COLUMN // BLOCK, 0))
    return pl.pallas_call(
        project_back_kernel,
        grid=(COLUMN // BLOCK,),
        out_shape=(
            jax.ShapeDtypeStruct((COLUMN, 4 * HEAD), BF),
            jax.ShapeDtypeStruct((COLUMN, WIDTH), BF),
            jax.ShapeDtypeStruct((8, HEAD), F32),
        ),
        in_specs=[
            rows_spec(2 * HEAD),
            own,
            rows_spec(2 * HEAD),
            rows_spec(4 * HEAD),
            VMEM,
            VMEM,
            VMEM,
            rows_spec(HEAD),
            rows_spec(HEAD),
        ],
        out_specs=(rows_spec(4 * HEAD), rows_spec(WIDTH), VMEM),
        compiler_params=local_params(),
        name="project_back",
    )(dq, dkv, came, raw, weights, q_gain, k_gain, cosine, sine)


def mine_of(weight, dp):
    rows, columns = weight.shape
    quarter = lax.dynamic_slice_in_dim(weight, dp * (columns // 2), columns // 2, 1)
    return quarter.reshape(rows, 2, columns // 4).transpose(1, 0, 2)


def on_device(
    tokens, lengths, attn_norm, w_query, w_key, w_value, w_output, q_gain, k_gain, mlp_norm, w_gate, w_up, w_down, cotangent,
):
    shard = lax.axis_index("shard")
    dp = lax.axis_index("dp")
    freq = THETA ** (-jnp.arange(0, HEAD, 2).astype(F32) / HEAD)
    freq = jnp.concatenate([freq, freq])[None]
    gains = jnp.pad(jnp.stack([attn_norm, mlp_norm], axis=1), ((0, 0), (0, 126)))
    pack_a = jnp.concatenate(
        [mine_of(w_query, dp), mine_of(w_key, dp), mine_of(w_value, dp), jnp.stack([gains, gains])], axis=-1
    )
    pack_w = mine_of(w_output.T, dp)
    pack_b = jnp.concatenate([mine_of(w_gate, dp), mine_of(w_up, dp), mine_of(w_down.T, dp)], axis=-1)
    (
        normed1, w_a, w_w, w_b, cot, raw, query, kv, before, attended, inverse, middle, normed2, cosine, sine, gains, doc_row, doc_col,
    ) = forward_call(tokens, cotangent, pack_a, pack_w, pack_b, lengths, freq, q_gain[None], k_gain[None])
    w_a, w_w, w_b = w_a.reshape(WIDTH, 640), w_w.reshape(WIDTH, 256), w_b.reshape(WIDTH, 2304)
    attn_gain, mlp_gain = gains[0:1], gains[1:2]
    q_scale, k_scale = q_gain.astype(F32)[None], k_gain.astype(F32)[None]
    blocks = (2, 2, 2, 128, WIDTH)
    normed2 = normed2.reshape(COLUMN, WIDTH)
    cot_rows = cot.reshape(COLUMN, WIDTH)
    mixed, d_norm2, hidden, d_both = hidden_call(normed2, cot_rows, w_b)
    grads2 = two_grads_call(normed2, d_both, cot_rows, hidden).reshape(4, 4, 128, 2304)
    d_middle, d_branch, result, g_mlp, both2 = turn_call(
        d_norm2.reshape(blocks), mixed.reshape(blocks), middle, cot.reshape(blocks), mlp_gain, grads2
    )
    d_branch = d_branch.reshape(COLUMN, WIDTH)
    d_query, d_kv = attend_back_call(
        d_branch, w_w, attended, query, before, kv, doc_row, doc_col, inverse
    )
    came, out, whole2 = back_column_call(d_kv[:COLUMN].astype(BF), result, both2)
    d_qkv, d_norm1, g_gain = project_back_call(
        d_query, d_kv, came, raw, w_a, q_scale, k_scale, cosine, sine
    )
    grads1 = two_grads_call(normed1, d_qkv, d_branch, attended).reshape(4, 4, 128, 768)
    small = jnp.concatenate([jnp.zeros((16, 128), F32), g_mlp.reshape(16, 128), g_gain], axis=0)
    g_tokens, whole1, sums = close_call(
        d_norm1.reshape(blocks), tokens.reshape(2, 128, WIDTH), attn_gain, d_middle, grads1, small
    )

    def spread(whole, low, size):
        piece = whole[..., low : low + size].astype(F32)
        return piece.transpose(2, 0, 1, 3).reshape(64, 4 * size)

    def rows_of(block):
        return lax.dynamic_slice_in_dim(block.reshape(WIDTH), shard * 64, 64)

    return (
        out.reshape(256, WIDTH),
        g_tokens.reshape(256, WIDTH),
        rows_of(sums[0:16]),
        spread(whole1, 0, 256),
        spread(whole1, 256, 128),
        spread(whole1, 384, 128),
        spread(whole1, 512, 256).T,
        sums[32],
        sums[33],
        rows_of(sums[16:32]),
        spread(whole2, 0, 768),
        spread(whole2, 768, 768),
        spread(whole2, 1536, 768).T,
    )


def solution(mesh):
    rows = P(("shard", "dp"), None)
    down = P("shard", "tensor")
    across = P("tensor", "shard")
    one = P("shard")
    return jax.shard_map(
        on_device,
        mesh=mesh,
        in_specs=(rows, P(), one, down, down, down, across, P(), P(), one, down, down, across, rows),
        out_specs=(rows, rows, one, down, down, down, across, P(), P(), one, down, down, across),
        check_vma=False,
    )
```

```python
import functools

import jax
import jax.numpy as jnp
from jax import lax
from jax.experimental import pallas as pl
from jax.experimental.pallas import tpu as pltpu
from jax.sharding import PartitionSpec as P

HEAD = 128
EPS = 1e-06
THETA = 1000000.0
SCALE = HEAD ** (-0.5)
WIDTH = 2048
COLUMN = 1024
MESH = pl.DeviceIdType.MESH
BF = jnp.bfloat16
F32 = jnp.float32
HBM = pl.BlockSpec(memory_space=pl.ANY)
VMEM = pl.BlockSpec(memory_space=pltpu.VMEM)
LIMIT = 60 * 2**20


class Spot:
    def __init__(self):
        shard = lax.axis_index("shard")
        self.lo = lax.axis_index("dp")
        self.hi = lax.axis_index("tensor")
        self.x = self.hi * 2 + self.lo
        self.y = shard // 8
        self.z = (shard // 2) % 4
        self.c = shard % 2

    def dev(self, dx=0, dy=0, dz=0, other=False):
        x = (self.x + dx) % 4
        y = (self.y + dy) % 4
        z = (self.z + dz) % 4
        c = 1 - self.c if other else self.c
        return ((y * 4 + z) * 2 + c, x % 2, x // 2)

    def dp_mate(self):
        return ((self.y * 4 + self.z) * 2 + self.c, 1 - self.lo, self.hi)

    def column(self, step):
        flat = (self.y * 4 + self.z + step + 16) % 16
        return (flat * 2 + self.c, self.lo, self.hi)


def greet(devices):
    barrier = pltpu.get_barrier_semaphore()
    for device in devices:
        pl.semaphore_signal(barrier, inc=1, device_id=device, device_id_type=MESH)
    pl.semaphore_wait(barrier, len(devices))


class Wires:
    def __init__(self, send, recv, local):
        self.send, self.recv, self.here = send, recv, local
        self.count, self.near = 0, 0
        self.sent = []

    def push(self, src, dst, device):
        i = self.count
        self.count += 1
        copy = pltpu.make_async_remote_copy(
            src_ref=src,
            dst_ref=dst,
            send_sem=self.send.at[i],
            recv_sem=self.recv.at[i],
            device_id=device,
            device_id_type=MESH,
        )
        copy.start()
        self.sent.append(copy)
        return copy

    def local(self, src, dst):
        copy = pltpu.make_async_copy(src, dst, self.here.at[self.near])
        self.near += 1
        copy.start()
        return copy

    def sent_now(self, copy):
        copy.wait_send()
        self.sent = [other for other in self.sent if other is not copy]

    def drain(self):
        for copy in self.sent:
            copy.wait_send()


def wires_scratch(remote, local):
    return [
        pltpu.SemaphoreType.DMA((remote,)),
        pltpu.SemaphoreType.DMA((remote,)),
        pltpu.SemaphoreType.DMA((max(local, 1),)),
    ]


def by_rows(count, step, body):
    def run(i, _):
        body(pl.ds(pl.multiple_of(i * step, step), step))
        return 0

    lax.fori_loop(0, count // step, run, 0)


def add_into(dst, *sources):
    def body(rows):
        total = dst[rows, :].astype(F32)
        for source in sources:
            total = total + source[rows, :].astype(F32)
        dst[rows, :] = total.astype(dst.dtype)

    by_rows(dst.shape[0], 16, body)


def run_all(*parts):
    parts = list(parts)
    while parts:
        for part in list(parts):
            if next(part, StopIteration) is StopIteration:
                parts.remove(part)


def plane_gather(w, spot, pack, out):
    y, z, c = spot.y, spot.z, spot.c
    rows = pl.ds(pl.multiple_of(c * 64, 64), 64)
    swap = w.push(pack.at[1 - c], out.at[y, z, rows], spot.dev(other=True))
    own = w.local(pack.at[c], out.at[y, z, rows])
    yield
    swap.wait_recv()
    own.wait()
    ym, yp, zm, zp = (y + 3) % 4, (y + 1) % 4, (z + 3) % 4, (z + 1) % 4
    to_zp, to_zm = spot.dev(dz=1), spot.dev(dz=-1)
    to_yp, to_ym = spot.dev(dy=1), spot.dev(dy=-1)
    a, b = pl.ds(0, 64), pl.ds(64, 64)
    mine_a, mine_b = out.at[y, z, a], out.at[y, z, b]
    a1 = w.push(mine_a, mine_a, to_zp)
    a2 = w.push(mine_a, mine_a, to_zm)
    b1 = w.push(mine_b, mine_b, to_yp)
    b2 = w.push(mine_b, mine_b, to_ym)
    yield
    a1.wait_recv()
    part = out.at[y, zm, pl.ds(0, 32)]
    a3 = w.push(part, part, to_zp)
    b1.wait_recv()
    part = out.at[ym, z, pl.ds(64, 32)]
    b3 = w.push(part, part, to_yp)
    a2.wait_recv()
    part = out.at[y, zp, pl.ds(32, 32)]
    a4 = w.push(part, part, to_zm)
    b2.wait_recv()
    part = out.at[yp, z, pl.ds(96, 32)]
    b4 = w.push(part, part, to_ym)
    yield
    a3.wait_recv()
    a4.wait_recv()
    part = out.at[y, :, a]
    a5 = w.push(part, part, to_yp)
    a6 = w.push(part, part, to_ym)
    b3.wait_recv()
    b4.wait_recv()
    part = out.at[:, z, b]
    b5 = w.push(part, part, to_zp)
    b6 = w.push(part, part, to_zm)
    yield
    a5.wait_recv()
    part = out.at[ym, pl.ds(0, 2), a]
    a7 = w.push(part, part, to_yp)
    b5.wait_recv()
    part = out.at[pl.ds(0, 2), zm, b]
    b7 = w.push(part, part, to_zp)
    a6.wait_recv()
    part = out.at[yp, pl.ds(2, 2), a]
    a8 = w.push(part, part, to_ym)
    b6.wait_recv()
    part = out.at[pl.ds(2, 2), zp, b]
    b8 = w.push(part, part, to_zm)
    yield
    for copy in (a7, b7, a8, b8):
        copy.wait_recv()


def plane_sum_scratch(columns, resident):
    kept = [
        pltpu.VMEM((2, 2, 64, columns), BF),
        pltpu.VMEM((2, 2, 64, columns), BF),
        pltpu.VMEM((2, 4, 64, columns), BF),
    ]
    return ([] if resident else kept) + [
        pltpu.VMEM((2, 2, 2, 64, columns), BF),
        pltpu.VMEM((2, 2, 4, 64, columns), BF),
        pltpu.VMEM((2, 2, 32, columns), BF),
        pltpu.VMEM((2, 2, 64, columns), BF),
        pltpu.VMEM((128, columns), BF),
        pltpu.VMEM((2, 64, columns), BF),
    ]


def plane_sum(w, spot, part, scratch, resident=False):
    in1, in2, in3, in4, full, both = scratch[-6:]
    c = spot.c
    rows = (pl.ds(0, 64), pl.ds(64, 64))
    lanes = ((spot.y, spot.z), (spot.z, spot.y))
    steps = (("dy", "dz"), ("dz", "dy"))

    def view(h, k, low, size):
        at = (lanes[h][0] + k) % 4
        if h == 0:
            return part.at[at, pl.ds(low, size), rows[h]]
        return part.at[pl.ds(low, size), at, rows[h]]

    def held(h, j):
        if not resident:
            return scratch[2].at[h, j]
        if h == 0:
            return part.at[spot.y, j, rows[h]]
        return part.at[j, spot.z, rows[h]]

    def to(h, stage, step):
        return spot.dev(**{steps[h][stage]: step})

    loads, first, second, early = [], [], [], []
    for h in range(2):
        first.append(
            (
                w.push(view(h, 2, 0, 2), in1.at[h, 0], to(h, 0, 1)),
                w.push(view(h, 2, 2, 2), in1.at[h, 1], to(h, 0, -1)),
            )
        )
    for h in range(2):
        if resident:
            plus, minus = view(h, 1, 0, 2), view(h, 3, 2, 2)
            loads.append((plus, minus))
            continue
        plus, minus = scratch[0].at[h], scratch[1].at[h]
        loads.append(
            (
                plus,
                minus,
                w.local(view(h, 1, 0, 2), plus),
                w.local(view(h, 3, 2, 2), minus),
                w.local(view(h, 0, 0, 4), scratch[2].at[h]),
            )
        )
    for h in range(2):
        early.append(
            (
                w.push(view(h, 1, 2, 2), in2.at[h, 0, pl.ds(2, 2)], to(h, 0, 1)),
                w.push(view(h, 3, 0, 2), in2.at[h, 1, pl.ds(0, 2)], to(h, 0, -1)),
            )
        )
    yield
    for h in range(2):
        plus, minus = loads[h][:2]
        if not resident:
            loads[h][2].wait()
        first[h][0].wait_recv()
        for j in range(2):
            add_into(plus.at[j], in1.at[h, 0, j])
        one = w.push(plus, in2.at[h, 0, pl.ds(0, 2)], to(h, 0, 1))
        if not resident:
            loads[h][3].wait()
        first[h][1].wait_recv()
        for j in range(2):
            add_into(minus.at[j], in1.at[h, 1, j])
        two = w.push(minus, in2.at[h, 1, pl.ds(2, 2)], to(h, 0, -1))
        second.append((one, two))
    yield
    third, early3 = [], []
    for h in range(2):
        if not resident:
            loads[h][4].wait()
        for copy in early[h] + second[h]:
            copy.wait_recv()
        at = [(lanes[h][1] + k) % 4 for k in range(4)]
        add_into(held(h, at[2]), in2.at[h, 0, at[2]], in2.at[h, 1, at[2]])
        far = held(h, at[2])
        third.append(
            (
                w.push(far.at[pl.ds(0, 32)], in3.at[h, 0], to(h, 1, 1)),
                w.push(far.at[pl.ds(32, 32)], in3.at[h, 1], to(h, 1, -1)),
            )
        )
        add_into(held(h, at[1]), in2.at[h, 0, at[1]], in2.at[h, 1, at[1]])
        one = w.push(held(h, at[1]).at[pl.ds(32, 32)], in4.at[h, 0, pl.ds(32, 32)], to(h, 1, 1))
        add_into(held(h, at[3]), in2.at[h, 0, at[3]], in2.at[h, 1, at[3]])
        two = w.push(held(h, at[3]).at[pl.ds(0, 32)], in4.at[h, 1, pl.ds(0, 32)], to(h, 1, -1))
        early3.append((one, two))
        add_into(held(h, at[0]), in2.at[h, 0, at[0]], in2.at[h, 1, at[0]])
    yield
    fourth = []
    for h in range(2):
        at = [(lanes[h][1] + k) % 4 for k in range(4)]
        third[h][0].wait_recv()
        piece = held(h, at[1]).at[pl.ds(0, 32)]
        add_into(piece, in3.at[h, 0])
        one = w.push(piece, in4.at[h, 0, pl.ds(0, 32)], to(h, 1, 1))
        third[h][1].wait_recv()
        piece = held(h, at[3]).at[pl.ds(32, 32)]
        add_into(piece, in3.at[h, 1])
        two = w.push(piece, in4.at[h, 1, pl.ds(32, 32)], to(h, 1, -1))
        fourth.append((one, two))
    yield
    for h in range(2):
        for copy in early3[h] + fourth[h]:
            copy.wait_recv()
        mine = held(h, lanes[h][1])
        target = full.at[rows[h]]

        def body(r):
            total = mine[r, :].astype(F32) + in4[h, 0, r, :].astype(F32)
            target[r, :] = (total + in4[h, 1, r, :].astype(F32)).astype(BF)

        by_rows(64, 16, body)
    theirs = full.at[pl.ds(pl.multiple_of((1 - c) * 64, 64), 64)]
    mine = full.at[pl.ds(pl.multiple_of(c * 64, 64), 64)]
    swap = w.push(theirs, both.at[c], spot.dev(other=True))

    def keep(r):
        both[c, r, :] = mine[r, :]

    by_rows(64, 16, keep)
    yield
    swap.wait_recv()


def mate_share(w, spot, both, outs):
    copies = []
    for out, low, size in outs:
        for core in range(2):
            piece = both.at[core, :, pl.ds(low, size)]
            at = pl.ds(pl.multiple_of((spot.lo * 2 + core) * size, size), size)
            copies.append((w.local(piece, out.at[:, at]), w.push(piece, out.at[:, at], spot.dp_mate())))
    yield
    for near, far in copies:
        near.wait()
        far.wait_recv()


def column_sum_scratch():
    return [
        pltpu.VMEM((4, 128, WIDTH), BF),
        pltpu.VMEM((4, 128, WIDTH), BF),
        pltpu.VMEM((2, 64, WIDTH), BF),
        pltpu.VMEM((2, 128, WIDTH), BF),
    ]


def column_sum(w, spot, part, scratch, finish, resident=False):
    own, got, in1, in2 = scratch
    x, c = spot.x, spot.c
    right, left = spot.dev(dx=1), spot.dev(dx=-1)
    places = [((x + k) % 4 % 2, (x + k) % 4 // 2) for k in range(4)]
    swaps, loads = {}, {}
    for k in (2, 1, 3, 0):
        swaps[k] = w.push(part.at[1 - c, places[k][0], places[k][1]], got.at[k], spot.dev(other=True))
    if resident:
        own = [part.at[c, lo, hi] for lo, hi in places]
    else:
        for k in (2, 1, 3, 0):
            loads[k] = w.local(part.at[c, places[k][0], places[k][1]], own.at[k])
        own = [own.at[k] for k in range(4)]
    yield

    def merge(k):
        if not resident:
            loads[k].wait()
        swaps[k].wait_recv()
        add_into(own[k], got.at[k])

    low, high = pl.ds(0, 64), pl.ds(64, 64)
    merge(2)
    far1 = w.push(own[2].at[low], in1.at[0], right)
    far2 = w.push(own[2].at[high], in1.at[1], left)
    merge(1)
    one = w.push(own[1].at[high], in2.at[0, high], right)
    merge(3)
    two = w.push(own[3].at[low], in2.at[1, low], left)
    merge(0)
    yield
    far1.wait_recv()
    add_into(own[1].at[low], in1.at[0])
    three = w.push(own[1].at[low], in2.at[0, low], right)
    far2.wait_recv()
    add_into(own[3].at[high], in1.at[1])
    four = w.push(own[3].at[high], in2.at[1, high], left)
    yield
    for copy in (one, two, three, four):
        copy.wait_recv()

    def total(rows):
        return own[0][rows, :].astype(F32) + in2[0, rows, :].astype(F32) + in2[1, rows, :].astype(F32)

    finish(total)


def column_share(w, spot, mine, out):
    x, c = spot.x, spot.c
    right, left, mate = spot.dev(dx=1), spot.dev(dx=-1), spot.dev(other=True)

    def slot(k):
        at = (x + k + 4) % 4
        return out.at[c, at % 2, at // 2]

    low, high = pl.ds(0, 64), pl.ds(64, 64)
    own = w.local(mine, slot(0))
    a = w.push(mine, slot(0), right)
    b = w.push(mine, slot(0), left)
    d = w.push(mine, slot(0), mate)
    yield
    a.wait_recv()
    e = w.push(slot(-1).at[low], slot(-1).at[low], right)
    f = w.push(slot(-1), slot(-1), mate)
    b.wait_recv()
    g = w.push(slot(1).at[high], slot(1).at[high], left)
    h = w.push(slot(1), slot(1), mate)
    yield
    e.wait_recv()
    i = w.push(slot(2).at[low], slot(2).at[low], mate)
    g.wait_recv()
    j = w.push(slot(2).at[high], slot(2).at[high], mate)
    yield
    own.wait()
    for copy in (d, f, h, i, j):
        copy.wait_recv()


def token_share(w, spot, block, out):
    own_at, far_at = spot.c * 2 + spot.lo, spot.c * 2 + 1 - spot.lo
    right, left, mate = spot.dev(dx=1), spot.dev(dx=-1), spot.dev(other=True)
    low, high = pl.ds(0, 128), pl.ds(128, 128)
    own = w.local(block, out.at[own_at])
    a = w.push(block.at[low], out.at[own_at, low], right)
    b = w.push(block.at[high], out.at[own_at, high], left)
    d = w.push(block, out.at[own_at], mate)
    yield
    a.wait_recv()
    part = out.at[far_at, low]
    e = w.push(part, part, mate)
    b.wait_recv()
    part = out.at[far_at, high]
    f = w.push(part, part, mate)
    yield
    own.wait()
    for copy in (d, e, f):
        copy.wait_recv()


def pair_share(w, spot, mine, out):
    own = w.local(mine, out.at[spot.hi])
    a = w.push(mine, out.at[spot.hi], spot.dev(dx=2))
    yield
    own.wait()
    a.wait_recv()


def neighbours(spot, x=False, yz=False, core=False, pair=False, far=False):
    found = []
    if x:
        found += [spot.dev(dx=1), spot.dev(dx=-1)]
    if yz:
        found += [spot.dev(dy=1), spot.dev(dy=-1), spot.dev(dz=1), spot.dev(dz=-1)]
    if core:
        found += [spot.dev(other=True)]
    if pair:
        found += [spot.dev(dx=2)]
    if far:
        found += [spot.dev(dy=2), spot.dev(dz=2)]
    return found


BLOCK = 256
SPAN = COLUMN + BLOCK
NT = (((1,), (1,)), ((), ()))
TN = (((0,), (0,)), ((), ()))
NN = (((1,), (0,)), ((), ()))


def dot(a, b, dims):
    return lax.dot_general(a, b, dims, preferred_element_type=F32)


def rms_of(rows):
    inverse = lax.rsqrt(jnp.mean(rows * rows, axis=-1, keepdims=True) + EPS)
    return rows * inverse, inverse


def turn_half(rows):
    half = HEAD // 2
    return jnp.concatenate([-rows[:, half:], rows[:, :half]], axis=-1)


def params(collective_id):
    return pltpu.CompilerParams(
        collective_id=collective_id, has_side_effects=True, vmem_limit_bytes=LIMIT
    )


def own_block(ref, spot):
    return ref.at[spot.c, spot.lo, spot.hi]


def place_rows(spot, lengths, freq, doc_row, doc_col, cosine, sine):
    first = (spot.y * 4 + spot.z - 1) * COLUMN
    rows = lax.broadcasted_iota(jnp.int32, (16, 128), 0) * 128 + first
    rows = rows + lax.broadcasted_iota(jnp.int32, (16, 128), 1)
    document = jnp.zeros((16, 128), jnp.int32)
    start = jnp.zeros((16, 128), jnp.int32)
    bound = jnp.int32(0)
    for d in range(lengths.shape[1]):
        bound = bound + lengths[0, d]
        passed = rows >= bound
        document = document + passed.astype(jnp.int32)
        start = jnp.where(passed, bound, start)
    document = jnp.where(rows >= 0, document, -1).astype(F32)
    place = (rows - start).astype(F32)
    for g in range(16):
        line = document[g : g + 1, :]
        at = slice(g * 128, (g + 1) * 128)
        doc_row[:, at] = line
        doc_col[at, :] = jnp.transpose(jnp.broadcast_to(line, (128, 128)))
        if g >= 8:
            down = jnp.transpose(jnp.broadcast_to(place[g : g + 1, :], (128, 128)))
            angles = down * freq[...]
            at = slice((g - 8) * 128, (g - 7) * 128)
            cosine[at, :] = jnp.cos(angles)
            sine[at, :] = jnp.sin(angles)


def turned_head(raw, scale, cosine, sine):
    unit = rms_of(raw)[0] * scale
    return (unit * cosine + turn_half(unit) * sine).astype(BF)


def forward_kernel(
    tok, cot, pack_a, pack_w, pack_b, lengths, freq, q_gain, k_gain,
    normed1, w_a, w_w, w_b, cot_all, raw, query, kv, before, attended, inverse, mid, normed2, cosine, sine, gains, doc_row, doc_col,
    tok_all, low1, roots, top, total, branch, got, in1, in2, low, send, recv, here,
):
    spot = Spot()
    greet(neighbours(spot, x=True, yz=True, core=True) + [spot.column(1), spot.column(-1)])
    w = Wires(send, recv, here)
    take_a = plane_gather(w, spot, pack_a, w_a)
    take_w = plane_gather(w, spot, pack_w, w_w)
    take_b = plane_gather(w, spot, pack_b, w_b)
    take_tok = token_share(w, spot, tok, tok_all)
    take_cot = token_share(w, spot, cot, cot_all)

    def go(*parts):
        for part in parts:
            next(part, None)

    go(take_a, take_tok, take_w, take_b, take_a)
    place_rows(spot, lengths, freq, doc_row, doc_col, cosine, sine)
    go(take_a, take_tok, take_a, take_tok)

    def roots_of(i, _):
        rows = pl.ds(pl.multiple_of(i * 32, 32), 32)
        values = tok_all[i // 8, pl.ds(pl.multiple_of(i % 8 * 32, 32), 32), :].astype(F32)
        roots[rows, :] = lax.rsqrt(jnp.mean(values * values, axis=-1, keepdims=True) + EPS)
        return 0

    lax.fori_loop(0, 32, roots_of, 0)
    go(take_a, take_w, take_a)
    go(take_cot, take_b)
    for i in range(16):
        block = jnp.transpose(w_a[i // 4, i % 4, :, 512:640].astype(F32))
        gains[:, i * 128 : (i + 1) * 128] = block[0:2, :]

    def norm_rows(i, _):
        rows = pl.ds(pl.multiple_of(i * 32, 32), 32)
        values = tok_all[i // 8, pl.ds(pl.multiple_of(i % 8 * 32, 32), 32), :].astype(F32)
        low1[rows, :] = (values * roots[rows, :] * gains[0:1, :]).astype(BF)
        return 0

    lax.fori_loop(0, 32, norm_rows, 0)
    keep = w.local(low1, normed1)

    def project_kv(i, _):
        rows = pl.ds(pl.multiple_of(i * BLOCK, BLOCK), BLOCK)
        out = dot(low1[rows, :], w_a[:, :, :, 256:512].reshape(WIDTH, 256), NN)
        raw[rows, 256:512] = out
        kv[rows, :HEAD] = turned_head(out[:, :HEAD], k_gain[...].astype(F32), cosine[rows, :], sine[rows, :])
        kv[rows, HEAD:] = out[:, HEAD:].astype(BF)
        return 0

    def project_q(i, _):
        rows = pl.ds(pl.multiple_of(i * BLOCK, BLOCK), BLOCK)
        out = dot(low1[rows, :], w_a[:, :, :, 0:256].reshape(WIDTH, 256), NN)
        raw[rows, 0:256] = out
        for h in range(2):
            span = slice(h * HEAD, (h + 1) * HEAD)
            query[rows, span] = turned_head(out[:, span], q_gain[...].astype(F32), cosine[rows, :], sine[rows, :])
        return 0

    lax.fori_loop(0, 4, project_kv, 0)
    pass_kv = w.push(kv, before, spot.column(1))
    go(take_w, take_b)
    lax.fori_loop(0, 4, project_q, 0)
    go(take_cot)

    def weights_of(i, h, keys, docs, causal):
        rows = slice(i * BLOCK, (i + 1) * BLOCK)
        scores = dot(query[rows, h * HEAD : (h + 1) * HEAD], keys, NT) * SCALE
        valid = doc_col[COLUMN + i * BLOCK : COLUMN + (i + 1) * BLOCK, 0:1] == docs
        if causal:
            row = lax.broadcasted_iota(jnp.int32, scores.shape, 0) + i * BLOCK
            valid = valid & (lax.broadcasted_iota(jnp.int32, scores.shape, 1) <= row)
        return jnp.where(valid, jnp.exp(scores), 0.0)

    for i in range(4):
        rows, end = slice(i * BLOCK, (i + 1) * BLOCK), (i + 1) * BLOCK
        for h in range(2):
            weight = weights_of(i, h, kv[0:end, :HEAD], doc_row[:, COLUMN : COLUMN + end], True)
            total[rows, h : h + 1] = jnp.sum(weight, axis=-1, keepdims=True)
            top[rows, h * HEAD : (h + 1) * HEAD] = dot(weight.astype(BF), kv[0:end, HEAD:], NN)
        if i == 1:
            go(take_w)
    pass_kv.wait_recv()
    go(take_w, take_b)
    for i in range(4):
        rows, low_key = slice(i * BLOCK, (i + 1) * BLOCK), i * BLOCK
        for h in range(2):
            span = slice(h * HEAD, (h + 1) * HEAD)
            weight = weights_of(i, h, before[low_key:, :HEAD], doc_row[:, low_key:COLUMN], False)
            back = 1.0 / (total[rows, h : h + 1] + jnp.sum(weight, axis=-1, keepdims=True))
            inverse[rows, h : h + 1] = back
            attended[rows, span] = ((top[rows, span] + dot(weight.astype(BF), before[low_key:, HEAD:], NN)) * back).astype(BF)
    go(take_w)

    def branch_of(core):
        def one(lo, _):
            rows = pl.ds(pl.multiple_of((core * 2 + lo) * BLOCK, BLOCK), BLOCK)
            out = dot(attended[rows, :], w_w[...].reshape(WIDTH, 256), NT)
            branch[core, lo] = out.astype(BF).reshape(2, 128, WIDTH)
            return 0

        lax.fori_loop(0, 2, one, 0)

    def finish(add):
        def body(rows):
            base = tok[pl.ds(pl.multiple_of(spot.hi * 128 + rows.start, 16), 16), :].astype(F32)
            middle = base + add(rows)
            mid[rows, :] = middle
            root = lax.rsqrt(jnp.mean(middle * middle, axis=-1, keepdims=True) + EPS)
            low[rows, :] = (middle * root * gains[1:2, :]).astype(BF)

        by_rows(128, 16, body)

    branch_of(1 - spot.c)
    fold = column_sum(w, spot, branch, (None, got, in1, in2), finish, resident=True)
    go(fold)
    branch_of(spot.c)
    go(fold, fold, fold, take_cot)
    share = column_share(w, spot, low, normed2)
    go(share, take_b, share, share, take_b, share)
    keep.wait()
    w.drain()


def forward_call(tok, cot, pack_a, pack_w, pack_b, lengths, freq, q_gain, k_gain):
    def gathered(pack):
        return jax.ShapeDtypeStruct((4, 4, 128, pack.shape[-1]), BF)

    def shape(*sizes, kind=BF):
        return jax.ShapeDtypeStruct(sizes, kind)

    outs = (
        (shape(COLUMN, WIDTH), HBM),
        (gathered(pack_a), VMEM),
        (gathered(pack_w), VMEM),
        (gathered(pack_b), HBM),
        (shape(4, 256, WIDTH), HBM),
        (shape(COLUMN, 512, kind=F32), VMEM),
        (shape(COLUMN, 256), VMEM),
        (shape(COLUMN, 256), VMEM),
        (shape(COLUMN, 256), VMEM),
        (shape(COLUMN, 256), VMEM),
        (shape(COLUMN, 2, kind=F32), VMEM),
        (shape(128, WIDTH, kind=F32), VMEM),
        (shape(2, 2, 2, 128, WIDTH), HBM),
        (shape(COLUMN, HEAD, kind=F32), VMEM),
        (shape(COLUMN, HEAD, kind=F32), VMEM),
        (shape(2, WIDTH, kind=F32), VMEM),
        (shape(1, 2 * COLUMN, kind=F32), VMEM),
        (shape(2 * COLUMN, 128, kind=F32), VMEM),
    )
    return pl.pallas_call(
        forward_kernel,
        out_shape=tuple(o[0] for o in outs),
        in_specs=[VMEM] * 5 + [pl.BlockSpec(memory_space=pltpu.SMEM)] + [VMEM] * 3,
        out_specs=tuple(o[1] for o in outs),
        scratch_shapes=[
            pltpu.VMEM((4, 256, WIDTH), BF),
            pltpu.VMEM((COLUMN, WIDTH), BF),
            pltpu.VMEM((COLUMN, 1), F32),
            pltpu.VMEM((COLUMN, 256), F32),
            pltpu.VMEM((COLUMN, 2), F32),
            pltpu.VMEM((2, 2, 2, 128, WIDTH), BF),
        ]
        + column_sum_scratch()[1:]
        + [pltpu.VMEM((128, WIDTH), BF)]
        + wires_scratch(96, 12),
        compiler_params=params(1),
        name="forward",
    )(tok, cot, pack_a, pack_w, pack_b, lengths, freq, q_gain, k_gain)


def rms_back(total, base, gain, rows, extra, out, gain_grad):
    values = base[rows, :].astype(F32)
    inverse = lax.rsqrt(jnp.mean(values * values, axis=-1, keepdims=True) + EPS)
    normed = values * inverse
    grad = total(rows)
    scaled = grad * gain[...]
    back = inverse * (scaled - normed * jnp.mean(scaled * normed, axis=-1, keepdims=True))
    gain_grad[...] += jnp.sum(grad * normed, axis=0, keepdims=True)
    out[rows, :] = extra[rows, :].astype(F32) + back


def turn_kernel(
    normed, cot, w_b, mid, cot_own, gain, dmid, d_branch, mixed, g_in, gain_grad, both_out,
    nv, cv, wv, hidden, d_both, part, g_down, g_part, mixed_part, got, in1, in2, low, top,
    p0, p1, p2, p3, p4, p5, send, recv, here, tiles,
):
    spot = Spot()
    w = Wires(send, recv, here)
    first = w.local(w_b, wv)

    def block(i):
        rows = pl.ds(pl.multiple_of(i * BLOCK, BLOCK), BLOCK)
        one = pltpu.make_async_copy(normed.at[rows], nv.at[rows], tiles.at[0, i])
        return one, pltpu.make_async_copy(cot.at[rows], cv.at[rows], tiles.at[1, i])

    for i in range(4):
        for copy in block(i):
            copy.start()
    load = w.local(cot_own.at[spot.hi], top)
    greet(neighbours(spot, x=True, yz=True, core=True))
    gain_grad[...] = jnp.zeros_like(gain_grad)
    first.wait()

    def weight(low_column, size):
        return wv[:, :, :, low_column : low_column + size].reshape(WIDTH, size)

    def units(i, _):
        rows = pl.ds(pl.multiple_of(i * BLOCK, BLOCK), BLOCK)
        for copy in block(i):
            copy.wait()
        for j in range(3):
            a = slice(j * 256, (j + 1) * 256)
            b = slice(768 + j * 256, 1024 + j * 256)
            gate = dot(nv[rows, :], weight(j * 256, 256), NN)
            up = dot(nv[rows, :], weight(768 + j * 256, 256), NN)
            d_hidden = dot(cv[rows, :], weight(1536 + j * 256, 256), NN)
            sigma = lax.logistic(gate)
            active = gate * sigma
            hidden[rows, a] = (active * up).astype(BF)
            d_both[rows, a] = (d_hidden * up * sigma * (1.0 + gate * (1.0 - sigma))).astype(BF)
            d_both[rows, b] = (d_hidden * active).astype(BF)
        return 0

    lax.fori_loop(0, 4, units, 0)

    def back_of(core):
        def one(lo, _):
            rows = pl.ds(pl.multiple_of((core * 2 + lo) * BLOCK, BLOCK), BLOCK)
            out = dot(d_both[rows, :], weight(0, 1536), NT)
            part[core, lo] = out.astype(BF).reshape(2, 128, WIDTH)
            return 0

        lax.fori_loop(0, 2, one, 0)

    def finish(total):
        load.wait()

        def body(rows):
            rms_back(total, mid, gain, rows, top, dmid, gain_grad)
            low[rows, :] = dmid[rows, :].astype(BF)

        by_rows(128, 16, body)

    def go(*parts):
        for one in parts:
            next(one, None)

    def down_tile(t, _):
        lanes = pl.ds(pl.multiple_of(t * BLOCK, BLOCK), BLOCK)
        out = dot(cv[:, lanes], hidden[...], TN)
        g_down[t // 2, pl.ds(t % 2 * 2, 2)] = out.astype(BF).reshape(2, 128, 768)
        return 0

    def in_copy(t):
        at = (t // 2, pl.ds(t % 2 * 2, 2))
        return pltpu.make_async_copy(g_part.at[at], g_in.at[at], tiles.at[2, t])

    def in_tile(t, _):
        lanes = pl.ds(pl.multiple_of(t * BLOCK, BLOCK), BLOCK)
        out = dot(nv[:, lanes], d_both[...], TN)
        g_part[t // 2, pl.ds(t % 2 * 2, 2)] = out.astype(BF).reshape(2, 128, 1536)
        in_copy(t).start()
        return 0

    def mixed_block(i, _):
        rows = pl.ds(pl.multiple_of(i * BLOCK, BLOCK), BLOCK)
        out = dot(hidden[rows, :], weight(1536, 768), NT)
        mixed_part[i // 2, i % 2] = out.astype(BF).reshape(2, 128, WIDTH)
        return 0

    back_of(1 - spot.c)
    fold = column_sum(w, spot, part, (None, got, in1, in2), finish, resident=True)
    go(fold)
    back_of(spot.c)
    go(fold)
    lax.fori_loop(0, 8, down_tile, 0)
    down = plane_sum(w, spot, g_down, (p0, p1, p2, p3, p4, p5), resident=True)
    go(fold, down)
    lax.fori_loop(0, 4, in_tile, 0)
    go(fold)
    share = column_share(w, spot, low, d_branch)
    go(share, down)
    lax.fori_loop(0, 4, mixed_block, 0)
    keep = w.local(mixed_part, mixed)
    go(share, down)
    lax.fori_loop(4, 8, in_tile, 0)
    go(share, down, share, down, down)
    last = w.local(p5, both_out)
    for t in range(8):
        in_copy(t).wait()
    keep.wait()
    last.wait()
    w.drain()


def turn_call(normed, cot, w_b, mid, cot_own, gain):
    blocks = jax.ShapeDtypeStruct((2, 2, 2, 128, WIDTH), BF)
    return pl.pallas_call(
        turn_kernel,
        out_shape=(
            jax.ShapeDtypeStruct((128, WIDTH), F32),
            blocks,
            blocks,
            jax.ShapeDtypeStruct((4, 4, 128, 1536), BF),
            jax.ShapeDtypeStruct((1, WIDTH), F32),
            jax.ShapeDtypeStruct((2, 64, 768), BF),
        ),
        in_specs=[HBM, HBM, HBM, VMEM, HBM, VMEM],
        out_specs=(VMEM, HBM, HBM, HBM, VMEM, HBM),
        scratch_shapes=[
            pltpu.VMEM((COLUMN, WIDTH), BF),
            pltpu.VMEM((COLUMN, WIDTH), BF),
            pltpu.VMEM((4, 4, 128, 2304), BF),
            pltpu.VMEM((COLUMN, 768), BF),
            pltpu.VMEM((COLUMN, 1536), BF),
            pltpu.VMEM((2, 2, 2, 128, WIDTH), BF),
            pltpu.VMEM((4, 4, 128, 768), BF),
            pltpu.VMEM((4, 4, 128, 1536), BF),
            pltpu.VMEM((2, 2, 2, 128, WIDTH), BF),
        ]
        + column_sum_scratch()[1:]
        + [pltpu.VMEM((128, WIDTH), BF)] * 2
        + plane_sum_scratch(768, True)
        + wires_scratch(64, 12)
        + [pltpu.SemaphoreType.DMA((3, 8))],
        compiler_params=params(4),
        name="turn",
    )(normed, cot, w_b, mid, cot_own, gain)


def sum_everywhere(w, spot, vector, pair, lines):
    a = w.push(vector, pair, spot.dev(other=True))
    yield
    a.wait_recv()
    w.sent_now(a)
    vector[...] = vector[...] + pair[...]
    yield
    for stage, (axis, at) in enumerate((("dx", spot.x), ("dy", spot.y), ("dz", spot.z))):
        slots = lines.at[stage]
        slots[at] = vector[...]
        copies = [w.push(vector, slots.at[at], spot.dev(**{axis: k})) for k in (1, 2, 3)]
        yield
        for copy in copies:
            copy.wait_recv()
            w.sent_now(copy)
        vector[...] = slots[0] + slots[1] + slots[2] + slots[3]
        yield


def as_row(column):
    return jnp.transpose(jnp.broadcast_to(column, (column.shape[0], HEAD)))[0:1, :]


def close_kernel(
    d_branch, w_w, w_a, attended, query, before, kv, raw, cosine, sine, doc_row, doc_col, inverse, q_gain, k_gain,
    g_in, both_down, mixed, mid, dmid, tok, gain, normed1, g_mlp,
    out, gtok, o_gate, o_up, o_down, o_q, o_k, o_v, o_out, vector,
    db, do, dq, dkv, d_before, came, d_raw, part, g_out, got, in1, in2,
    m_own, m_got, m_in1, m_in2, result, base, final, gain_grad, low, theirs,
    a0, a1, a2, a3, a4, a5, a6, a7, a8, b0, b1, b2, b3, b4, b5, pair, lines, send, recv, here, tiles,
):
    spot = Spot()
    w = Wires(send, recv, here)

    def block(i):
        rows = pl.ds(pl.multiple_of(i * BLOCK, BLOCK), BLOCK)
        return pltpu.make_async_copy(d_branch.at[rows], db.at[rows], tiles.at[i])

    for i in range(4):
        block(i).start()
    load_tok = w.local(tok.at[spot.hi], base)
    greet(
        neighbours(spot, x=True, yz=True, core=True, pair=True, far=True)
        + [spot.column(1), spot.column(-1)]
    )

    def go(*parts):
        for one in parts:
            next(one, None)

    sum_in = plane_sum(w, spot, g_in, (a0, a1, a2, a3, a4, a5, a6, a7, a8))
    go(sum_in)

    def finish_out(total):
        def body(rows):
            result[rows, :] = (mid[rows, :] + total(rows)).astype(BF)

        by_rows(128, 16, body)

    fold_out = column_sum(w, spot, mixed, (m_own, m_got, m_in1, m_in2), finish_out)
    share_out = pair_share(w, spot, result, out)
    share_down = mate_share(w, spot, both_down, ((o_down, 0, 768),))
    go(fold_out)
    gain_grad[...] = jnp.zeros_like(gain_grad)
    vector[...] = jnp.zeros_like(vector)
    dkv[...] = jnp.zeros_like(dkv)

    def upstream_of(i, _):
        block(i).wait()
        rows = pl.ds(pl.multiple_of(i * BLOCK, BLOCK), BLOCK)
        do[rows, :] = dot(db[rows, :], w_w[...], NN).astype(BF)
        return 0

    lax.fori_loop(0, 4, upstream_of, 0)
    go(fold_out)

    def tile_out(t, _):
        lanes = pl.ds(pl.multiple_of(t * BLOCK, BLOCK), BLOCK)
        at = (t // 2, pl.ds(t % 2 * 2, 2), slice(None), slice(512, 768))
        g_out[at] = dot(db[:, lanes], attended[...], TN).astype(BF).reshape(2, 128, 256)
        return 0

    def tile(t, _):
        lanes = pl.ds(pl.multiple_of(t * BLOCK, BLOCK), BLOCK)
        at = (t // 2, pl.ds(t % 2 * 2, 2), slice(None), slice(0, 512))
        g_out[at] = dot(db[:, lanes], d_raw[...], TN).astype(BF).reshape(2, 128, 512)
        return 0


    def attend_back(i, keys_of, docs, causal, grads, fresh):
        rows = slice(i * BLOCK, (i + 1) * BLOCK)
        product = attended[rows, :].astype(F32) * do[rows, :].astype(F32)
        valid = docs == doc_row[:, COLUMN + i * BLOCK : COLUMN + (i + 1) * BLOCK]
        if causal:
            row = lax.broadcasted_iota(jnp.int32, valid.shape, 0)
            valid = valid & (row <= lax.broadcasted_iota(jnp.int32, valid.shape, 1) + i * BLOCK)
        for h in range(2):
            span = slice(h * HEAD, (h + 1) * HEAD)
            asked, upstream = query[rows, span], do[rows, span]
            back = as_row(inverse[rows, h : h + 1])
            delta = as_row(jnp.sum(product[:, span], axis=-1, keepdims=True))
            scores = dot(keys_of[:, :HEAD], asked, NT) * SCALE
            probs = jnp.where(valid, jnp.exp(scores), 0.0) * back
            d_probs = dot(keys_of[:, HEAD:], upstream, NT)
            d_scores = (probs * (d_probs - delta)).astype(BF)
            grads[:, :HEAD] += dot(d_scores, asked, NN) * SCALE
            grads[:, HEAD:] += dot(probs.astype(BF), upstream, NN)
            d_asked = dot(d_scores, keys_of[:, :HEAD], TN) * SCALE
            if fresh:
                dq[rows, span] = d_asked
            else:
                dq[rows, span] += d_asked

    for i in range(4):
        attend_back(
            i, before.at[i * BLOCK :], doc_col[i * BLOCK : COLUMN, 0:1], False, dkv.at[i * BLOCK : COLUMN], True
        )
    by_rows(COLUMN, 32, lambda r: d_before.__setitem__((r, slice(None)), dkv[r, :].astype(BF)))
    back_kv = w.push(d_before, came, spot.column(-1))
    go(sum_in, fold_out, share_down)
    lax.fori_loop(0, 8, tile_out, 0)
    load_n1 = w.local(normed1, db)
    for i in range(4):
        end = (i + 1) * BLOCK
        attend_back(
            i, kv.at[0:end], doc_col[COLUMN : COLUMN + end, 0:1], True, dkv.at[COLUMN : COLUMN + end], False
        )
        if i == 1:
            go(fold_out)
    go(share_out)
    back_kv.wait_recv()

    def project_back(i):
        rows = pl.ds(pl.multiple_of(i * BLOCK, BLOCK), BLOCK)
        own = pl.ds(pl.multiple_of(i * BLOCK + COLUMN, BLOCK), BLOCK)
        for h, scale in enumerate((q_gain, q_gain, k_gain)):
            span = slice(h * HEAD, (h + 1) * HEAD)
            if h < 2:
                grad = dq[rows, span]
            else:
                grad = dkv[own, :HEAD] + came[rows, :HEAD].astype(F32)
            grad = grad * cosine[rows, :] - turn_half(grad) * sine[rows, :]
            unit, root = rms_of(raw[rows, span])
            scaled = grad * scale[...].astype(F32)
            back = root * (scaled - unit * jnp.mean(scaled * unit, axis=-1, keepdims=True))
            d_raw[rows, span] = back.astype(BF)
            at = 32 + h // 2
            vector[at : at + 1, :] += jnp.sum(grad * unit, axis=0, keepdims=True)
        d_raw[rows, 3 * HEAD :] = (dkv[own, HEAD:] + came[rows, HEAD:].astype(F32)).astype(BF)

    def norm_of(core):
        def one(lo, _):
            project_back(core * 2 + lo)
            rows = pl.ds(pl.multiple_of((core * 2 + lo) * BLOCK, BLOCK), BLOCK)
            value = dot(d_raw[rows, :], w_a[:, :512], NT)
            part[core, lo] = value.astype(BF).reshape(2, 128, WIDTH)
            return 0

        lax.fori_loop(0, 2, one, 0)

    def finish(total):
        load_tok.wait()

        def body(rows):
            rms_back(total, base, gain, rows, dmid, final, gain_grad)
            low[rows, :] = final[rows, :].astype(BF)

        by_rows(128, 16, body)

    norm_of(1 - spot.c)
    fold = column_sum(w, spot, part, (None, got, in1, in2), finish, resident=True)
    go(fold, sum_in)
    norm_of(spot.c)
    go(fold)
    load_n1.wait()
    lax.fori_loop(0, 8, tile, 0)
    sum_out = plane_sum(w, spot, g_out, (b0, b1, b2, b3, b4, b5), resident=True)
    go(fold, sum_out, sum_in)
    go(fold)
    sent = w.push(low, theirs, spot.dev(dx=2))
    vector[16:32, :] = g_mlp[...]
    for i in range(16):
        vector[i : i + 1, :] = gain_grad[:, i * 128 : (i + 1) * 128]
    everywhere = sum_everywhere(w, spot, vector, pair, lines)
    go(everywhere, sum_out, sum_in)
    share_in = mate_share(w, spot, a8, ((o_gate, 0, 768), (o_up, 768, 768)))
    go(everywhere, sum_in, share_in)
    by_rows(128, 16, lambda rows: final.__setitem__((rows, slice(None)), low[rows, :].astype(F32)))
    one = w.local(final, gtok.at[spot.hi])
    go(everywhere, sum_out, everywhere)
    go(everywhere, sum_out, everywhere)
    go(everywhere, sum_out, everywhere)
    go(everywhere, sum_out, share_out, share_down, everywhere)
    share_grads = mate_share(
        w, spot, b5, ((o_q, 0, 256), (o_k, 256, 128), (o_v, 384, 128), (o_out, 512, 256))
    )
    go(share_grads, share_in)
    sent.wait_recv()
    one.wait()
    by_rows(128, 16, lambda rows: final.__setitem__((rows, slice(None)), theirs[rows, :].astype(F32)))
    two = w.local(final, gtok.at[1 - spot.hi])
    two.wait()
    go(share_grads)
    for part_left in (sum_in, fold_out, share_out, share_down, fold, sum_out, everywhere, share_in, share_grads):
        assert next(part_left, StopIteration) is StopIteration
    w.drain()


def close_call(*args):
    def shape(*sizes, kind=BF):
        return jax.ShapeDtypeStruct(sizes, kind)

    return pl.pallas_call(
        close_kernel,
        out_shape=(
            shape(2, 128, WIDTH),
            shape(2, 128, WIDTH, kind=F32),
            shape(64, 3072),
            shape(64, 3072),
            shape(64, 3072),
            shape(64, 1024),
            shape(64, 512),
            shape(64, 512),
            shape(64, 1024),
            shape(40, 128, kind=F32),
        ),
        in_specs=[HBM] + [VMEM] * 14 + [HBM, VMEM, HBM, VMEM, VMEM, HBM, VMEM, HBM, VMEM],
        out_specs=(HBM,) * 9 + (VMEM,),
        scratch_shapes=[
            pltpu.VMEM((COLUMN, WIDTH), BF),
            pltpu.VMEM((COLUMN, 256), BF),
            pltpu.VMEM((COLUMN, 256), F32),
            pltpu.VMEM((2 * COLUMN, 256), F32),
            pltpu.VMEM((COLUMN, 256), BF),
            pltpu.VMEM((COLUMN, 256), BF),
            pltpu.VMEM((COLUMN, 512), BF),
            pltpu.VMEM((2, 2, 2, 128, WIDTH), BF),
            pltpu.VMEM((4, 4, 128, 768), BF),
        ]
        + column_sum_scratch()[1:]
        + column_sum_scratch()
        + [
            pltpu.VMEM((128, WIDTH), BF),
            pltpu.VMEM((128, WIDTH), BF),
            pltpu.VMEM((128, WIDTH), F32),
            pltpu.VMEM((1, WIDTH), F32),
            pltpu.VMEM((128, WIDTH), BF),
            pltpu.VMEM((128, WIDTH), BF),
        ]
        + plane_sum_scratch(1536, False)
        + plane_sum_scratch(768, True)
        + [pltpu.VMEM((40, 128), F32), pltpu.VMEM((3, 4, 40, 128), F32)]
        + wires_scratch(100, 32)
        + [pltpu.SemaphoreType.DMA((4,))],
        compiler_params=params(6),
        name="close",
    )(*args)


def mine_of(weight, dp):
    rows, columns = weight.shape
    quarter = lax.dynamic_slice_in_dim(weight, dp * (columns // 2), columns // 2, 1)
    return quarter.reshape(rows, 2, columns // 4).transpose(1, 0, 2)


def on_device(
    tokens, lengths, attn_norm, w_query, w_key, w_value, w_output, q_gain, k_gain, mlp_norm, w_gate, w_up, w_down, cotangent,
):
    shard = lax.axis_index("shard")
    dp = lax.axis_index("dp")
    freq = THETA ** (-jnp.arange(0, HEAD, 2).astype(F32) / HEAD)
    freq = jnp.concatenate([freq, freq])[None]
    gains = jnp.pad(jnp.stack([attn_norm, mlp_norm], axis=1), ((0, 0), (0, 126)))
    pack_a = jnp.concatenate(
        [mine_of(w_query, dp), mine_of(w_key, dp), mine_of(w_value, dp), jnp.stack([gains, gains])], axis=-1
    )
    pack_w = mine_of(w_output.T, dp)
    pack_b = jnp.concatenate([mine_of(w_gate, dp), mine_of(w_up, dp), mine_of(w_down.T, dp)], axis=-1)
    (
        normed1, w_a, w_w, w_b, cot, raw, query, kv, before, attended, inverse, middle, normed2, cosine, sine, gains, doc_row, doc_col,
    ) = forward_call(tokens, cotangent, pack_a, pack_w, pack_b, lengths, freq, q_gain[None], k_gain[None])
    w_a, w_w = w_a.reshape(WIDTH, 640), w_w.reshape(WIDTH, 256)
    attn_gain, mlp_gain = gains[0:1], gains[1:2]
    d_middle, d_branch, mixed, g_in, g_mlp, both_down = turn_call(
        normed2.reshape(COLUMN, WIDTH),
        cot.reshape(COLUMN, WIDTH),
        w_b,
        middle,
        cotangent.reshape(2, 128, WIDTH),
        mlp_gain,
    )
    out, g_tokens, g_gate, g_up, g_down, g_query, g_key, g_value, g_output, sums = close_call(
        d_branch.reshape(COLUMN, WIDTH), w_w, w_a, attended, query, before, kv, raw, cosine, sine, doc_row, doc_col, inverse,
        q_gain[None], k_gain[None], g_in, both_down, mixed, middle, d_middle, tokens.reshape(2, 128, WIDTH), attn_gain,
        normed1, g_mlp.reshape(16, 128),
    )

    def rows_of(block):
        return lax.dynamic_slice_in_dim(block.reshape(WIDTH), shard * 64, 64)

    return (
        out.reshape(256, WIDTH),
        g_tokens.reshape(256, WIDTH),
        rows_of(sums[0:16]),
        g_query.astype(F32),
        g_key.astype(F32),
        g_value.astype(F32),
        g_output.astype(F32).T,
        sums[32],
        sums[33],
        rows_of(sums[16:32]),
        g_gate.astype(F32),
        g_up.astype(F32),
        g_down.astype(F32).T,
    )


def solution(mesh):
    rows = P(("shard", "dp"), None)
    down = P("shard", "tensor")
    across = P("tensor", "shard")
    one = P("shard")
    return jax.shard_map(
        on_device,
        mesh=mesh,
        in_specs=(rows, P(), one, down, down, down, across, P(), P(), one, down, down, across, rows),
        out_specs=(rows, rows, one, down, down, down, across, P(), P(), one, down, down, across),
        check_vma=False,
    )
```

```python
import functools

import jax
import jax.numpy as jnp
from jax import lax
from jax.experimental import pallas as pl
from jax.experimental.pallas import tpu as pltpu
from jax.sharding import PartitionSpec as P

HEAD = 128
EPS = 1e-06
THETA = 1000000.0
SCALE = HEAD ** (-0.5)
WIDTH = 2048
COLUMN = 1024
MESH = pl.DeviceIdType.MESH
BF = jnp.bfloat16
F32 = jnp.float32
HBM = pl.BlockSpec(memory_space=pl.ANY)
VMEM = pl.BlockSpec(memory_space=pltpu.VMEM)
LIMIT = 60 * 2**20


class Spot:
    def __init__(self):
        shard = lax.axis_index("shard")
        self.lo = lax.axis_index("dp")
        self.hi = lax.axis_index("tensor")
        self.x = self.hi * 2 + self.lo
        self.y = shard // 8
        self.z = (shard // 2) % 4
        self.c = shard % 2

    def dev(self, dx=0, dy=0, dz=0, other=False):
        x = (self.x + dx) % 4
        y = (self.y + dy) % 4
        z = (self.z + dz) % 4
        c = 1 - self.c if other else self.c
        return ((y * 4 + z) * 2 + c, x % 2, x // 2)

    def dp_mate(self):
        return ((self.y * 4 + self.z) * 2 + self.c, 1 - self.lo, self.hi)

    def column(self, step):
        flat = (self.y * 4 + self.z + step + 16) % 16
        return (flat * 2 + self.c, self.lo, self.hi)


def greet(devices):
    barrier = pltpu.get_barrier_semaphore()
    for device in devices:
        pl.semaphore_signal(barrier, inc=1, device_id=device, device_id_type=MESH)
    pl.semaphore_wait(barrier, len(devices))


class Wires:
    def __init__(self, send, recv, local):
        self.send, self.recv, self.here = send, recv, local
        self.count, self.near = 0, 0
        self.sent = []

    def push(self, src, dst, device):
        i = self.count
        self.count += 1
        copy = pltpu.make_async_remote_copy(
            src_ref=src,
            dst_ref=dst,
            send_sem=self.send.at[i],
            recv_sem=self.recv.at[i],
            device_id=device,
            device_id_type=MESH,
        )
        copy.start()
        self.sent.append(copy)
        return copy

    def local(self, src, dst):
        copy = pltpu.make_async_copy(src, dst, self.here.at[self.near])
        self.near += 1
        copy.start()
        return copy

    def sent_now(self, copy):
        copy.wait_send()
        self.sent = [other for other in self.sent if other is not copy]

    def drain(self):
        for copy in self.sent:
            copy.wait_send()


def wires_scratch(remote, local):
    return [
        pltpu.SemaphoreType.DMA((remote,)),
        pltpu.SemaphoreType.DMA((remote,)),
        pltpu.SemaphoreType.DMA((max(local, 1),)),
    ]


def by_rows(count, step, body):
    def run(i, _):
        body(pl.ds(pl.multiple_of(i * step, step), step))
        return 0

    lax.fori_loop(0, count // step, run, 0)


def add_into(dst, *sources):
    def body(rows):
        total = dst[rows, :].astype(F32)
        for source in sources:
            total = total + source[rows, :].astype(F32)
        dst[rows, :] = total.astype(dst.dtype)

    by_rows(dst.shape[0], 16, body)


def run_all(*parts):
    parts = list(parts)
    while parts:
        for part in list(parts):
            if next(part, StopIteration) is StopIteration:
                parts.remove(part)


def plane_gather(w, spot, pieces, out):
    y, z, c = spot.y, spot.z, spot.c
    rows = pl.ds(pl.multiple_of(c * 64, 64), 64)
    swaps, owns = [], []
    for source, size, low in pieces:
        theirs = pl.ds(pl.multiple_of((spot.lo * 2 + 1 - c) * size, size), size)
        mine = pl.ds(pl.multiple_of((spot.lo * 2 + c) * size, size), size)
        at = out.at[y, z, rows, pl.ds(low, size)]
        swaps.append(w.push(source.at[:, theirs], at, spot.dev(other=True)))
        owns.append(w.local(source.at[:, mine], at))
    yield
    for swap, own in zip(swaps, owns):
        swap.wait_recv()
        own.wait()
    ym, yp, zm, zp = (y + 3) % 4, (y + 1) % 4, (z + 3) % 4, (z + 1) % 4
    to_zp, to_zm = spot.dev(dz=1), spot.dev(dz=-1)
    to_yp, to_ym = spot.dev(dy=1), spot.dev(dy=-1)
    a, b = pl.ds(0, 64), pl.ds(64, 64)
    mine_a, mine_b = out.at[y, z, a], out.at[y, z, b]
    a1 = w.push(mine_a, mine_a, to_zp)
    a2 = w.push(mine_a, mine_a, to_zm)
    b1 = w.push(mine_b, mine_b, to_yp)
    b2 = w.push(mine_b, mine_b, to_ym)
    yield
    a1.wait_recv()
    part = out.at[y, zm, pl.ds(0, 32)]
    a3 = w.push(part, part, to_zp)
    b1.wait_recv()
    part = out.at[ym, z, pl.ds(64, 32)]
    b3 = w.push(part, part, to_yp)
    a2.wait_recv()
    part = out.at[y, zp, pl.ds(32, 32)]
    a4 = w.push(part, part, to_zm)
    b2.wait_recv()
    part = out.at[yp, z, pl.ds(96, 32)]
    b4 = w.push(part, part, to_ym)
    yield
    a3.wait_recv()
    a4.wait_recv()
    part = out.at[y, :, a]
    a5 = w.push(part, part, to_yp)
    a6 = w.push(part, part, to_ym)
    b3.wait_recv()
    b4.wait_recv()
    part = out.at[:, z, b]
    b5 = w.push(part, part, to_zp)
    b6 = w.push(part, part, to_zm)
    yield
    a5.wait_recv()
    part = out.at[ym, pl.ds(0, 2), a]
    a7 = w.push(part, part, to_yp)
    b5.wait_recv()
    part = out.at[pl.ds(0, 2), zm, b]
    b7 = w.push(part, part, to_zp)
    a6.wait_recv()
    part = out.at[yp, pl.ds(2, 2), a]
    a8 = w.push(part, part, to_ym)
    b6.wait_recv()
    part = out.at[pl.ds(2, 2), zp, b]
    b8 = w.push(part, part, to_zm)
    yield
    for copy in (a7, b7, a8, b8):
        copy.wait_recv()


def plane_sum_scratch(columns, resident):
    kept = [
        pltpu.VMEM((2, 2, 64, columns), BF),
        pltpu.VMEM((2, 2, 64, columns), BF),
        pltpu.VMEM((2, 4, 64, columns), BF),
    ]
    return ([] if resident else kept) + [
        pltpu.VMEM((2, 2, 2, 64, columns), BF),
        pltpu.VMEM((2, 2, 4, 64, columns), BF),
        pltpu.VMEM((2, 2, 32, columns), BF),
        pltpu.VMEM((2, 2, 64, columns), BF),
        pltpu.VMEM((128, columns), BF),
        pltpu.VMEM((2, 64, columns), BF),
    ]


def plane_sum(w, spot, part, scratch, resident=False):
    in1, in2, in3, in4, full, both = scratch[-6:]
    c = spot.c
    rows = (pl.ds(0, 64), pl.ds(64, 64))
    lanes = ((spot.y, spot.z), (spot.z, spot.y))
    steps = (("dy", "dz"), ("dz", "dy"))

    def view(h, k, low, size):
        at = (lanes[h][0] + k) % 4
        if h == 0:
            return part.at[at, pl.ds(low, size), rows[h]]
        return part.at[pl.ds(low, size), at, rows[h]]

    def held(h, j):
        if not resident:
            return scratch[2].at[h, j]
        if h == 0:
            return part.at[spot.y, j, rows[h]]
        return part.at[j, spot.z, rows[h]]

    def to(h, stage, step):
        return spot.dev(**{steps[h][stage]: step})

    loads, first, second, early = [], [], [], []
    for h in range(2):
        first.append(
            (
                w.push(view(h, 2, 0, 2), in1.at[h, 0], to(h, 0, 1)),
                w.push(view(h, 2, 2, 2), in1.at[h, 1], to(h, 0, -1)),
            )
        )
    for h in range(2):
        if resident:
            plus, minus = view(h, 1, 0, 2), view(h, 3, 2, 2)
            loads.append((plus, minus))
            continue
        plus, minus = scratch[0].at[h], scratch[1].at[h]
        loads.append(
            (
                plus,
                minus,
                w.local(view(h, 1, 0, 2), plus),
                w.local(view(h, 3, 2, 2), minus),
                w.local(view(h, 0, 0, 4), scratch[2].at[h]),
            )
        )
    yield
    for h in range(2):
        plus, minus = loads[h][:2]
        if not resident:
            loads[h][2].wait()
        first[h][0].wait_recv()
        for j in range(2):
            add_into(plus.at[j], in1.at[h, 0, j])
        one = w.push(plus, in2.at[h, 0, pl.ds(0, 2)], to(h, 0, 1))
        if not resident:
            loads[h][3].wait()
        first[h][1].wait_recv()
        for j in range(2):
            add_into(minus.at[j], in1.at[h, 1, j])
        two = w.push(minus, in2.at[h, 1, pl.ds(2, 2)], to(h, 0, -1))
        second.append((one, two))
    for h in range(2):
        early.append(
            (
                w.push(view(h, 1, 2, 2), in2.at[h, 0, pl.ds(2, 2)], to(h, 0, 1)),
                w.push(view(h, 3, 0, 2), in2.at[h, 1, pl.ds(0, 2)], to(h, 0, -1)),
            )
        )
    yield
    third, early3 = [], []
    for h in range(2):
        if not resident:
            loads[h][4].wait()
        for copy in early[h] + second[h]:
            copy.wait_recv()
        at = [(lanes[h][1] + k) % 4 for k in range(4)]
        add_into(held(h, at[2]), in2.at[h, 0, at[2]], in2.at[h, 1, at[2]])
        far = held(h, at[2])
        third.append(
            (
                w.push(far.at[pl.ds(0, 32)], in3.at[h, 0], to(h, 1, 1)),
                w.push(far.at[pl.ds(32, 32)], in3.at[h, 1], to(h, 1, -1)),
            )
        )
        add_into(held(h, at[1]), in2.at[h, 0, at[1]], in2.at[h, 1, at[1]])
        one = w.push(held(h, at[1]).at[pl.ds(32, 32)], in4.at[h, 0, pl.ds(32, 32)], to(h, 1, 1))
        add_into(held(h, at[3]), in2.at[h, 0, at[3]], in2.at[h, 1, at[3]])
        two = w.push(held(h, at[3]).at[pl.ds(0, 32)], in4.at[h, 1, pl.ds(0, 32)], to(h, 1, -1))
        early3.append((one, two))
        add_into(held(h, at[0]), in2.at[h, 0, at[0]], in2.at[h, 1, at[0]])
    yield
    fourth = []
    for h in range(2):
        at = [(lanes[h][1] + k) % 4 for k in range(4)]
        third[h][0].wait_recv()
        piece = held(h, at[1]).at[pl.ds(0, 32)]
        add_into(piece, in3.at[h, 0])
        one = w.push(piece, in4.at[h, 0, pl.ds(0, 32)], to(h, 1, 1))
        third[h][1].wait_recv()
        piece = held(h, at[3]).at[pl.ds(32, 32)]
        add_into(piece, in3.at[h, 1])
        two = w.push(piece, in4.at[h, 1, pl.ds(32, 32)], to(h, 1, -1))
        fourth.append((one, two))
    yield
    for h in range(2):
        for copy in early3[h] + fourth[h]:
            copy.wait_recv()
        mine = held(h, lanes[h][1])
        target = full.at[rows[h]]

        def body(r):
            total = mine[r, :].astype(F32) + in4[h, 0, r, :].astype(F32)
            target[r, :] = (total + in4[h, 1, r, :].astype(F32)).astype(BF)

        by_rows(64, 16, body)
    theirs = full.at[pl.ds(pl.multiple_of((1 - c) * 64, 64), 64)]
    mine = full.at[pl.ds(pl.multiple_of(c * 64, 64), 64)]
    swap = w.push(theirs, both.at[c], spot.dev(other=True))

    def keep(r):
        both[c, r, :] = mine[r, :]

    by_rows(64, 16, keep)
    yield
    swap.wait_recv()


def mate_share(w, spot, both, outs):
    copies = []
    for out, low, size in outs:
        for core in range(2):
            piece = both.at[core, :, pl.ds(low, size)]
            at = pl.ds(pl.multiple_of((spot.lo * 2 + core) * size, size), size)
            copies.append((w.local(piece, out.at[:, at]), w.push(piece, out.at[:, at], spot.dp_mate())))
    yield
    for near, far in copies:
        near.wait()
        far.wait_recv()


def column_sum_scratch():
    return [
        pltpu.VMEM((4, 128, WIDTH), BF),
        pltpu.VMEM((4, 128, WIDTH), BF),
        pltpu.VMEM((2, 64, WIDTH), BF),
        pltpu.VMEM((2, 128, WIDTH), BF),
    ]


def column_sum(w, spot, part, scratch, finish, resident=False):
    own, got, in1, in2 = scratch
    x, c = spot.x, spot.c
    right, left = spot.dev(dx=1), spot.dev(dx=-1)
    places = [((x + k) % 4 % 2, (x + k) % 4 // 2) for k in range(4)]
    swaps, loads = {}, {}
    for k in (2, 1, 3, 0):
        swaps[k] = w.push(part.at[1 - c, places[k][0], places[k][1]], got.at[k], spot.dev(other=True))
    if resident:
        own = [part.at[c, lo, hi] for lo, hi in places]
    else:
        for k in (2, 1, 3, 0):
            loads[k] = w.local(part.at[c, places[k][0], places[k][1]], own.at[k])
        own = [own.at[k] for k in range(4)]
    yield

    def merge(k):
        if not resident:
            loads[k].wait()
        swaps[k].wait_recv()
        add_into(own[k], got.at[k])

    low, high = pl.ds(0, 64), pl.ds(64, 64)
    merge(2)
    far1 = w.push(own[2].at[low], in1.at[0], right)
    far2 = w.push(own[2].at[high], in1.at[1], left)
    merge(1)
    one = w.push(own[1].at[high], in2.at[0, high], right)
    merge(3)
    two = w.push(own[3].at[low], in2.at[1, low], left)
    merge(0)
    yield
    far1.wait_recv()
    add_into(own[1].at[low], in1.at[0])
    three = w.push(own[1].at[low], in2.at[0, low], right)
    far2.wait_recv()
    add_into(own[3].at[high], in1.at[1])
    four = w.push(own[3].at[high], in2.at[1, high], left)
    yield
    for copy in (one, two, three, four):
        copy.wait_recv()

    def total(rows):
        return own[0][rows, :].astype(F32) + in2[0, rows, :].astype(F32) + in2[1, rows, :].astype(F32)

    finish(total)


def column_share(w, spot, mine, out):
    x, c = spot.x, spot.c
    right, left, mate = spot.dev(dx=1), spot.dev(dx=-1), spot.dev(other=True)

    def slot(k):
        at = (x + k + 4) % 4
        return out.at[c, at % 2, at // 2]

    low, high = pl.ds(0, 64), pl.ds(64, 64)
    own = w.local(mine, slot(0))
    a = w.push(mine.at[low], slot(0).at[low], right)
    b = w.push(mine.at[high], slot(0).at[high], left)
    d = w.push(mine, slot(0), mate)
    a2 = w.push(mine.at[high], slot(0).at[high], right)
    b2 = w.push(mine.at[low], slot(0).at[low], left)
    yield
    a.wait_recv()
    e = w.push(slot(-1).at[low], slot(-1).at[low], right)
    last = [w.push(slot(-1).at[low], slot(-1).at[low], mate)]
    b.wait_recv()
    g = w.push(slot(1).at[high], slot(1).at[high], left)
    last.append(w.push(slot(1).at[high], slot(1).at[high], mate))
    yield
    a2.wait_recv()
    last.append(w.push(slot(-1).at[high], slot(-1).at[high], mate))
    b2.wait_recv()
    last.append(w.push(slot(1).at[low], slot(1).at[low], mate))
    e.wait_recv()
    last.append(w.push(slot(2).at[low], slot(2).at[low], mate))
    g.wait_recv()
    last.append(w.push(slot(2).at[high], slot(2).at[high], mate))
    yield
    own.wait()
    for copy in [d] + last:
        copy.wait_recv()


def token_share(w, spot, block, out):
    own_at, far_at = spot.c * 2 + spot.lo, spot.c * 2 + 1 - spot.lo
    right, left, mate = spot.dev(dx=1), spot.dev(dx=-1), spot.dev(other=True)
    low, high = pl.ds(0, 128), pl.ds(128, 128)
    own = w.local(block, out.at[own_at])
    a = w.push(block.at[low], out.at[own_at, low], right)
    b = w.push(block.at[high], out.at[own_at, high], left)
    d = w.push(block, out.at[own_at], mate)
    yield
    a.wait_recv()
    part = out.at[far_at, low]
    e = w.push(part, part, mate)
    b.wait_recv()
    part = out.at[far_at, high]
    f = w.push(part, part, mate)
    yield
    own.wait()
    for copy in (d, e, f):
        copy.wait_recv()


def pair_share(w, spot, mine, out):
    own = w.local(mine, out.at[spot.hi])
    a = w.push(mine, out.at[spot.hi], spot.dev(dx=2))
    yield
    own.wait()
    a.wait_recv()


def neighbours(spot, x=False, yz=False, core=False, pair=False, far=False):
    found = []
    if x:
        found += [spot.dev(dx=1), spot.dev(dx=-1)]
    if yz:
        found += [spot.dev(dy=1), spot.dev(dy=-1), spot.dev(dz=1), spot.dev(dz=-1)]
    if core:
        found += [spot.dev(other=True)]
    if pair:
        found += [spot.dev(dx=2)]
    if far:
        found += [spot.dev(dy=2), spot.dev(dz=2)]
    return found


BLOCK = 256
SPAN = COLUMN + BLOCK
NT = (((1,), (1,)), ((), ()))
TN = (((0,), (0,)), ((), ()))
NN = (((1,), (0,)), ((), ()))


def dot(a, b, dims):
    return lax.dot_general(a, b, dims, preferred_element_type=F32)


def rms_of(rows):
    inverse = lax.rsqrt(jnp.mean(rows * rows, axis=-1, keepdims=True) + EPS)
    return rows * inverse, inverse


def turn_half(rows):
    half = HEAD // 2
    return jnp.concatenate([-rows[:, half:], rows[:, :half]], axis=-1)


def params(collective_id):
    return pltpu.CompilerParams(
        collective_id=collective_id, has_side_effects=True, vmem_limit_bytes=LIMIT
    )


def own_block(ref, spot):
    return ref.at[spot.c, spot.lo, spot.hi]


def place_rows(spot, lengths, freq, doc_row, doc_col, cosine, sine):
    first = (spot.y * 4 + spot.z - 1) * COLUMN
    rows = lax.broadcasted_iota(jnp.int32, (16, 128), 0) * 128 + first
    rows = rows + lax.broadcasted_iota(jnp.int32, (16, 128), 1)
    document = jnp.zeros((16, 128), jnp.int32)
    start = jnp.zeros((16, 128), jnp.int32)
    bound = jnp.int32(0)
    for d in range(lengths.shape[1]):
        bound = bound + lengths[0, d]
        passed = rows >= bound
        document = document + passed.astype(jnp.int32)
        start = jnp.where(passed, bound, start)
    document = jnp.where(rows >= 0, document, -1).astype(F32)
    place = (rows - start).astype(F32)
    for g in range(16):
        line = document[g : g + 1, :]
        at = slice(g * 128, (g + 1) * 128)
        doc_row[:, at] = line
        doc_col[at, :] = jnp.transpose(jnp.broadcast_to(line, (128, 128)))
        if g >= 8:
            down = jnp.transpose(jnp.broadcast_to(place[g : g + 1, :], (128, 128)))
            angles = down * freq[...]
            at = slice((g - 8) * 128, (g - 7) * 128)
            cosine[at, :] = jnp.cos(angles)
            sine[at, :] = jnp.sin(angles)


def turned_head(raw, scale, cosine, sine):
    unit = rms_of(raw)[0] * scale
    return (unit * cosine + turn_half(unit) * sine).astype(BF)


def forward_kernel(
    tok, cot, x_q, x_k, x_v, x_o, x_gains, x_gate, x_up, x_down, lengths, freq, q_gain, k_gain,
    normed1, o_a, o_w, w_b, cot_all, o_raw, o_query, o_kv, o_before, o_attended, o_inverse, mid, normed2, o_cosine, o_sine, gains, doc_row, o_docs,
    w_a, w_w, raw, query, kv, before, attended, inverse, cosine, sine, doc_col,
    tok_all, low1, roots, top, total, branch, got, in1, in2, low, send, recv, here,
):
    spot = Spot()
    greet(neighbours(spot, x=True, yz=True, core=True) + [spot.column(1), spot.column(-1)])
    w = Wires(send, recv, here)
    first_pieces = ((x_q, 256, 0), (x_k, 128, 256), (x_v, 128, 384), (x_gains, 128, 512))
    take_a = plane_gather(w, spot, first_pieces, w_a)
    take_w = plane_gather(w, spot, ((x_o, 256, 0),), w_w)
    take_b = plane_gather(w, spot, ((x_gate, 768, 0), (x_up, 768, 768), (x_down, 768, 1536)), w_b)
    take_tok = token_share(w, spot, tok, tok_all)
    take_cot = token_share(w, spot, cot, cot_all)
    keeps = []

    def keep(source, target):
        keeps.append(w.local(source, target))

    def go(*parts):
        for part in parts:
            next(part, None)

    go(take_a, take_tok, take_a, take_w, take_b)
    place_rows(spot, lengths, freq, doc_row, doc_col, cosine, sine)
    keep(cosine, o_cosine)
    keep(sine, o_sine)
    keep(doc_col, o_docs)
    go(take_a, take_a, take_w, take_tok, take_a, take_tok, take_w)

    def roots_of(i, _):
        rows = pl.ds(pl.multiple_of(i * 32, 32), 32)
        values = tok_all[i // 8, pl.ds(pl.multiple_of(i % 8 * 32, 32), 32), :].astype(F32)
        roots[rows, :] = lax.rsqrt(jnp.mean(values * values, axis=-1, keepdims=True) + EPS)
        return 0

    lax.fori_loop(0, 32, roots_of, 0)
    go(take_a, take_cot, take_b, take_w)
    keep(w_a, o_a)
    for i in range(16):
        block = jnp.transpose(w_a[i // 4, i % 4, :, 512:640].astype(F32))
        gains[:, i * 128 : (i + 1) * 128] = block[0:2, :]

    def norm_rows(i, _):
        rows = pl.ds(pl.multiple_of(i * 32, 32), 32)
        values = tok_all[i // 8, pl.ds(pl.multiple_of(i % 8 * 32, 32), 32), :].astype(F32)
        low1[rows, :] = (values * roots[rows, :] * gains[0:1, :]).astype(BF)
        return 0

    lax.fori_loop(0, 32, norm_rows, 0)
    keep(low1, normed1)

    def project_kv(i, _):
        rows = pl.ds(pl.multiple_of(i * BLOCK, BLOCK), BLOCK)
        out = dot(low1[rows, :], w_a[:, :, :, 256:512].reshape(WIDTH, 256), NN)
        raw[rows, 256:512] = out
        kv[rows, :HEAD] = turned_head(out[:, :HEAD], k_gain[...].astype(F32), cosine[rows, :], sine[rows, :])
        kv[rows, HEAD:] = out[:, HEAD:].astype(BF)
        return 0

    def project_q(i, _):
        rows = pl.ds(pl.multiple_of(i * BLOCK, BLOCK), BLOCK)
        out = dot(low1[rows, :], w_a[:, :, :, 0:256].reshape(WIDTH, 256), NN)
        raw[rows, 0:256] = out
        for h in range(2):
            span = slice(h * HEAD, (h + 1) * HEAD)
            query[rows, span] = turned_head(out[:, span], q_gain[...].astype(F32), cosine[rows, :], sine[rows, :])
        return 0

    lax.fori_loop(0, 4, project_kv, 0)
    pass_kv = w.push(kv, before, spot.column(1))
    keep(kv, o_kv)
    go(take_w, take_b)
    lax.fori_loop(0, 4, project_q, 0)
    keep(raw, o_raw)
    keep(query, o_query)
    go(take_cot)

    def weights_of(i, h, keys, docs, causal):
        rows = slice(i * BLOCK, (i + 1) * BLOCK)
        scores = dot(query[rows, h * HEAD : (h + 1) * HEAD], keys, NT) * SCALE
        valid = doc_col[COLUMN + i * BLOCK : COLUMN + (i + 1) * BLOCK, 0:1] == docs
        if causal:
            row = lax.broadcasted_iota(jnp.int32, scores.shape, 0) + i * BLOCK
            valid = valid & (lax.broadcasted_iota(jnp.int32, scores.shape, 1) <= row)
        return jnp.where(valid, jnp.exp(scores), 0.0)

    for i in range(4):
        rows, end = slice(i * BLOCK, (i + 1) * BLOCK), (i + 1) * BLOCK
        for h in range(2):
            weight = weights_of(i, h, kv[0:end, :HEAD], doc_row[:, COLUMN : COLUMN + end], True)
            total[rows, h : h + 1] = jnp.sum(weight, axis=-1, keepdims=True)
            top[rows, h * HEAD : (h + 1) * HEAD] = dot(weight.astype(BF), kv[0:end, HEAD:], NN)
    pass_kv.wait_recv()
    keep(before, o_before)
    go(take_w, take_b)
    keep(w_w, o_w)
    for i in range(4):
        rows, low_key = slice(i * BLOCK, (i + 1) * BLOCK), i * BLOCK
        for h in range(2):
            span = slice(h * HEAD, (h + 1) * HEAD)
            weight = weights_of(i, h, before[low_key:, :HEAD], doc_row[:, low_key:COLUMN], False)
            back = 1.0 / (total[rows, h : h + 1] + jnp.sum(weight, axis=-1, keepdims=True))
            inverse[rows, h : h + 1] = back
            attended[rows, span] = ((top[rows, span] + dot(weight.astype(BF), before[low_key:, HEAD:], NN)) * back).astype(BF)
    keep(attended, o_attended)
    keep(inverse, o_inverse)

    def branch_of(core):
        def one(lo, _):
            rows = pl.ds(pl.multiple_of((core * 2 + lo) * BLOCK, BLOCK), BLOCK)
            out = dot(attended[rows, :], w_w[...].reshape(WIDTH, 256), NT)
            branch[core, lo] = out.astype(BF).reshape(2, 128, WIDTH)
            return 0

        lax.fori_loop(0, 2, one, 0)

    def finish(add):
        def body(rows):
            base = tok[pl.ds(pl.multiple_of(spot.hi * 128 + rows.start, 16), 16), :].astype(F32)
            middle = base + add(rows)
            mid[rows, :] = middle
            root = lax.rsqrt(jnp.mean(middle * middle, axis=-1, keepdims=True) + EPS)
            low[rows, :] = (middle * root * gains[1:2, :]).astype(BF)

        by_rows(128, 16, body)

    branch_of(1 - spot.c)
    fold = column_sum(w, spot, branch, (None, got, in1, in2), finish, resident=True)
    go(fold)
    branch_of(spot.c)
    go(fold, fold, fold, take_cot)
    share = column_share(w, spot, low, normed2)
    go(share, take_b, share, share, take_b, share)
    assert all(g.gi_frame is None for g in (take_a, take_w, take_b, take_tok, take_cot, fold, share))
    for copy in keeps:
        copy.wait()
    w.drain()


def forward_call(*args):
    def shape(*sizes, kind=BF):
        return jax.ShapeDtypeStruct(sizes, kind)

    kept = (
        shape(4, 4, 128, 640),
        shape(4, 4, 128, 256),
        shape(COLUMN, 512, kind=F32),
        shape(COLUMN, 256),
        shape(COLUMN, 256),
        shape(COLUMN, 256),
        shape(COLUMN, 256),
        shape(COLUMN, 2, kind=F32),
        shape(COLUMN, HEAD, kind=F32),
        shape(COLUMN, HEAD, kind=F32),
        shape(2 * COLUMN, 128, kind=F32),
    )
    outs = (
        (shape(COLUMN, WIDTH), HBM),
        (kept[0], HBM),
        (kept[1], HBM),
        (shape(4, 4, 128, 2304), HBM),
        (shape(4, 256, WIDTH), HBM),
        *((k, HBM) for k in kept[2:8]),
        (shape(128, WIDTH, kind=F32), VMEM),
        (shape(2, 2, 2, 128, WIDTH), HBM),
        (kept[8], HBM),
        (kept[9], HBM),
        (shape(2, WIDTH, kind=F32), VMEM),
        (shape(1, 2 * COLUMN, kind=F32), VMEM),
        (kept[10], HBM),
    )
    return pl.pallas_call(
        forward_kernel,
        out_shape=tuple(o[0] for o in outs),
        in_specs=[VMEM] * 10 + [pl.BlockSpec(memory_space=pltpu.SMEM)] + [VMEM] * 3,
        out_specs=tuple(o[1] for o in outs),
        scratch_shapes=[pltpu.VMEM(o.shape, o.dtype) for o in kept]
        + [
            pltpu.VMEM((4, 256, WIDTH), BF),
            pltpu.VMEM((COLUMN, WIDTH), BF),
            pltpu.VMEM((COLUMN, 1), F32),
            pltpu.VMEM((COLUMN, 256), F32),
            pltpu.VMEM((COLUMN, 2), F32),
            pltpu.VMEM((2, 2, 2, 128, WIDTH), BF),
        ]
        + column_sum_scratch()[1:]
        + [pltpu.VMEM((128, WIDTH), BF)]
        + wires_scratch(90, 30),
        compiler_params=params(1),
        name="forward",
    )(*args)


def rms_back(total, base, gain, rows, extra, out, gain_grad):
    values = base[rows, :].astype(F32)
    inverse = lax.rsqrt(jnp.mean(values * values, axis=-1, keepdims=True) + EPS)
    normed = values * inverse
    grad = total(rows)
    scaled = grad * gain[...]
    back = inverse * (scaled - normed * jnp.mean(scaled * normed, axis=-1, keepdims=True))
    gain_grad[...] += jnp.sum(grad * normed, axis=0, keepdims=True)
    out[rows, :] = (extra[rows, :].astype(F32) + back).astype(out.dtype)


def turn_kernel(
    normed, cot, w_b, mid, cot_own, gain, dmid, d_branch, mixed, g_in, gain_grad, both_out,
    nv, cv, wv, hidden, d_both, part, g_down, g_part, mixed_part, both_n, both_c, both_d, got, in1, in2, low, top,
    p0, p1, p2, p3, p4, p5, send, recv, here, tiles,
):
    spot = Spot()
    w = Wires(send, recv, here)
    first = w.local(w_b, wv)

    def block(i):
        rows = pl.ds(pl.multiple_of(i * BLOCK, BLOCK), BLOCK)
        one = pltpu.make_async_copy(normed.at[rows], nv.at[rows], tiles.at[0, i])
        return one, pltpu.make_async_copy(cot.at[rows], cv.at[rows], tiles.at[1, i])

    for i in range(4):
        for copy in block(i):
            copy.start()
    load = w.local(cot_own.at[spot.hi], top)
    greet(neighbours(spot, x=True, yz=True, core=True))
    gain_grad[...] = jnp.zeros_like(gain_grad)
    first.wait()

    def weight(low_column, size):
        return wv[:, :, :, low_column : low_column + size].reshape(WIDTH, size)

    for i in range(4):
        for copy in block(i):
            copy.wait()

    def two(k):
        at = (spot.x + k) % 4
        lo, hi = at % 2, at // 2
        theirs = pl.ds(pl.multiple_of(((1 - spot.c) * 2 + lo) * 256 + hi * 128, 128), 128)
        mine = pl.ds(pl.multiple_of((spot.c * 2 + lo) * 256 + hi * 128, 128), 128)
        return lo, hi, theirs, mine

    def units(k):
        _, _, theirs, mine = two(k)
        both_n[0:128, :] = nv[theirs, :]
        both_n[128:, :] = nv[mine, :]
        both_c[0:128, :] = cv[theirs, :]
        both_c[128:, :] = cv[mine, :]

        def one(j, _):
            a = pl.ds(pl.multiple_of(j * 256, 256), 256)
            b = pl.ds(pl.multiple_of(j * 256 + 768, 256), 256)
            d = pl.ds(pl.multiple_of(j * 256 + 1536, 256), 256)
            gate = dot(both_n[...], wv[:, :, :, a].reshape(WIDTH, 256), NN)
            up = dot(both_n[...], wv[:, :, :, b].reshape(WIDTH, 256), NN)
            d_hidden = dot(both_c[...], wv[:, :, :, d].reshape(WIDTH, 256), NN)
            sigma = lax.logistic(gate)
            active = gate * sigma
            unit = (active * up).astype(BF)
            d_gate = (d_hidden * up * sigma * (1.0 + gate * (1.0 - sigma))).astype(BF)
            d_up = (d_hidden * active).astype(BF)
            for half, rows in ((slice(0, 128), theirs), (slice(128, 256), mine)):
                hidden[rows, a] = unit[half, :]
                d_both[rows, a] = d_gate[half, :]
                d_both[rows, b] = d_up[half, :]
            return 0

        lax.fori_loop(0, 3, one, 0)

    def back(k):
        lo, hi, theirs, mine = two(k)
        both_d[0:128, :] = d_both[theirs, :]
        both_d[128:, :] = d_both[mine, :]
        out = dot(both_d[...], weight(0, 1536), NT).astype(BF)
        part[1 - spot.c, lo, hi] = out[:128]
        part[spot.c, lo, hi] = out[128:]
        swaps[k] = w.push(part.at[1 - spot.c, lo, hi], got.at[k], spot.dev(other=True))

    swaps = {}

    def own(k):
        lo, hi, _, _ = two(k)
        return part.at[spot.c, lo, hi]

    def merge(k):
        swaps[k].wait_recv()
        add_into(own(k), got.at[k])

    def finish(total):
        load.wait()

        def body(rows):
            rms_back(total, mid, gain, rows, top, dmid, gain_grad)
            low[rows, :] = dmid[rows, :].astype(BF)

        by_rows(128, 16, body)

    def go(*parts):
        for one in parts:
            next(one, None)

    def down_tile(t, _):
        lanes = pl.ds(pl.multiple_of(t * BLOCK, BLOCK), BLOCK)
        out = dot(cv[:, lanes], hidden[...], TN)
        g_down[t // 2, pl.ds(t % 2 * 2, 2)] = out.astype(BF).reshape(2, 128, 768)
        return 0

    def in_copy(t):
        at = (t // 2, pl.ds(t % 2 * 2, 2))
        return pltpu.make_async_copy(g_part.at[at], g_in.at[at], tiles.at[2, t])

    def in_tile(t, _):
        lanes = pl.ds(pl.multiple_of(t * BLOCK, BLOCK), BLOCK)
        out = dot(nv[:, lanes], d_both[...], TN)
        g_part[t // 2, pl.ds(t % 2 * 2, 2)] = out.astype(BF).reshape(2, 128, 1536)
        in_copy(t).start()
        return 0

    def mixed_block(i, _):
        rows = pl.ds(pl.multiple_of(i * BLOCK, BLOCK), BLOCK)
        out = dot(hidden[rows, :], weight(1536, 768), NT)
        mixed_part[i // 2, i % 2] = out.astype(BF).reshape(2, 128, WIDTH)
        return 0

    right, left = spot.dev(dx=1), spot.dev(dx=-1)
    lows, highs = pl.ds(0, 64), pl.ds(64, 64)
    units(2)
    back(2)
    units(1)
    merge(2)
    far1 = w.push(own(2).at[lows], in1.at[0], right)
    far2 = w.push(own(2).at[highs], in1.at[1], left)
    back(1)
    units(3)
    merge(1)
    one = w.push(own(1).at[highs], in2.at[0, highs], right)
    back(3)
    units(0)
    merge(3)
    two_ = w.push(own(3).at[lows], in2.at[1, lows], left)
    far1.wait_recv()
    add_into(own(1).at[lows], in1.at[0])
    three = w.push(own(1).at[lows], in2.at[0, lows], right)
    far2.wait_recv()
    add_into(own(3).at[highs], in1.at[1])
    four = w.push(own(3).at[highs], in2.at[1, highs], left)
    back(0)
    lax.fori_loop(0, 8, down_tile, 0)
    down = plane_sum(w, spot, g_down, (p0, p1, p2, p3, p4, p5), resident=True)
    go(down)
    merge(0)
    for copy in (one, two_, three, four):
        copy.wait_recv()
    mine_ref = own(0)

    def total(rows):
        return mine_ref[rows, :].astype(F32) + in2[0, rows, :].astype(F32) + in2[1, rows, :].astype(F32)

    finish(total)
    share = column_share(w, spot, low, d_branch)
    go(share)
    lax.fori_loop(0, 2, in_tile, 0)
    go(down, share)
    lax.fori_loop(2, 5, in_tile, 0)
    go(down, share)
    lax.fori_loop(5, 8, in_tile, 0)
    go(down)
    lax.fori_loop(0, 4, mixed_block, 0)
    keep = w.local(mixed_part, mixed)
    go(share, down, down)
    assert share.gi_frame is None and down.gi_frame is None
    last = w.local(p5, both_out)
    for t in range(8):
        in_copy(t).wait()
    keep.wait()
    last.wait()
    w.drain()


def turn_call(normed, cot, w_b, mid, cot_own, gain):
    blocks = jax.ShapeDtypeStruct((2, 2, 2, 128, WIDTH), BF)
    return pl.pallas_call(
        turn_kernel,
        out_shape=(
            jax.ShapeDtypeStruct((128, WIDTH), F32),
            blocks,
            blocks,
            jax.ShapeDtypeStruct((4, 4, 128, 1536), BF),
            jax.ShapeDtypeStruct((1, WIDTH), F32),
            jax.ShapeDtypeStruct((2, 64, 768), BF),
        ),
        in_specs=[HBM, HBM, HBM, VMEM, HBM, VMEM],
        out_specs=(VMEM, HBM, HBM, HBM, VMEM, HBM),
        scratch_shapes=[
            pltpu.VMEM((COLUMN, WIDTH), BF),
            pltpu.VMEM((COLUMN, WIDTH), BF),
            pltpu.VMEM((4, 4, 128, 2304), BF),
            pltpu.VMEM((COLUMN, 768), BF),
            pltpu.VMEM((COLUMN, 1536), BF),
            pltpu.VMEM((2, 2, 2, 128, WIDTH), BF),
            pltpu.VMEM((4, 4, 128, 768), BF),
            pltpu.VMEM((4, 4, 128, 1536), BF),
            pltpu.VMEM((2, 2, 2, 128, WIDTH), BF),
            pltpu.VMEM((BLOCK, WIDTH), BF),
            pltpu.VMEM((BLOCK, WIDTH), BF),
            pltpu.VMEM((BLOCK, 1536), BF),
        ]
        + column_sum_scratch()[1:]
        + [pltpu.VMEM((128, WIDTH), BF)] * 2
        + plane_sum_scratch(768, True)
        + wires_scratch(64, 12)
        + [pltpu.SemaphoreType.DMA((3, 8))],
        compiler_params=params(4),
        name="turn",
    )(normed, cot, w_b, mid, cot_own, gain)


def sum_everywhere(w, spot, vector, pair, lines):
    a = w.push(vector, pair, spot.dev(other=True))
    yield
    a.wait_recv()
    w.sent_now(a)
    vector[...] = vector[...] + pair[...]
    yield
    for stage, (axis, at) in enumerate((("dx", spot.x), ("dy", spot.y), ("dz", spot.z))):
        slots = lines.at[stage]
        slots[at] = vector[...]
        copies = [w.push(vector, slots.at[at], spot.dev(**{axis: k})) for k in (1, 2, 3)]
        yield
        for copy in copies:
            copy.wait_recv()
            w.sent_now(copy)
        vector[...] = slots[0] + slots[1] + slots[2] + slots[3]
        yield


def as_row(column):
    return jnp.transpose(jnp.broadcast_to(column, (column.shape[0], HEAD)))[0:1, :]


def close_kernel(
    d_branch, h_w, h_a, h_attended, h_query, h_before, h_kv, h_raw, h_cosine, h_sine, doc_row, h_docs, h_inverse, q_gain, k_gain,
    g_in, both_down, mixed, mid, dmid, tok, gain, normed1, g_mlp,
    out, g_tok, o_gate, o_up, o_down, o_q, o_k, o_v, o_out, vector,
    w_w, w_a, attended, query, before, kv, raw, cosine, sine, doc_col, inverse,
    db, do, dq, dkv, d_before, came, d_raw, part, g_out, got, in1, in2,
    m_own, m_got, m_in1, m_in2, result, base, gain_grad, low,
    a0, a1, a2, a3, a4, a5, a6, a7, a8, b0, b1, b2, b3, b4, b5, pair, lines, send, recv, here, tiles,
):
    spot = Spot()
    w = Wires(send, recv, here)

    def block(i):
        rows = pl.ds(pl.multiple_of(i * BLOCK, BLOCK), BLOCK)
        return pltpu.make_async_copy(d_branch.at[rows], db.at[rows], tiles.at[i])

    for i in range(4):
        block(i).start()
    fetched_w = w.local(h_w, w_w)
    fetched = [
        w.local(source, target)
        for source, target in (
            (h_attended, attended), (h_query, query), (h_before, before), (h_inverse, inverse), (h_docs, doc_col),
            (h_kv, kv), (h_raw, raw), (h_cosine, cosine), (h_sine, sine), (h_a, w_a),
        )
    ]
    load_tok = w.local(tok.at[spot.hi], base)
    greet(
        neighbours(spot, x=True, yz=True, core=True, pair=True, far=True)
        + [spot.column(1), spot.column(-1)]
    )

    def go(*parts):
        for one in parts:
            next(one, None)

    sum_in = plane_sum(w, spot, g_in, (a0, a1, a2, a3, a4, a5, a6, a7, a8))
    go(sum_in)

    def finish_out(total):
        def body(rows):
            result[rows, :] = (mid[rows, :] + total(rows)).astype(BF)

        by_rows(128, 16, body)

    fold_out = column_sum(w, spot, mixed, (m_own, m_got, m_in1, m_in2), finish_out)
    share_out = pair_share(w, spot, result, out)
    share_down = mate_share(w, spot, both_down, ((o_down, 0, 768),))
    go(fold_out, share_down)
    gain_grad[...] = jnp.zeros_like(gain_grad)
    vector[...] = jnp.zeros_like(vector)
    dkv[...] = jnp.zeros_like(dkv)

    fetched_w.wait()

    def upstream_of(i, _):
        block(i).wait()
        rows = pl.ds(pl.multiple_of(i * BLOCK, BLOCK), BLOCK)
        do[rows, :] = dot(db[rows, :], w_w[...], NN).astype(BF)
        return 0

    lax.fori_loop(0, 4, upstream_of, 0)
    go(fold_out)
    for copy in fetched:
        copy.wait()

    def tile_out(t, _):
        lanes = pl.ds(pl.multiple_of(t * BLOCK, BLOCK), BLOCK)
        at = (t // 2, pl.ds(t % 2 * 2, 2), slice(None), slice(512, 768))
        g_out[at] = dot(db[:, lanes], attended[...], TN).astype(BF).reshape(2, 128, 256)
        return 0

    def tile(t, _):
        lanes = pl.ds(pl.multiple_of(t * BLOCK, BLOCK), BLOCK)
        at = (t // 2, pl.ds(t % 2 * 2, 2), slice(None), slice(0, 512))
        g_out[at] = dot(db[:, lanes], d_raw[...], TN).astype(BF).reshape(2, 128, 512)
        return 0


    def attend_back(i, keys_of, docs, causal, grads, fresh):
        rows = slice(i * BLOCK, (i + 1) * BLOCK)
        product = attended[rows, :].astype(F32) * do[rows, :].astype(F32)
        valid = docs == doc_row[:, COLUMN + i * BLOCK : COLUMN + (i + 1) * BLOCK]
        if causal:
            row = lax.broadcasted_iota(jnp.int32, valid.shape, 0)
            valid = valid & (row <= lax.broadcasted_iota(jnp.int32, valid.shape, 1) + i * BLOCK)
        for h in range(2):
            span = slice(h * HEAD, (h + 1) * HEAD)
            asked, upstream = query[rows, span], do[rows, span]
            back = as_row(inverse[rows, h : h + 1])
            delta = as_row(jnp.sum(product[:, span], axis=-1, keepdims=True))
            scores = dot(keys_of[:, :HEAD], asked, NT) * SCALE
            probs = jnp.where(valid, jnp.exp(scores), 0.0) * back
            d_probs = dot(keys_of[:, HEAD:], upstream, NT)
            d_scores = (probs * (d_probs - delta)).astype(BF)
            grads[:, :HEAD] += dot(d_scores, asked, NN) * SCALE
            grads[:, HEAD:] += dot(probs.astype(BF), upstream, NN)
            d_asked = dot(d_scores, keys_of[:, :HEAD], TN) * SCALE
            if fresh:
                dq[rows, span] = d_asked
            else:
                dq[rows, span] += d_asked

    for i in range(4):
        attend_back(
            i, before.at[i * BLOCK :], doc_col[i * BLOCK : COLUMN, 0:1], False, dkv.at[i * BLOCK : COLUMN], True
        )
    by_rows(COLUMN, 32, lambda r: d_before.__setitem__((r, slice(None)), dkv[r, :].astype(BF)))
    back_kv = w.push(d_before, came, spot.column(-1))
    go(fold_out)
    lax.fori_loop(0, 8, tile_out, 0)
    load_n1 = w.local(normed1, db)
    for i in range(4):
        end = (i + 1) * BLOCK
        attend_back(
            i, kv.at[0:end], doc_col[COLUMN : COLUMN + end, 0:1], True, dkv.at[COLUMN : COLUMN + end], False
        )
        if i == 1:
            go(fold_out, share_out)
    back_kv.wait_recv()
    go(sum_in)

    def project_back(i, _):
        rows = pl.ds(pl.multiple_of(i * BLOCK, BLOCK), BLOCK)
        own = pl.ds(pl.multiple_of(i * BLOCK + COLUMN, BLOCK), BLOCK)
        for h, scale in enumerate((q_gain, q_gain, k_gain)):
            span = slice(h * HEAD, (h + 1) * HEAD)
            if h < 2:
                grad = dq[rows, span]
            else:
                grad = dkv[own, :HEAD] + came[rows, :HEAD].astype(F32)
            grad = grad * cosine[rows, :] - turn_half(grad) * sine[rows, :]
            unit, root = rms_of(raw[rows, span])
            scaled = grad * scale[...].astype(F32)
            back = root * (scaled - unit * jnp.mean(scaled * unit, axis=-1, keepdims=True))
            d_raw[rows, span] = back.astype(BF)
            at = 32 + h // 2
            vector[at : at + 1, :] += jnp.sum(grad * unit, axis=0, keepdims=True)
        d_raw[rows, 3 * HEAD :] = (dkv[own, HEAD:] + came[rows, HEAD:].astype(F32)).astype(BF)
        return 0

    def norm_of(core):
        def one(lo, _):
            rows = pl.ds(pl.multiple_of((core * 2 + lo) * BLOCK, BLOCK), BLOCK)
            value = dot(d_raw[rows, :], w_a[:, :512], NT)
            part[core, lo] = value.astype(BF).reshape(2, 128, WIDTH)
            return 0

        lax.fori_loop(0, 2, one, 0)

    def finish(total):
        load_tok.wait()

        def body(rows):
            rms_back(total, base, gain, rows, dmid, low, gain_grad)

        by_rows(128, 16, body)

    lax.fori_loop(0, 4, project_back, 0)
    load_n1.wait()
    sum_out = plane_sum(w, spot, g_out, (b0, b1, b2, b3, b4, b5), resident=True)
    fold = column_sum(w, spot, part, (None, got, in1, in2), finish, resident=True)
    norm_of(1 - spot.c)
    go(fold)
    norm_of(spot.c)
    go(fold)
    lax.fori_loop(0, 8, tile, 0)
    go(sum_out, fold, sum_in, sum_out, fold)
    share_tok = pair_share(w, spot, low, g_tok)
    vector[16:32, :] = g_mlp[...]
    for i in range(16):
        vector[i : i + 1, :] = gain_grad[:, i * 128 : (i + 1) * 128]
    share_in = mate_share(w, spot, a8, ((o_gate, 0, 768), (o_up, 768, 768)))
    go(share_tok, sum_in, sum_in, sum_in, share_in)
    everywhere = sum_everywhere(w, spot, vector, pair, lines)
    go(everywhere, sum_out, everywhere, everywhere, sum_out, everywhere, everywhere, sum_out, sum_out)
    share_grads = mate_share(
        w, spot, b5, ((o_q, 0, 256), (o_k, 256, 128), (o_v, 384, 128), (o_out, 512, 256))
    )
    go(share_grads, everywhere, everywhere, share_out, share_down, everywhere, everywhere, share_in, share_tok, share_grads)
    for part_left in (sum_in, fold_out, share_out, share_down, fold, sum_out, everywhere, share_in, share_grads, share_tok):
        assert part_left.gi_frame is None
    w.drain()


def close_call(*args):
    def shape(*sizes, kind=BF):
        return jax.ShapeDtypeStruct(sizes, kind)

    return pl.pallas_call(
        close_kernel,
        out_shape=(
            shape(2, 128, WIDTH),
            shape(2, 128, WIDTH),
            shape(64, 3072),
            shape(64, 3072),
            shape(64, 3072),
            shape(64, 1024),
            shape(64, 512),
            shape(64, 512),
            shape(64, 1024),
            shape(40, 128, kind=F32),
        ),
        in_specs=[HBM] * 10 + [VMEM, HBM, HBM, VMEM, VMEM] + [HBM, VMEM, HBM, VMEM, VMEM, HBM, VMEM, HBM, VMEM],
        out_specs=(HBM,) * 9 + (VMEM,),
        scratch_shapes=[
            pltpu.VMEM((WIDTH, 256), BF),
            pltpu.VMEM((WIDTH, 640), BF),
            pltpu.VMEM((COLUMN, 256), BF),
            pltpu.VMEM((COLUMN, 256), BF),
            pltpu.VMEM((COLUMN, 256), BF),
            pltpu.VMEM((COLUMN, 256), BF),
            pltpu.VMEM((COLUMN, 512), F32),
            pltpu.VMEM((COLUMN, HEAD), F32),
            pltpu.VMEM((COLUMN, HEAD), F32),
            pltpu.VMEM((2 * COLUMN, 128), F32),
            pltpu.VMEM((COLUMN, 2), F32),
            pltpu.VMEM((COLUMN, WIDTH), BF),
            pltpu.VMEM((COLUMN, 256), BF),
            pltpu.VMEM((COLUMN, 256), F32),
            pltpu.VMEM((2 * COLUMN, 256), F32),
            pltpu.VMEM((COLUMN, 256), BF),
            pltpu.VMEM((COLUMN, 256), BF),
            pltpu.VMEM((COLUMN, 512), BF),
            pltpu.VMEM((2, 2, 2, 128, WIDTH), BF),
            pltpu.VMEM((4, 4, 128, 768), BF),
        ]
        + column_sum_scratch()[1:]
        + column_sum_scratch()
        + [
            pltpu.VMEM((128, WIDTH), BF),
            pltpu.VMEM((128, WIDTH), BF),
            pltpu.VMEM((1, WIDTH), F32),
            pltpu.VMEM((128, WIDTH), BF),
        ]
        + plane_sum_scratch(1536, False)
        + plane_sum_scratch(768, True)
        + [pltpu.VMEM((40, 128), F32), pltpu.VMEM((3, 4, 40, 128), F32)]
        + wires_scratch(100, 44)
        + [pltpu.SemaphoreType.DMA((4,))],
        compiler_params=params(6),
        name="close",
    )(*args)


def finish_kernel(*refs):
    ins, outs = refs[:10], refs[10:]
    vector = ins[9]
    outs[0][...] = ins[0][...]
    for source, target in zip(ins[1:9], outs[1:9]):
        target[...] = source[...].astype(F32)
    shard = lax.axis_index("shard")
    for first, target in ((0, outs[9]), (16, outs[10])):
        line = vector[pl.ds(first + shard // 2, 1), :]
        target[...] = jnp.where(shard % 2 == 0, line[:, 0:64], line[:, 64:128])
    outs[11][...] = vector[32:33, :]
    outs[12][...] = vector[33:34, :]


def finish_call(out, g_tok, *rest):
    tall = pl.BlockSpec((64, WIDTH), lambda i: (i, 0))
    grads, vector = rest[:-1], rest[-1]
    wide = [pl.BlockSpec((64, g.shape[1] // 4), lambda i: (0, i)) for g in grads]
    tops = [jax.ShapeDtypeStruct((1, n), F32) for n in (64, 64, 128, 128)]
    return pl.pallas_call(
        finish_kernel,
        grid=(4,),
        out_shape=(
            jax.ShapeDtypeStruct(out.shape, BF),
            jax.ShapeDtypeStruct(g_tok.shape, F32),
            *(jax.ShapeDtypeStruct(g.shape, F32) for g in grads),
            *tops,
        ),
        in_specs=[tall, tall] + wide + [VMEM],
        out_specs=[tall, tall] + wide + [VMEM] * 4,
        compiler_params=pltpu.CompilerParams(vmem_limit_bytes=LIMIT),
        name="finish",
    )(out, g_tok, *grads, vector)


def on_device(
    tokens, lengths, attn_norm, w_query, w_key, w_value, w_output, q_gain, k_gain, mlp_norm, w_gate, w_up, w_down, cotangent,
):
    freq = THETA ** (-jnp.arange(0, HEAD, 2).astype(F32) / HEAD)
    freq = jnp.concatenate([freq, freq])[None]
    both_gains = jnp.tile(jnp.pad(jnp.stack([attn_norm, mlp_norm], axis=1), ((0, 0), (0, 126))), (1, 4))
    (
        normed1, w_a, w_w, w_b, cot, raw, query, kv, before, attended, inverse, middle, normed2, cosine, sine, gains, doc_row, doc_col,
    ) = forward_call(
        tokens, cotangent, w_query, w_key, w_value, w_output.T, both_gains, w_gate, w_up, w_down.T, lengths, freq, q_gain[None], k_gain[None]
    )
    w_a, w_w = w_a.reshape(WIDTH, 640), w_w.reshape(WIDTH, 256)
    attn_gain, mlp_gain = gains[0:1], gains[1:2]
    d_middle, d_branch, mixed, g_in, g_mlp, both_down = turn_call(
        normed2.reshape(COLUMN, WIDTH),
        cot.reshape(COLUMN, WIDTH),
        w_b,
        middle,
        cotangent.reshape(2, 128, WIDTH),
        mlp_gain,
    )
    out, g_tokens, g_gate, g_up, g_down, g_query, g_key, g_value, g_output, sums = close_call(
        d_branch.reshape(COLUMN, WIDTH), w_w, w_a, attended, query, before, kv, raw, cosine, sine, doc_row, doc_col, inverse,
        q_gain[None], k_gain[None], g_in, both_down, mixed, middle, d_middle, tokens.reshape(2, 128, WIDTH), attn_gain,
        normed1, g_mlp.reshape(16, 128),
    )

    (
        out, g_tokens, g_gate, g_up, g_down, g_query, g_key, g_value, g_output, g_attn, g_mlp, g_q_gain, g_k_gain,
    ) = finish_call(
        out.reshape(256, WIDTH), g_tokens.reshape(256, WIDTH), g_gate, g_up, g_down, g_query, g_key, g_value, g_output, sums
    )
    return (
        out, g_tokens, g_attn[0], g_query, g_key, g_value, g_output.T, g_q_gain[0], g_k_gain[0], g_mlp[0], g_gate, g_up, g_down.T,
    )


def solution(mesh):
    rows = P(("shard", "dp"), None)
    down = P("shard", "tensor")
    across = P("tensor", "shard")
    one = P("shard")
    return jax.shard_map(
        on_device,
        mesh=mesh,
        in_specs=(rows, P(), one, down, down, down, across, P(), P(), one, down, down, across, rows),
        out_specs=(rows, rows, one, down, down, down, across, P(), P(), one, down, down, across),
        check_vma=False,
    )
```

```python
import functools

import jax
import jax.numpy as jnp
import numpy as np
from jax import lax
from jax.experimental import pallas as pl
from jax.experimental.pallas import tpu as pltpu
from jax.sharding import PartitionSpec as P

HEAD = 128
EPS = 1e-06
THETA = 1000000.0
SCALE = HEAD ** (-0.5)
WIDTH = 2048
COLUMN = 1024
MESH = pl.DeviceIdType.MESH
BF = jnp.bfloat16
F32 = jnp.float32
HBM = pl.BlockSpec(memory_space=pl.ANY)
VMEM = pl.BlockSpec(memory_space=pltpu.VMEM)
LIMIT = 60 * 2**20


class Spot:
    def __init__(self):
        shard = lax.axis_index("shard")
        self.lo = lax.axis_index("dp")
        self.hi = lax.axis_index("tensor")
        self.x = self.hi * 2 + self.lo
        self.y = shard // 8
        self.z = (shard // 2) % 4
        self.c = shard % 2

    def dev(self, dx=0, dy=0, dz=0, other=False):
        x = (self.x + dx) % 4
        y = (self.y + dy) % 4
        z = (self.z + dz) % 4
        c = 1 - self.c if other else self.c
        return ((y * 4 + z) * 2 + c, x % 2, x // 2)

    def dp_mate(self):
        return ((self.y * 4 + self.z) * 2 + self.c, 1 - self.lo, self.hi)

    def column(self, step):
        flat = (self.y * 4 + self.z + step + 16) % 16
        return (flat * 2 + self.c, self.lo, self.hi)


def greet(devices):
    barrier = pltpu.get_barrier_semaphore()
    for device in devices:
        pl.semaphore_signal(barrier, inc=1, device_id=device, device_id_type=MESH)
    pl.semaphore_wait(barrier, len(devices))


class Wires:
    def __init__(self, send, recv, local):
        self.send, self.recv, self.here = send, recv, local
        self.count, self.near = 0, 0
        self.sent = []

    def push(self, src, dst, device):
        i = self.count
        self.count += 1
        copy = pltpu.make_async_remote_copy(
            src_ref=src,
            dst_ref=dst,
            send_sem=self.send.at[i],
            recv_sem=self.recv.at[i],
            device_id=device,
            device_id_type=MESH,
        )
        copy.start()
        self.sent.append(copy)
        return copy

    def local(self, src, dst):
        copy = pltpu.make_async_copy(src, dst, self.here.at[self.near])
        self.near += 1
        copy.start()
        return copy

    def sent_now(self, copy):
        copy.wait_send()
        self.sent = [other for other in self.sent if other is not copy]

    def drain(self):
        assert self.count <= self.send.shape[0] and self.near <= self.here.shape[0]
        for copy in self.sent:
            copy.wait_send()


def wires_scratch(remote, local):
    return [
        pltpu.SemaphoreType.DMA((remote,)),
        pltpu.SemaphoreType.DMA((remote,)),
        pltpu.SemaphoreType.DMA((max(local, 1),)),
    ]


def by_rows(count, step, body):
    def run(i, _):
        body(pl.ds(pl.multiple_of(i * step, step), step))
        return 0

    lax.fori_loop(0, count // step, run, 0)


def add_into(dst, *sources):
    def body(rows):
        total = dst[rows, :].astype(F32)
        for source in sources:
            total = total + source[rows, :].astype(F32)
        dst[rows, :] = total.astype(dst.dtype)

    by_rows(dst.shape[0], 16, body)


def run_all(*parts):
    parts = list(parts)
    while parts:
        for part in list(parts):
            if next(part, StopIteration) is StopIteration:
                parts.remove(part)


def plane_gather(w, spot, pieces, out):
    y, z, c = spot.y, spot.z, spot.c
    rows = pl.ds(pl.multiple_of(c * 64, 64), 64)
    swaps, owns = [], []
    for source, size, low in pieces:
        theirs = pl.ds(pl.multiple_of((spot.lo * 2 + 1 - c) * size, size), size)
        mine = pl.ds(pl.multiple_of((spot.lo * 2 + c) * size, size), size)
        at = out.at[y, z, rows, pl.ds(low, size)]
        swaps.append(w.push(source.at[:, theirs], at, spot.dev(other=True)))
        owns.append(w.local(source.at[:, mine], at))
    yield
    for swap, own in zip(swaps, owns):
        swap.wait_recv()
        own.wait()
    ym, yp, zm, zp = (y + 3) % 4, (y + 1) % 4, (z + 3) % 4, (z + 1) % 4
    to_zp, to_zm = spot.dev(dz=1), spot.dev(dz=-1)
    to_yp, to_ym = spot.dev(dy=1), spot.dev(dy=-1)
    a, b = pl.ds(0, 64), pl.ds(64, 64)
    mine_a, mine_b = out.at[y, z, a], out.at[y, z, b]
    a1 = w.push(mine_a, mine_a, to_zp)
    a2 = w.push(mine_a, mine_a, to_zm)
    b1 = w.push(mine_b, mine_b, to_yp)
    b2 = w.push(mine_b, mine_b, to_ym)
    yield
    a1.wait_recv()
    part = out.at[y, zm, pl.ds(0, 32)]
    a3 = w.push(part, part, to_zp)
    b1.wait_recv()
    part = out.at[ym, z, pl.ds(64, 32)]
    b3 = w.push(part, part, to_yp)
    a2.wait_recv()
    part = out.at[y, zp, pl.ds(32, 32)]
    a4 = w.push(part, part, to_zm)
    b2.wait_recv()
    part = out.at[yp, z, pl.ds(96, 32)]
    b4 = w.push(part, part, to_ym)
    yield
    a3.wait_recv()
    a4.wait_recv()
    part = out.at[y, :, a]
    a5 = w.push(part, part, to_yp)
    a6 = w.push(part, part, to_ym)
    b3.wait_recv()
    b4.wait_recv()
    part = out.at[:, z, b]
    b5 = w.push(part, part, to_zp)
    b6 = w.push(part, part, to_zm)
    yield
    a5.wait_recv()
    part = out.at[ym, pl.ds(0, 2), a]
    a7 = w.push(part, part, to_yp)
    b5.wait_recv()
    part = out.at[pl.ds(0, 2), zm, b]
    b7 = w.push(part, part, to_zp)
    a6.wait_recv()
    part = out.at[yp, pl.ds(2, 2), a]
    a8 = w.push(part, part, to_ym)
    b6.wait_recv()
    part = out.at[pl.ds(2, 2), zp, b]
    b8 = w.push(part, part, to_zm)
    yield
    for copy in (a7, b7, a8, b8):
        copy.wait_recv()


def plane_sum_scratch(columns, resident):
    kept = [
        pltpu.VMEM((2, 2, 64, columns), BF),
        pltpu.VMEM((2, 2, 64, columns), BF),
        pltpu.VMEM((2, 4, 64, columns), BF),
    ]
    return ([] if resident else kept) + [
        pltpu.VMEM((2, 2, 2, 64, columns), BF),
        pltpu.VMEM((2, 2, 4, 64, columns), BF),
        pltpu.VMEM((2, 2, 32, columns), BF),
        pltpu.VMEM((2, 2, 64, columns), BF),
        pltpu.VMEM((128, columns), BF),
        pltpu.VMEM((2, 64, columns), BF),
    ]


def plane_sum(w, spot, part, scratch, resident=False):
    in1, in2, in3, in4, full, both = scratch[-6:]
    c = spot.c
    rows = (pl.ds(0, 64), pl.ds(64, 64))
    lanes = ((spot.y, spot.z), (spot.z, spot.y))
    steps = (("dy", "dz"), ("dz", "dy"))

    def view(h, k, low, size):
        at = (lanes[h][0] + k) % 4
        if h == 0:
            return part.at[at, pl.ds(low, size), rows[h]]
        return part.at[pl.ds(low, size), at, rows[h]]

    def held(h, j):
        if not resident:
            return scratch[2].at[h, j]
        if h == 0:
            return part.at[spot.y, j, rows[h]]
        return part.at[j, spot.z, rows[h]]

    def to(h, stage, step):
        return spot.dev(**{steps[h][stage]: step})

    loads, first, second, early = [], [], [], []
    for h in range(2):
        first.append(
            (
                w.push(view(h, 2, 0, 2), in1.at[h, 0], to(h, 0, 1)),
                w.push(view(h, 2, 2, 2), in1.at[h, 1], to(h, 0, -1)),
            )
        )
    for h in range(2):
        if resident:
            plus, minus = view(h, 1, 0, 2), view(h, 3, 2, 2)
            loads.append((plus, minus))
            continue
        plus, minus = scratch[0].at[h], scratch[1].at[h]
        loads.append(
            (
                plus,
                minus,
                w.local(view(h, 1, 0, 2), plus),
                w.local(view(h, 3, 2, 2), minus),
                w.local(view(h, 0, 0, 4), scratch[2].at[h]),
            )
        )
    yield
    for h in range(2):
        plus, minus = loads[h][:2]
        if not resident:
            loads[h][2].wait()
        first[h][0].wait_recv()
        for j in range(2):
            add_into(plus.at[j], in1.at[h, 0, j])
        one = w.push(plus, in2.at[h, 0, pl.ds(0, 2)], to(h, 0, 1))
        if not resident:
            loads[h][3].wait()
        first[h][1].wait_recv()
        for j in range(2):
            add_into(minus.at[j], in1.at[h, 1, j])
        two = w.push(minus, in2.at[h, 1, pl.ds(2, 2)], to(h, 0, -1))
        second.append((one, two))
    for h in range(2):
        early.append(
            (
                w.push(view(h, 1, 2, 2), in2.at[h, 0, pl.ds(2, 2)], to(h, 0, 1)),
                w.push(view(h, 3, 0, 2), in2.at[h, 1, pl.ds(0, 2)], to(h, 0, -1)),
            )
        )
    yield
    third, early3 = [], []
    for h in range(2):
        if not resident:
            loads[h][4].wait()
        for copy in early[h] + second[h]:
            copy.wait_recv()
        at = [(lanes[h][1] + k) % 4 for k in range(4)]
        add_into(held(h, at[2]), in2.at[h, 0, at[2]], in2.at[h, 1, at[2]])
        far = held(h, at[2])
        third.append(
            (
                w.push(far.at[pl.ds(0, 32)], in3.at[h, 0], to(h, 1, 1)),
                w.push(far.at[pl.ds(32, 32)], in3.at[h, 1], to(h, 1, -1)),
            )
        )
        add_into(held(h, at[1]), in2.at[h, 0, at[1]], in2.at[h, 1, at[1]])
        one = w.push(held(h, at[1]).at[pl.ds(32, 32)], in4.at[h, 0, pl.ds(32, 32)], to(h, 1, 1))
        add_into(held(h, at[3]), in2.at[h, 0, at[3]], in2.at[h, 1, at[3]])
        two = w.push(held(h, at[3]).at[pl.ds(0, 32)], in4.at[h, 1, pl.ds(0, 32)], to(h, 1, -1))
        early3.append((one, two))
        add_into(held(h, at[0]), in2.at[h, 0, at[0]], in2.at[h, 1, at[0]])
    yield
    fourth = []
    for h in range(2):
        at = [(lanes[h][1] + k) % 4 for k in range(4)]
        third[h][0].wait_recv()
        piece = held(h, at[1]).at[pl.ds(0, 32)]
        add_into(piece, in3.at[h, 0])
        one = w.push(piece, in4.at[h, 0, pl.ds(0, 32)], to(h, 1, 1))
        third[h][1].wait_recv()
        piece = held(h, at[3]).at[pl.ds(32, 32)]
        add_into(piece, in3.at[h, 1])
        two = w.push(piece, in4.at[h, 1, pl.ds(32, 32)], to(h, 1, -1))
        fourth.append((one, two))
    yield
    for h in range(2):
        for copy in early3[h] + fourth[h]:
            copy.wait_recv()
        mine = held(h, lanes[h][1])
        target = full.at[rows[h]]

        def body(r):
            total = mine[r, :].astype(F32) + in4[h, 0, r, :].astype(F32)
            target[r, :] = (total + in4[h, 1, r, :].astype(F32)).astype(BF)

        by_rows(64, 16, body)
    theirs = full.at[pl.ds(pl.multiple_of((1 - c) * 64, 64), 64)]
    mine = full.at[pl.ds(pl.multiple_of(c * 64, 64), 64)]
    swap = w.push(theirs, both.at[c], spot.dev(other=True))

    def keep(r):
        both[c, r, :] = mine[r, :]

    by_rows(64, 16, keep)
    yield
    swap.wait_recv()


def mate_share(w, spot, both, outs):
    copies = []
    for out, low, size in outs:
        for core in range(2):
            piece = both.at[core, :, pl.ds(low, size)]
            at = pl.ds(pl.multiple_of((spot.lo * 2 + core) * size, size), size)
            copies.append((w.local(piece, out.at[:, at]), w.push(piece, out.at[:, at], spot.dp_mate())))
    yield
    for near, far in copies:
        near.wait()
        far.wait_recv()


def column_sum_scratch():
    return [
        pltpu.VMEM((4, 128, WIDTH), BF),
        pltpu.VMEM((4, 128, WIDTH), BF),
        pltpu.VMEM((2, 64, WIDTH), BF),
        pltpu.VMEM((2, 128, WIDTH), BF),
    ]


def column_sum(w, spot, part, scratch, finish, resident=False):
    own, got, in1, in2 = scratch
    x, c = spot.x, spot.c
    right, left = spot.dev(dx=1), spot.dev(dx=-1)
    places = [((x + k) % 4 % 2, (x + k) % 4 // 2) for k in range(4)]
    swaps, loads = {}, {}
    for k in (2, 1, 3, 0):
        swaps[k] = w.push(part.at[1 - c, places[k][0], places[k][1]], got.at[k], spot.dev(other=True))
    if resident:
        own = [part.at[c, lo, hi] for lo, hi in places]
    else:
        for k in (2, 1, 3, 0):
            loads[k] = w.local(part.at[c, places[k][0], places[k][1]], own.at[k])
        own = [own.at[k] for k in range(4)]
    yield

    def merge(k):
        if not resident:
            loads[k].wait()
        swaps[k].wait_recv()
        add_into(own[k], got.at[k])

    low, high = pl.ds(0, 64), pl.ds(64, 64)
    merge(2)
    far1 = w.push(own[2].at[low], in1.at[0], right)
    far2 = w.push(own[2].at[high], in1.at[1], left)
    merge(1)
    one = w.push(own[1].at[high], in2.at[0, high], right)
    merge(3)
    two = w.push(own[3].at[low], in2.at[1, low], left)
    merge(0)
    yield
    far1.wait_recv()
    add_into(own[1].at[low], in1.at[0])
    three = w.push(own[1].at[low], in2.at[0, low], right)
    far2.wait_recv()
    add_into(own[3].at[high], in1.at[1])
    four = w.push(own[3].at[high], in2.at[1, high], left)
    yield
    for copy in (one, two, three, four):
        copy.wait_recv()

    def total(rows):
        return own[0][rows, :].astype(F32) + in2[0, rows, :].astype(F32) + in2[1, rows, :].astype(F32)

    finish(total)


def column_share(w, spot, mine, out):
    x, c = spot.x, spot.c
    right, left, mate = spot.dev(dx=1), spot.dev(dx=-1), spot.dev(other=True)

    def slot(k):
        at = (x + k + 4) % 4
        return out.at[c, at % 2, at // 2]

    low, high = pl.ds(0, 64), pl.ds(64, 64)
    own = w.local(mine, slot(0))
    a = w.push(mine.at[low], slot(0).at[low], right)
    b = w.push(mine.at[high], slot(0).at[high], left)
    d = w.push(mine, slot(0), mate)
    a2 = w.push(mine.at[high], slot(0).at[high], right)
    b2 = w.push(mine.at[low], slot(0).at[low], left)
    yield
    a.wait_recv()
    e = w.push(slot(-1).at[low], slot(-1).at[low], right)
    last = [w.push(slot(-1).at[low], slot(-1).at[low], mate)]
    b.wait_recv()
    g = w.push(slot(1).at[high], slot(1).at[high], left)
    last.append(w.push(slot(1).at[high], slot(1).at[high], mate))
    yield
    a2.wait_recv()
    last.append(w.push(slot(-1).at[high], slot(-1).at[high], mate))
    b2.wait_recv()
    last.append(w.push(slot(1).at[low], slot(1).at[low], mate))
    e.wait_recv()
    last.append(w.push(slot(2).at[low], slot(2).at[low], mate))
    g.wait_recv()
    last.append(w.push(slot(2).at[high], slot(2).at[high], mate))
    yield
    own.wait()
    for copy in [d] + last:
        copy.wait_recv()


def token_share(w, spot, block, out):
    own_at, far_at = spot.c * 2 + spot.lo, spot.c * 2 + 1 - spot.lo
    right, left, mate = spot.dev(dx=1), spot.dev(dx=-1), spot.dev(other=True)
    low, high = pl.ds(0, 128), pl.ds(128, 128)
    own = w.local(block, out.at[own_at])
    a = w.push(block.at[low], out.at[own_at, low], right)
    b = w.push(block.at[high], out.at[own_at, high], left)
    d = w.push(block, out.at[own_at], mate)
    yield
    a.wait_recv()
    part = out.at[far_at, low]
    e = w.push(part, part, mate)
    b.wait_recv()
    part = out.at[far_at, high]
    f = w.push(part, part, mate)
    yield
    own.wait()
    for copy in (d, e, f):
        copy.wait_recv()


def pair_share(w, spot, mine, out):
    own = w.local(mine, out.at[spot.hi])
    a = w.push(mine, out.at[spot.hi], spot.dev(dx=2))
    yield
    own.wait()
    a.wait_recv()


def neighbours(spot, x=False, yz=False, core=False, pair=False, far=False):
    found = []
    if x:
        found += [spot.dev(dx=1), spot.dev(dx=-1)]
    if yz:
        found += [spot.dev(dy=1), spot.dev(dy=-1), spot.dev(dz=1), spot.dev(dz=-1)]
    if core:
        found += [spot.dev(other=True)]
    if pair:
        found += [spot.dev(dx=2)]
    if far:
        found += [spot.dev(dy=2), spot.dev(dz=2)]
    return found


BLOCK = 256
SPAN = COLUMN + BLOCK
NT = (((1,), (1,)), ((), ()))
TN = (((0,), (0,)), ((), ()))
NN = (((1,), (0,)), ((), ()))


def dot(a, b, dims):
    return lax.dot_general(a, b, dims, preferred_element_type=F32)


def rms_of(rows):
    inverse = lax.rsqrt(jnp.mean(rows * rows, axis=-1, keepdims=True) + EPS)
    return rows * inverse, inverse


def turn_half(rows):
    half = HEAD // 2
    return jnp.concatenate([-rows[:, half:], rows[:, :half]], axis=-1)


def params(collective_id):
    return pltpu.CompilerParams(
        collective_id=collective_id, has_side_effects=True, vmem_limit_bytes=LIMIT
    )


def own_block(ref, spot):
    return ref.at[spot.c, spot.lo, spot.hi]


def place_rows(spot, lengths, freq, doc_row, doc_col, cosine, sine):
    first = (spot.y * 4 + spot.z - 1) * COLUMN
    rows = lax.broadcasted_iota(jnp.int32, (16, 128), 0) * 128 + first
    rows = rows + lax.broadcasted_iota(jnp.int32, (16, 128), 1)
    document = jnp.zeros((16, 128), jnp.int32)
    start = jnp.zeros((16, 128), jnp.int32)
    bound = jnp.int32(0)
    for d in range(lengths.shape[1]):
        bound = bound + lengths[0, d]
        passed = rows >= bound
        document = document + passed.astype(jnp.int32)
        start = jnp.where(passed, bound, start)
    document = jnp.where(rows >= 0, document, -1).astype(F32)
    place = (rows - start).astype(F32)
    for g in range(16):
        line = document[g : g + 1, :]
        at = slice(g * 128, (g + 1) * 128)
        doc_row[:, at] = line
        doc_col[at, :] = jnp.transpose(jnp.broadcast_to(line, (128, 128)))
        if g >= 8:
            down = jnp.transpose(jnp.broadcast_to(place[g : g + 1, :], (128, 128)))
            angles = down * freq[...]
            at = slice((g - 8) * 128, (g - 7) * 128)
            cosine[at, :] = jnp.cos(angles)
            sine[at, :] = jnp.sin(angles)


def turned_head(raw, scale, cosine, sine):
    unit = rms_of(raw)[0] * scale
    return (unit * cosine + turn_half(unit) * sine).astype(BF)


def forward_kernel(
    tok, cot, x_q, x_k, x_v, x_o, x_gains, x_gate, x_up, x_down, lengths, freq, q_gain, k_gain,
    normed1, o_a, o_w, w_b, cot_all, o_raw, o_query, o_kv, o_before, o_attended, o_inverse, mid, normed2, o_cosine, o_sine, gains, doc_row, o_docs,
    w_a, w_w, raw, query, kv, before, attended, inverse, cosine, sine, doc_col,
    tok_all, low1, roots, top, total, branch, got, in1, in2, low, send, recv, here,
):
    spot = Spot()
    greet(neighbours(spot, x=True, yz=True, core=True) + [spot.column(1), spot.column(-1)])
    w = Wires(send, recv, here)
    first_pieces = ((x_q, 256, 0), (x_k, 128, 256), (x_v, 128, 384), (x_gains, 128, 512))
    take_a = plane_gather(w, spot, first_pieces, w_a)
    take_w = plane_gather(w, spot, ((x_o, 256, 0),), w_w)
    take_b = plane_gather(w, spot, ((x_gate, 768, 0), (x_up, 768, 768), (x_down, 768, 1536)), w_b)
    take_tok = token_share(w, spot, tok, tok_all)
    take_cot = token_share(w, spot, cot, cot_all)
    keeps = []

    def keep(source, target):
        keeps.append(w.local(source, target))

    def go(*parts):
        for part in parts:
            next(part, None)

    go(take_a, take_tok, take_a, take_w, take_b)
    place_rows(spot, lengths, freq, doc_row, doc_col, cosine, sine)
    keep(cosine, o_cosine)
    keep(sine, o_sine)
    keep(doc_col, o_docs)
    go(take_a, take_a, take_w, take_tok, take_a, take_tok, take_w)

    def roots_of(i, _):
        rows = pl.ds(pl.multiple_of(i * 32, 32), 32)
        values = tok_all[i // 8, pl.ds(pl.multiple_of(i % 8 * 32, 32), 32), :].astype(F32)
        roots[rows, :] = lax.rsqrt(jnp.mean(values * values, axis=-1, keepdims=True) + EPS)
        return 0

    lax.fori_loop(0, 32, roots_of, 0)
    go(take_a, take_cot, take_b, take_w)
    keep(w_a, o_a)
    for i in range(16):
        block = jnp.transpose(w_a[i // 4, i % 4, :, 512:640].astype(F32))
        gains[:, i * 128 : (i + 1) * 128] = block[0:2, :]

    def norm_rows(i, _):
        rows = pl.ds(pl.multiple_of(i * 32, 32), 32)
        values = tok_all[i // 8, pl.ds(pl.multiple_of(i % 8 * 32, 32), 32), :].astype(F32)
        low1[rows, :] = (values * roots[rows, :] * gains[0:1, :]).astype(BF)
        return 0

    lax.fori_loop(0, 32, norm_rows, 0)
    keep(low1, normed1)

    def project_kv(i, _):
        rows = pl.ds(pl.multiple_of(i * BLOCK, BLOCK), BLOCK)
        out = dot(low1[rows, :], w_a[:, :, :, 256:512].reshape(WIDTH, 256), NN)
        raw[rows, 256:512] = out
        kv[rows, :HEAD] = turned_head(out[:, :HEAD], k_gain[...].astype(F32), cosine[rows, :], sine[rows, :])
        kv[rows, HEAD:] = out[:, HEAD:].astype(BF)
        return 0

    def project_q(i, _):
        rows = pl.ds(pl.multiple_of(i * BLOCK, BLOCK), BLOCK)
        out = dot(low1[rows, :], w_a[:, :, :, 0:256].reshape(WIDTH, 256), NN)
        raw[rows, 0:256] = out
        for h in range(2):
            span = slice(h * HEAD, (h + 1) * HEAD)
            query[rows, span] = turned_head(out[:, span], q_gain[...].astype(F32), cosine[rows, :], sine[rows, :])
        return 0

    pass_kv = []
    for i in range(4):
        project_kv(i, 0)
        rows = pl.ds(i * BLOCK, BLOCK)
        pass_kv.append(w.push(kv.at[rows], before.at[rows], spot.column(1)))
    keep(kv, o_kv)
    go(take_w, take_b)
    lax.fori_loop(0, 4, project_q, 0)
    keep(raw, o_raw)
    keep(query, o_query)
    go(take_cot)

    def weights_of(i, h, keys, docs, causal):
        rows = slice(i * BLOCK, (i + 1) * BLOCK)
        scores = dot(query[rows, h * HEAD : (h + 1) * HEAD], keys, NT) * SCALE
        valid = doc_col[COLUMN + i * BLOCK : COLUMN + (i + 1) * BLOCK, 0:1] == docs
        if causal:
            row = lax.broadcasted_iota(jnp.int32, scores.shape, 0) + i * BLOCK
            valid = valid & (lax.broadcasted_iota(jnp.int32, scores.shape, 1) <= row)
        return jnp.where(valid, jnp.exp(scores), 0.0)

    for i in range(4):
        rows, end = slice(i * BLOCK, (i + 1) * BLOCK), (i + 1) * BLOCK
        for h in range(2):
            weight = weights_of(i, h, kv[0:end, :HEAD], doc_row[:, COLUMN : COLUMN + end], True)
            total[rows, h : h + 1] = jnp.sum(weight, axis=-1, keepdims=True)
            top[rows, h * HEAD : (h + 1) * HEAD] = dot(weight.astype(BF), kv[0:end, HEAD:], NN)
    for copy in pass_kv:
        copy.wait_recv()
    keep(before, o_before)
    go(take_w, take_b)
    keep(w_w, o_w)
    for i in range(4):
        rows, low_key = slice(i * BLOCK, (i + 1) * BLOCK), i * BLOCK
        for h in range(2):
            span = slice(h * HEAD, (h + 1) * HEAD)
            weight = weights_of(i, h, before[low_key:, :HEAD], doc_row[:, low_key:COLUMN], False)
            back = 1.0 / (total[rows, h : h + 1] + jnp.sum(weight, axis=-1, keepdims=True))
            inverse[rows, h : h + 1] = back
            attended[rows, span] = ((top[rows, span] + dot(weight.astype(BF), before[low_key:, HEAD:], NN)) * back).astype(BF)
    keep(attended, o_attended)
    keep(inverse, o_inverse)

    def branch_of(core):
        def one(lo, _):
            rows = pl.ds(pl.multiple_of((core * 2 + lo) * BLOCK, BLOCK), BLOCK)
            out = dot(attended[rows, :], w_w[...].reshape(WIDTH, 256), NT)
            branch[core, lo] = out.astype(BF).reshape(2, 128, WIDTH)
            return 0

        lax.fori_loop(0, 2, one, 0)

    def finish(add):
        def body(rows):
            base = tok[pl.ds(pl.multiple_of(spot.hi * 128 + rows.start, 16), 16), :].astype(F32)
            middle = base + add(rows)
            mid[rows, :] = middle
            root = lax.rsqrt(jnp.mean(middle * middle, axis=-1, keepdims=True) + EPS)
            low[rows, :] = (middle * root * gains[1:2, :]).astype(BF)

        by_rows(128, 16, body)

    branch_of(1 - spot.c)
    fold = column_sum(w, spot, branch, (None, got, in1, in2), finish, resident=True)
    go(fold)
    branch_of(spot.c)
    go(fold, fold, fold, take_cot)
    share = column_share(w, spot, low, normed2)
    go(share, take_b, share, share, take_b, share)
    assert all(g.gi_frame is None for g in (take_a, take_w, take_b, take_tok, take_cot, fold, share))
    for copy in keeps:
        copy.wait()
    w.drain()


def forward_call(*args):
    def shape(*sizes, kind=BF):
        return jax.ShapeDtypeStruct(sizes, kind)

    kept = (
        shape(4, 4, 128, 640),
        shape(4, 4, 128, 256),
        shape(COLUMN, 512, kind=F32),
        shape(COLUMN, 256),
        shape(COLUMN, 256),
        shape(COLUMN, 256),
        shape(COLUMN, 256),
        shape(COLUMN, 2, kind=F32),
        shape(COLUMN, HEAD, kind=F32),
        shape(COLUMN, HEAD, kind=F32),
        shape(2 * COLUMN, 128, kind=F32),
    )
    outs = (
        (shape(COLUMN, WIDTH), HBM),
        (kept[0], HBM),
        (kept[1], HBM),
        (shape(4, 4, 128, 2304), HBM),
        (shape(4, 256, WIDTH), HBM),
        *((k, HBM) for k in kept[2:8]),
        (shape(128, WIDTH, kind=F32), VMEM),
        (shape(2, 2, 2, 128, WIDTH), HBM),
        (kept[8], HBM),
        (kept[9], HBM),
        (shape(2, WIDTH, kind=F32), VMEM),
        (shape(1, 2 * COLUMN, kind=F32), VMEM),
        (kept[10], HBM),
    )
    return pl.pallas_call(
        forward_kernel,
        out_shape=tuple(o[0] for o in outs),
        in_specs=[VMEM] * 10 + [pl.BlockSpec(memory_space=pltpu.SMEM)] + [VMEM] * 3,
        out_specs=tuple(o[1] for o in outs),
        scratch_shapes=[pltpu.VMEM(o.shape, o.dtype) for o in kept]
        + [
            pltpu.VMEM((4, 256, WIDTH), BF),
            pltpu.VMEM((COLUMN, WIDTH), BF),
            pltpu.VMEM((COLUMN, 1), F32),
            pltpu.VMEM((COLUMN, 256), F32),
            pltpu.VMEM((COLUMN, 2), F32),
            pltpu.VMEM((2, 2, 2, 128, WIDTH), BF),
        ]
        + column_sum_scratch()[1:]
        + [pltpu.VMEM((128, WIDTH), BF)]
        + wires_scratch(104, 36),
        compiler_params=params(1),
        name="forward",
    )(*args)


def rms_back(total, base, gain, rows, extra, out, gain_grad):
    values = base[rows, :].astype(F32)
    inverse = lax.rsqrt(jnp.mean(values * values, axis=-1, keepdims=True) + EPS)
    normed = values * inverse
    grad = total(rows)
    scaled = grad * gain[...]
    back = inverse * (scaled - normed * jnp.mean(scaled * normed, axis=-1, keepdims=True))
    gain_grad[...] += jnp.sum(grad * normed, axis=0, keepdims=True)
    out[rows, :] = (extra[rows, :].astype(F32) + back).astype(out.dtype)


def turn_kernel(
    normed, cot, w_b, mid, cot_own, gain, dmid, d_branch, mixed, g_in, gain_grad, both_out,
    nv, cv, wv, hidden, d_both, part, g_down, g_part, mixed_part, both_n, both_c, both_d, got, in1, in2, low, top,
    p0, p1, p2, p3, p4, p5, send, recv, here, tiles,
):
    spot = Spot()
    w = Wires(send, recv, here)
    first = w.local(w_b, wv)

    def block(i):
        rows = pl.ds(pl.multiple_of(i * BLOCK, BLOCK), BLOCK)
        one = pltpu.make_async_copy(normed.at[rows], nv.at[rows], tiles.at[0, i])
        return one, pltpu.make_async_copy(cot.at[rows], cv.at[rows], tiles.at[1, i])

    for i in range(4):
        for copy in block(i):
            copy.start()
    load = w.local(cot_own.at[spot.hi], top)
    greet(neighbours(spot, x=True, yz=True, core=True))
    gain_grad[...] = jnp.zeros_like(gain_grad)
    first.wait()

    def weight(low_column, size):
        return wv[:, :, :, low_column : low_column + size].reshape(WIDTH, size)

    for i in range(4):
        for copy in block(i):
            copy.wait()

    def two(k):
        at = (spot.x + k) % 4
        lo, hi = at % 2, at // 2
        theirs = pl.ds(pl.multiple_of(((1 - spot.c) * 2 + lo) * 256 + hi * 128, 128), 128)
        mine = pl.ds(pl.multiple_of((spot.c * 2 + lo) * 256 + hi * 128, 128), 128)
        return lo, hi, theirs, mine

    def units(k):
        _, _, theirs, mine = two(k)
        both_n[0:128, :] = nv[theirs, :]
        both_n[128:, :] = nv[mine, :]
        both_c[0:128, :] = cv[theirs, :]
        both_c[128:, :] = cv[mine, :]

        def one(j, _):
            a = pl.ds(pl.multiple_of(j * 256, 256), 256)
            b = pl.ds(pl.multiple_of(j * 256 + 768, 256), 256)
            d = pl.ds(pl.multiple_of(j * 256 + 1536, 256), 256)
            gate = dot(both_n[...], wv[:, :, :, a].reshape(WIDTH, 256), NN)
            up = dot(both_n[...], wv[:, :, :, b].reshape(WIDTH, 256), NN)
            d_hidden = dot(both_c[...], wv[:, :, :, d].reshape(WIDTH, 256), NN)
            sigma = lax.logistic(gate)
            active = gate * sigma
            unit = (active * up).astype(BF)
            d_gate = (d_hidden * up * sigma * (1.0 + gate * (1.0 - sigma))).astype(BF)
            d_up = (d_hidden * active).astype(BF)
            for half, rows in ((slice(0, 128), theirs), (slice(128, 256), mine)):
                hidden[rows, a] = unit[half, :]
                d_both[rows, a] = d_gate[half, :]
                d_both[rows, b] = d_up[half, :]
            return 0

        lax.fori_loop(0, 3, one, 0)

    def back(k):
        lo, hi, theirs, mine = two(k)
        both_d[0:128, :] = d_both[theirs, :]
        both_d[128:, :] = d_both[mine, :]
        out = dot(both_d[...], weight(0, 1536), NT).astype(BF)
        part[1 - spot.c, lo, hi] = out[:128]
        part[spot.c, lo, hi] = out[128:]
        swaps[k] = w.push(part.at[1 - spot.c, lo, hi], got.at[k], spot.dev(other=True))

    swaps = {}

    def own(k):
        lo, hi, _, _ = two(k)
        return part.at[spot.c, lo, hi]

    def merge(k):
        swaps[k].wait_recv()
        add_into(own(k), got.at[k])

    def finish(total):
        load.wait()

        def body(rows):
            rms_back(total, mid, gain.at[1:2], rows, top, dmid, gain_grad)
            low[rows, :] = dmid[rows, :].astype(BF)

        by_rows(128, 16, body)

    def go(*parts):
        for one in parts:
            next(one, None)

    def down_tile(t, _):
        lanes = pl.ds(pl.multiple_of(t * BLOCK, BLOCK), BLOCK)
        out = dot(cv[:, lanes], hidden[...], TN)
        g_down[t // 2, pl.ds(t % 2 * 2, 2)] = out.astype(BF).reshape(2, 128, 768)
        return 0

    def in_copy(t):
        at = (t // 2, pl.ds(t % 2 * 2, 2))
        return pltpu.make_async_copy(g_part.at[at], g_in.at[at], tiles.at[2, t])

    def in_tile(t, _):
        lanes = pl.ds(pl.multiple_of(t * BLOCK, BLOCK), BLOCK)
        out = dot(nv[:, lanes], d_both[...], TN)
        g_part[t // 2, pl.ds(t % 2 * 2, 2)] = out.astype(BF).reshape(2, 128, 1536)
        in_copy(t).start()
        return 0

    def mixed_block(i, _):
        rows = pl.ds(pl.multiple_of(i * BLOCK, BLOCK), BLOCK)
        out = dot(hidden[rows, :], weight(1536, 768), NT)
        mixed_part[i // 2, i % 2] = out.astype(BF).reshape(2, 128, WIDTH)
        return 0

    right, left = spot.dev(dx=1), spot.dev(dx=-1)
    lows, highs = pl.ds(0, 64), pl.ds(64, 64)
    units(2)
    back(2)
    units(1)
    merge(2)
    far1 = w.push(own(2).at[lows], in1.at[0], right)
    far2 = w.push(own(2).at[highs], in1.at[1], left)
    back(1)
    units(3)
    merge(1)
    one = w.push(own(1).at[highs], in2.at[0, highs], right)
    back(3)
    units(0)
    merge(3)
    two_ = w.push(own(3).at[lows], in2.at[1, lows], left)
    far1.wait_recv()
    add_into(own(1).at[lows], in1.at[0])
    three = w.push(own(1).at[lows], in2.at[0, lows], right)
    far2.wait_recv()
    add_into(own(3).at[highs], in1.at[1])
    four = w.push(own(3).at[highs], in2.at[1, highs], left)
    back(0)
    lax.fori_loop(0, 8, down_tile, 0)
    down = plane_sum(w, spot, g_down, (p0, p1, p2, p3, p4, p5), resident=True)
    go(down)
    lax.fori_loop(0, 4, in_tile, 0)
    go(down)
    merge(0)
    for copy in (one, two_, three, four):
        copy.wait_recv()
    mine_ref = own(0)

    def total(rows):
        return mine_ref[rows, :].astype(F32) + in2[0, rows, :].astype(F32) + in2[1, rows, :].astype(F32)

    finish(total)
    share = column_share(w, spot, low, d_branch)
    go(share)
    lax.fori_loop(0, 4, mixed_block, 0)
    keep = w.local(mixed_part, mixed)
    go(share, down)
    lax.fori_loop(4, 8, in_tile, 0)
    go(share, down, share, down, down)
    assert share.gi_frame is None and down.gi_frame is None
    last = w.local(p5, both_out)
    for t in range(8):
        in_copy(t).wait()
    keep.wait()
    last.wait()
    w.drain()


def turn_call(normed, cot, w_b, mid, cot_own, gain):
    blocks = jax.ShapeDtypeStruct((2, 2, 2, 128, WIDTH), BF)
    return pl.pallas_call(
        turn_kernel,
        out_shape=(
            jax.ShapeDtypeStruct((128, WIDTH), F32),
            blocks,
            blocks,
            jax.ShapeDtypeStruct((4, 4, 128, 1536), BF),
            jax.ShapeDtypeStruct((1, WIDTH), F32),
            jax.ShapeDtypeStruct((2, 64, 768), BF),
        ),
        in_specs=[HBM, HBM, HBM, VMEM, HBM, VMEM],
        out_specs=(VMEM, HBM, HBM, HBM, VMEM, HBM),
        scratch_shapes=[
            pltpu.VMEM((COLUMN, WIDTH), BF),
            pltpu.VMEM((COLUMN, WIDTH), BF),
            pltpu.VMEM((4, 4, 128, 2304), BF),
            pltpu.VMEM((COLUMN, 768), BF),
            pltpu.VMEM((COLUMN, 1536), BF),
            pltpu.VMEM((2, 2, 2, 128, WIDTH), BF),
            pltpu.VMEM((4, 4, 128, 768), BF),
            pltpu.VMEM((4, 4, 128, 1536), BF),
            pltpu.VMEM((2, 2, 2, 128, WIDTH), BF),
            pltpu.VMEM((BLOCK, WIDTH), BF),
            pltpu.VMEM((BLOCK, WIDTH), BF),
            pltpu.VMEM((BLOCK, 1536), BF),
        ]
        + column_sum_scratch()[1:]
        + [pltpu.VMEM((128, WIDTH), BF)] * 2
        + plane_sum_scratch(768, True)
        + wires_scratch(64, 12)
        + [pltpu.SemaphoreType.DMA((3, 8))],
        compiler_params=params(4),
        name="turn",
    )(normed, cot, w_b, mid, cot_own, gain)


def sum_everywhere(w, spot, vector, pair, lines):
    a = w.push(vector, pair, spot.dev(other=True))
    yield
    a.wait_recv()
    w.sent_now(a)
    vector[...] = vector[...] + pair[...]
    yield
    for stage, (axis, at) in enumerate((("dx", spot.x), ("dy", spot.y), ("dz", spot.z))):
        slots = lines.at[stage]
        slots[at] = vector[...]
        copies = [w.push(vector, slots.at[at], spot.dev(**{axis: k})) for k in (1, 2, 3)]
        yield
        for copy in copies:
            copy.wait_recv()
            w.sent_now(copy)
        vector[...] = slots[0] + slots[1] + slots[2] + slots[3]
        yield


def as_row(column):
    return jnp.transpose(jnp.broadcast_to(column, (column.shape[0], HEAD)))[0:1, :]


def close_kernel(
    d_branch, h_w, h_a, h_attended, h_query, h_before, h_kv, h_raw, h_cosine, h_sine, doc_row, h_docs, h_inverse, q_gain, k_gain,
    g_in, both_down, mixed, mid, dmid, tok, gain, normed1, g_mlp,
    out, g_tok, o_gate, o_up, o_down, o_q, o_k, o_v, o_out, vector,
    w_w, w_a, attended, query, before, kv, raw, cosine, sine, doc_col, inverse,
    db, do, dq, dkv, d_before, came, d_raw, part, g_out, got, in1, in2,
    m_own, m_got, m_in1, m_in2, result, base, gain_grad, low, delta, back,
    a0, a1, a2, a3, a4, a5, a6, a7, a8, b0, b1, b2, b3, b4, b5, pair, lines, send, recv, here, tiles,
):
    spot = Spot()
    w = Wires(send, recv, here)

    def block(i):
        rows = pl.ds(pl.multiple_of(i * BLOCK, BLOCK), BLOCK)
        return pltpu.make_async_copy(d_branch.at[rows], db.at[rows], tiles.at[i])

    for i in range(4):
        block(i).start()
    fetched_w = w.local(h_w, w_w)
    fetched = [
        w.local(source, target)
        for source, target in (
            (h_attended, attended), (h_query, query), (h_before, before), (h_inverse, inverse), (h_docs, doc_col),
            (h_kv, kv), (h_raw, raw), (h_cosine, cosine), (h_sine, sine), (h_a, w_a),
        )
    ]
    load_tok = w.local(tok.at[spot.hi], base)
    greet(
        neighbours(spot, x=True, yz=True, core=True, pair=True, far=True)
        + [spot.column(1), spot.column(-1)]
    )

    def go(*parts):
        for one in parts:
            next(one, None)

    sum_in = plane_sum(w, spot, g_in, (a0, a1, a2, a3, a4, a5, a6, a7, a8))
    go(sum_in)

    def finish_out(total):
        def body(rows):
            result[rows, :] = (mid[rows, :] + total(rows)).astype(BF)

        by_rows(128, 16, body)

    fold_out = column_sum(w, spot, mixed, (m_own, m_got, m_in1, m_in2), finish_out)
    share_out = pair_share(w, spot, result, out)
    share_down = mate_share(w, spot, both_down, ((o_down, 0, 768),))
    go(fold_out, share_down)
    gain_grad[...] = jnp.zeros_like(gain_grad)
    vector[...] = jnp.zeros_like(vector)
    dkv[...] = jnp.zeros_like(dkv)
    dq[...] = jnp.zeros_like(dq)

    fetched_w.wait()

    def upstream_of(i, _):
        block(i).wait()
        rows = pl.ds(pl.multiple_of(i * BLOCK, BLOCK), BLOCK)
        do[rows, :] = dot(db[rows, :], w_w[...], NN).astype(BF)
        return 0

    lax.fori_loop(0, 4, upstream_of, 0)
    go(fold_out)
    for copy in fetched:
        copy.wait()

    def tile_out(t, _):
        lanes = pl.ds(pl.multiple_of(t * BLOCK, BLOCK), BLOCK)
        at = (t // 2, pl.ds(t % 2 * 2, 2), slice(None), slice(512, 768))
        g_out[at] = dot(db[:, lanes], attended[...], TN).astype(BF).reshape(2, 128, 256)
        return 0

    def tile(t, _):
        lanes = pl.ds(pl.multiple_of(t * BLOCK, BLOCK), BLOCK)
        at = (t // 2, pl.ds(t % 2 * 2, 2), slice(None), slice(0, 512))
        g_out[at] = dot(db[:, lanes], d_raw[...], TN).astype(BF).reshape(2, 128, 512)
        return 0


    for i in range(4):
        rows = slice(i * BLOCK, (i + 1) * BLOCK)
        product = attended[rows, :].astype(F32) * do[rows, :].astype(F32)
        for h in range(2):
            delta[h : h + 1, rows] = as_row(jnp.sum(product[:, h * HEAD : (h + 1) * HEAD], axis=-1, keepdims=True))
            back[h : h + 1, rows] = as_row(inverse[rows, h : h + 1])

    def attend_back(rows, keys_of, docs, causal, grads):
        valid = docs == doc_row[:, COLUMN + rows.start : COLUMN + rows.stop]
        if causal:
            row = lax.broadcasted_iota(jnp.int32, valid.shape, 0)
            valid = valid & (row <= lax.broadcasted_iota(jnp.int32, valid.shape, 1) + rows.start)
        for h in range(2):
            span = slice(h * HEAD, (h + 1) * HEAD)
            asked, upstream = query[rows, span], do[rows, span]
            scores = dot(keys_of[:, :HEAD], asked, NT) * SCALE
            probs = jnp.where(valid, jnp.exp(scores), 0.0) * back[h : h + 1, rows]
            d_probs = dot(keys_of[:, HEAD:], upstream, NT)
            d_scores = (probs * (d_probs - delta[h : h + 1, rows])).astype(BF)
            grads[:, :HEAD] += dot(d_scores, asked, NN) * SCALE
            grads[:, HEAD:] += dot(probs.astype(BF), upstream, NN)
            d_asked = dot(d_scores, keys_of[:, :HEAD], TN) * SCALE
            dq[rows, span] += d_asked

    back_kv = []
    for j in range(4):
        end, keys = (j + 1) * BLOCK, slice(j * BLOCK, (j + 1) * BLOCK)
        attend_back(slice(0, end), before.at[keys], doc_col[keys, 0:1], False, dkv.at[keys])
        d_before[keys, :] = dkv[keys, :].astype(BF)
        back_kv.append(w.push(d_before.at[keys], came.at[keys], spot.column(-1)))
    go(fold_out)
    lax.fori_loop(0, 8, tile_out, 0)
    load_n1 = w.local(normed1, db)
    for i in range(4):
        end = (i + 1) * BLOCK
        attend_back(
            slice(i * BLOCK, end), kv.at[0:end], doc_col[COLUMN : COLUMN + end, 0:1], True, dkv.at[COLUMN : COLUMN + end]
        )
        if i == 1:
            go(fold_out, share_out)
    for copy in back_kv:
        copy.wait_recv()
    go(sum_in)

    def project_back(i, _):
        rows = pl.ds(pl.multiple_of(i * BLOCK, BLOCK), BLOCK)
        own = pl.ds(pl.multiple_of(i * BLOCK + COLUMN, BLOCK), BLOCK)
        for h, scale in enumerate((q_gain, q_gain, k_gain)):
            span = slice(h * HEAD, (h + 1) * HEAD)
            if h < 2:
                grad = dq[rows, span]
            else:
                grad = dkv[own, :HEAD] + came[rows, :HEAD].astype(F32)
            grad = grad * cosine[rows, :] - turn_half(grad) * sine[rows, :]
            unit, root = rms_of(raw[rows, span])
            scaled = grad * scale[...].astype(F32)
            back = root * (scaled - unit * jnp.mean(scaled * unit, axis=-1, keepdims=True))
            d_raw[rows, span] = back.astype(BF)
            at = 32 + h // 2
            vector[at : at + 1, :] += jnp.sum(grad * unit, axis=0, keepdims=True)
        d_raw[rows, 3 * HEAD :] = (dkv[own, HEAD:] + came[rows, HEAD:].astype(F32)).astype(BF)
        return 0

    def norm_of(core):
        def one(lo, _):
            rows = pl.ds(pl.multiple_of((core * 2 + lo) * BLOCK, BLOCK), BLOCK)
            value = dot(d_raw[rows, :], w_a[:, :512], NT)
            part[core, lo] = value.astype(BF).reshape(2, 128, WIDTH)
            return 0

        lax.fori_loop(0, 2, one, 0)

    def finish(total):
        load_tok.wait()

        def body(rows):
            rms_back(total, base, gain.at[0:1], rows, dmid, low, gain_grad)

        by_rows(128, 16, body)

    lax.fori_loop(0, 4, project_back, 0)
    load_n1.wait()
    sum_out = plane_sum(w, spot, g_out, (b0, b1, b2, b3, b4, b5), resident=True)
    fold = column_sum(w, spot, part, (None, got, in1, in2), finish, resident=True)
    norm_of(1 - spot.c)
    go(fold)
    norm_of(spot.c)
    go(fold)
    lax.fori_loop(0, 8, tile, 0)
    go(sum_out, fold, sum_in, sum_out, fold)
    share_tok = pair_share(w, spot, low, g_tok)
    vector[16:32, :] = g_mlp[...]
    for i in range(16):
        vector[i : i + 1, :] = gain_grad[:, i * 128 : (i + 1) * 128]
    share_in = mate_share(w, spot, a8, ((o_gate, 0, 768), (o_up, 768, 768)))
    everywhere = sum_everywhere(w, spot, vector, pair, lines)
    go(share_tok, sum_in, everywhere, sum_out, everywhere, everywhere, sum_in, sum_out, sum_in, share_in, everywhere, everywhere, sum_out, sum_out)
    share_grads = mate_share(
        w, spot, b5, ((o_q, 0, 256), (o_k, 256, 128), (o_v, 384, 128), (o_out, 512, 256))
    )
    go(share_grads, everywhere, everywhere, share_out, share_down, everywhere, everywhere, share_in, share_tok, share_grads)
    for part_left in (sum_in, fold_out, share_out, share_down, fold, sum_out, everywhere, share_in, share_grads, share_tok):
        assert part_left.gi_frame is None
    w.drain()


def close_call(*args):
    def shape(*sizes, kind=BF):
        return jax.ShapeDtypeStruct(sizes, kind)

    return pl.pallas_call(
        close_kernel,
        out_shape=(
            shape(2, 128, WIDTH),
            shape(2, 128, WIDTH),
            shape(64, 3072),
            shape(64, 3072),
            shape(64, 3072),
            shape(64, 1024),
            shape(64, 512),
            shape(64, 512),
            shape(64, 1024),
            shape(40, 128, kind=F32),
        ),
        in_specs=[HBM] * 10 + [VMEM, HBM, HBM, VMEM, VMEM] + [HBM, VMEM, HBM, VMEM, VMEM, HBM, VMEM, HBM, VMEM],
        out_specs=(HBM,) * 9 + (VMEM,),
        scratch_shapes=[
            pltpu.VMEM((WIDTH, 256), BF),
            pltpu.VMEM((WIDTH, 640), BF),
            pltpu.VMEM((COLUMN, 256), BF),
            pltpu.VMEM((COLUMN, 256), BF),
            pltpu.VMEM((COLUMN, 256), BF),
            pltpu.VMEM((COLUMN, 256), BF),
            pltpu.VMEM((COLUMN, 512), F32),
            pltpu.VMEM((COLUMN, HEAD), F32),
            pltpu.VMEM((COLUMN, HEAD), F32),
            pltpu.VMEM((2 * COLUMN, 128), F32),
            pltpu.VMEM((COLUMN, 2), F32),
            pltpu.VMEM((COLUMN, WIDTH), BF),
            pltpu.VMEM((COLUMN, 256), BF),
            pltpu.VMEM((COLUMN, 256), F32),
            pltpu.VMEM((2 * COLUMN, 256), F32),
            pltpu.VMEM((COLUMN, 256), BF),
            pltpu.VMEM((COLUMN, 256), BF),
            pltpu.VMEM((COLUMN, 512), BF),
            pltpu.VMEM((2, 2, 2, 128, WIDTH), BF),
            pltpu.VMEM((4, 4, 128, 768), BF),
        ]
        + column_sum_scratch()[1:]
        + column_sum_scratch()
        + [
            pltpu.VMEM((128, WIDTH), BF),
            pltpu.VMEM((128, WIDTH), BF),
            pltpu.VMEM((1, WIDTH), F32),
            pltpu.VMEM((128, WIDTH), BF),
            pltpu.VMEM((2, COLUMN), F32),
            pltpu.VMEM((2, COLUMN), F32),
        ]
        + plane_sum_scratch(1536, False)
        + plane_sum_scratch(768, True)
        + [pltpu.VMEM((40, 128), F32), pltpu.VMEM((3, 4, 40, 128), F32)]
        + wires_scratch(120, 50)
        + [pltpu.SemaphoreType.DMA((4,))],
        compiler_params=params(6),
        name="close",
    )(*args)


def finish_kernel(*refs):
    ins, outs = refs[:10], refs[10:]
    vector = ins[9]
    outs[0][...] = ins[0][...]
    for source, target in zip(ins[1:9], outs[1:9]):
        target[...] = source[...].astype(F32)
    shard = lax.axis_index("shard")
    for first, target in ((0, outs[9]), (16, outs[10])):
        line = vector[pl.ds(first + shard // 2, 1), :]
        target[...] = jnp.where(shard % 2 == 0, line[:, 0:64], line[:, 64:128])
    outs[11][...] = vector[32:33, :]
    outs[12][...] = vector[33:34, :]


def finish_call(out, g_tok, *rest):
    tall = pl.BlockSpec((64, WIDTH), lambda i: (i, 0))
    grads, vector = rest[:-1], rest[-1]
    wide = [pl.BlockSpec((64, g.shape[1] // 4), lambda i: (0, i)) for g in grads]
    tops = [jax.ShapeDtypeStruct((1, n), F32) for n in (64, 64, 128, 128)]
    return pl.pallas_call(
        finish_kernel,
        grid=(4,),
        out_shape=(
            jax.ShapeDtypeStruct(out.shape, BF),
            jax.ShapeDtypeStruct(g_tok.shape, F32),
            *(jax.ShapeDtypeStruct(g.shape, F32) for g in grads),
            *tops,
        ),
        in_specs=[tall, tall] + wide + [VMEM],
        out_specs=[tall, tall] + wide + [VMEM] * 4,
        compiler_params=pltpu.CompilerParams(vmem_limit_bytes=LIMIT),
        name="finish",
    )(out, g_tok, *grads, vector)


def on_device(
    tokens, lengths, attn_norm, w_query, w_key, w_value, w_output, q_gain, k_gain, mlp_norm, w_gate, w_up, w_down, cotangent,
):
    freq = THETA ** (-np.arange(0, HEAD, 2).astype(np.float32) / np.float32(HEAD))
    freq = jnp.asarray(np.concatenate([freq, freq])[None].astype(np.float32))
    both_gains = jnp.tile(jnp.pad(jnp.stack([attn_norm, mlp_norm], axis=1), ((0, 0), (0, 126))), (1, 4))
    (
        normed1, w_a, w_w, w_b, cot, raw, query, kv, before, attended, inverse, middle, normed2, cosine, sine, gains, doc_row, doc_col,
    ) = forward_call(
        tokens, cotangent, w_query, w_key, w_value, w_output.T, both_gains, w_gate, w_up, w_down.T, lengths, freq, q_gain[None], k_gain[None]
    )
    w_a, w_w = w_a.reshape(WIDTH, 640), w_w.reshape(WIDTH, 256)
    d_middle, d_branch, mixed, g_in, g_mlp, both_down = turn_call(
        normed2.reshape(COLUMN, WIDTH),
        cot.reshape(COLUMN, WIDTH),
        w_b,
        middle,
        cotangent.reshape(2, 128, WIDTH),
        gains,
    )
    out, g_tokens, g_gate, g_up, g_down, g_query, g_key, g_value, g_output, sums = close_call(
        d_branch.reshape(COLUMN, WIDTH), w_w, w_a, attended, query, before, kv, raw, cosine, sine, doc_row, doc_col, inverse,
        q_gain[None], k_gain[None], g_in, both_down, mixed, middle, d_middle, tokens.reshape(2, 128, WIDTH), gains,
        normed1, g_mlp.reshape(16, 128),
    )

    (
        out, g_tokens, g_gate, g_up, g_down, g_query, g_key, g_value, g_output, g_attn, g_mlp, g_q_gain, g_k_gain,
    ) = finish_call(
        out.reshape(256, WIDTH), g_tokens.reshape(256, WIDTH), g_gate, g_up, g_down, g_query, g_key, g_value, g_output, sums
    )
    return (
        out, g_tokens, g_attn[0], g_query, g_key, g_value, g_output.T, g_q_gain[0], g_k_gain[0], g_mlp[0], g_gate, g_up, g_down.T,
    )


def solution(mesh):
    rows = P(("shard", "dp"), None)
    down = P("shard", "tensor")
    across = P("tensor", "shard")
    one = P("shard")
    return jax.shard_map(
        on_device,
        mesh=mesh,
        in_specs=(rows, P(), one, down, down, down, across, P(), P(), one, down, down, across, rows),
        out_specs=(rows, rows, one, down, down, down, across, P(), P(), one, down, down, across),
        check_vma=False,
    )
```

```python
import functools

import jax
import jax.numpy as jnp
import numpy as np
from jax import lax
from jax.experimental import pallas as pl
from jax.experimental.pallas import tpu as pltpu
from jax.sharding import PartitionSpec as P

HEAD = 128
EPS = 1e-06
THETA = 1000000.0
SCALE = HEAD ** (-0.5)
WIDTH = 2048
COLUMN = 1024
MESH = pl.DeviceIdType.MESH
BF = jnp.bfloat16
F32 = jnp.float32
HBM = pl.BlockSpec(memory_space=pl.ANY)
VMEM = pl.BlockSpec(memory_space=pltpu.VMEM)
LIMIT = 60 * 2**20


class Spot:
    def __init__(self):
        shard = lax.axis_index("shard")
        self.lo = lax.axis_index("dp")
        self.hi = lax.axis_index("tensor")
        self.x = self.hi * 2 + self.lo
        self.y = shard // 8
        self.z = (shard // 2) % 4
        self.c = shard % 2

    def dev(self, dx=0, dy=0, dz=0, other=False):
        x = (self.x + dx) % 4
        y = (self.y + dy) % 4
        z = (self.z + dz) % 4
        c = 1 - self.c if other else self.c
        return ((y * 4 + z) * 2 + c, x % 2, x // 2)

    def dp_mate(self):
        return ((self.y * 4 + self.z) * 2 + self.c, 1 - self.lo, self.hi)

    def column(self, step):
        flat = (self.y * 4 + self.z + step + 16) % 16
        return (flat * 2 + self.c, self.lo, self.hi)


def greet(devices):
    barrier = pltpu.get_barrier_semaphore()
    for device in devices:
        pl.semaphore_signal(barrier, inc=1, device_id=device, device_id_type=MESH)
    pl.semaphore_wait(barrier, len(devices))


class Wires:
    def __init__(self, send, recv, local):
        self.send, self.recv, self.here = send, recv, local
        self.count, self.near = 0, 0
        self.sent = []

    def push(self, src, dst, device):
        i = self.count
        self.count += 1
        copy = pltpu.make_async_remote_copy(
            src_ref=src,
            dst_ref=dst,
            send_sem=self.send.at[i],
            recv_sem=self.recv.at[i],
            device_id=device,
            device_id_type=MESH,
        )
        copy.start()
        self.sent.append(copy)
        return copy

    def local(self, src, dst):
        copy = pltpu.make_async_copy(src, dst, self.here.at[self.near])
        self.near += 1
        copy.start()
        return copy

    def sent_now(self, copy):
        copy.wait_send()
        self.sent = [other for other in self.sent if other is not copy]

    def drain(self):
        assert self.count <= self.send.shape[0] and self.near <= self.here.shape[0]
        for copy in self.sent:
            copy.wait_send()


def wires_scratch(remote, local):
    return [
        pltpu.SemaphoreType.DMA((remote,)),
        pltpu.SemaphoreType.DMA((remote,)),
        pltpu.SemaphoreType.DMA((max(local, 1),)),
    ]


def by_rows(count, step, body):
    def run(i, _):
        body(pl.ds(pl.multiple_of(i * step, step), step))
        return 0

    lax.fori_loop(0, count // step, run, 0)


def add_into(dst, *sources):
    def body(rows):
        total = dst[rows, :].astype(F32)
        for source in sources:
            total = total + source[rows, :].astype(F32)
        dst[rows, :] = total.astype(dst.dtype)

    by_rows(dst.shape[0], 16, body)


def run_all(*parts):
    parts = list(parts)
    while parts:
        for part in list(parts):
            if next(part, StopIteration) is StopIteration:
                parts.remove(part)


def plane_gather(w, spot, pieces, out, eager=False):
    y, z, c = spot.y, spot.z, spot.c
    rows = pl.ds(pl.multiple_of(c * 64, 64), 64)
    swaps, owns = [], []
    for source, size, low in pieces:
        theirs = pl.ds(pl.multiple_of((spot.lo * 2 + 1 - c) * size, size), size)
        mine = pl.ds(pl.multiple_of((spot.lo * 2 + c) * size, size), size)
        at = out.at[y, z, rows, pl.ds(low, size)]
        swaps.append(w.push(source.at[:, theirs], at, spot.dev(other=True)))
        owns.append(w.local(source.at[:, mine], at))
    yield
    for swap, own in zip(swaps, owns):
        swap.wait_recv()
        own.wait()
    ym, yp, zm, zp = (y + 3) % 4, (y + 1) % 4, (z + 3) % 4, (z + 1) % 4
    to_zp, to_zm = spot.dev(dz=1), spot.dev(dz=-1)
    to_yp, to_ym = spot.dev(dy=1), spot.dev(dy=-1)
    a, b = pl.ds(0, 64), pl.ds(64, 64)
    mine_a, mine_b = out.at[y, z, a], out.at[y, z, b]
    a1 = w.push(mine_a, mine_a, to_zp)
    a2 = w.push(mine_a, mine_a, to_zm)
    b1 = w.push(mine_b, mine_b, to_yp)
    b2 = w.push(mine_b, mine_b, to_ym)
    yield
    a1.wait_recv()
    part = out.at[y, zm, pl.ds(0, 32)]
    a3 = w.push(part, part, to_zp)
    b1.wait_recv()
    part = out.at[ym, z, pl.ds(64, 32)]
    b3 = w.push(part, part, to_yp)
    a2.wait_recv()
    part = out.at[y, zp, pl.ds(32, 32)]
    a4 = w.push(part, part, to_zm)
    b2.wait_recv()
    part = out.at[yp, z, pl.ds(96, 32)]
    b4 = w.push(part, part, to_ym)
    lines = ([], [], [], [])

    def pass_on(in_a, in_b):
        for chunk, near, one, two in ((in_a, 0, to_yp, to_ym), (in_b, 2, to_zp, to_zm)):
            lines[near].append(w.push(chunk, chunk, one))
            lines[near + 1].append(w.push(chunk, chunk, two))

    if eager:
        pass_on(mine_a, mine_b)
        pass_on(out.at[y, zm, a], out.at[ym, z, b])
        pass_on(out.at[y, zp, a], out.at[yp, z, b])
    yield
    for copy in (a3, a4, b3, b4):
        copy.wait_recv()
    if eager:
        pass_on(out.at[y, (z + 2) % 4, a], out.at[(y + 2) % 4, z, b])
    else:
        pass_on(out.at[y, :, a], out.at[:, z, b])
    yield

    def arrived(line):
        for copy in lines[line]:
            copy.wait_recv()

    arrived(0)
    part = out.at[ym, pl.ds(0, 2), a]
    a7 = w.push(part, part, to_yp)
    arrived(2)
    part = out.at[pl.ds(0, 2), zm, b]
    b7 = w.push(part, part, to_zp)
    arrived(1)
    part = out.at[yp, pl.ds(2, 2), a]
    a8 = w.push(part, part, to_ym)
    arrived(3)
    part = out.at[pl.ds(2, 2), zp, b]
    b8 = w.push(part, part, to_zm)
    yield
    for copy in (a7, b7, a8, b8):
        copy.wait_recv()


def plane_sum_scratch(columns, resident):
    kept = [
        pltpu.VMEM((2, 2, 64, columns), BF),
        pltpu.VMEM((2, 2, 64, columns), BF),
        pltpu.VMEM((2, 4, 64, columns), BF),
    ]
    return ([] if resident else kept) + [
        pltpu.VMEM((2, 2, 2, 64, columns), BF),
        pltpu.VMEM((2, 2, 4, 64, columns), BF),
        pltpu.VMEM((2, 2, 32, columns), BF),
        pltpu.VMEM((2, 2, 64, columns), BF),
        pltpu.VMEM((128, columns), BF),
        pltpu.VMEM((2, 64, columns), BF),
    ]


def plane_sum(w, spot, part, scratch, resident=False):
    in1, in2, in3, in4, full, both = scratch[-6:]
    c = spot.c
    rows = (pl.ds(0, 64), pl.ds(64, 64))
    lanes = ((spot.y, spot.z), (spot.z, spot.y))
    steps = (("dy", "dz"), ("dz", "dy"))

    def view(h, k, low, size):
        at = (lanes[h][0] + k) % 4
        if h == 0:
            return part.at[at, pl.ds(low, size), rows[h]]
        return part.at[pl.ds(low, size), at, rows[h]]

    def held(h, j):
        if not resident:
            return scratch[2].at[h, j]
        if h == 0:
            return part.at[spot.y, j, rows[h]]
        return part.at[j, spot.z, rows[h]]

    def to(h, stage, step):
        return spot.dev(**{steps[h][stage]: step})

    loads, first, second, early = [], [], [], []
    for h in range(2):
        first.append(
            (
                w.push(view(h, 2, 0, 2), in1.at[h, 0], to(h, 0, 1)),
                w.push(view(h, 2, 2, 2), in1.at[h, 1], to(h, 0, -1)),
            )
        )
    for h in range(2):
        if resident:
            plus, minus = view(h, 1, 0, 2), view(h, 3, 2, 2)
            loads.append((plus, minus))
            continue
        plus, minus = scratch[0].at[h], scratch[1].at[h]
        loads.append(
            (
                plus,
                minus,
                w.local(view(h, 1, 0, 2), plus),
                w.local(view(h, 3, 2, 2), minus),
                w.local(view(h, 0, 0, 4), scratch[2].at[h]),
            )
        )
    yield
    for h in range(2):
        plus, minus = loads[h][:2]
        if not resident:
            loads[h][2].wait()
        first[h][0].wait_recv()
        for j in range(2):
            add_into(plus.at[j], in1.at[h, 0, j])
        one = w.push(plus, in2.at[h, 0, pl.ds(0, 2)], to(h, 0, 1))
        if not resident:
            loads[h][3].wait()
        first[h][1].wait_recv()
        for j in range(2):
            add_into(minus.at[j], in1.at[h, 1, j])
        two = w.push(minus, in2.at[h, 1, pl.ds(2, 2)], to(h, 0, -1))
        second.append((one, two))
    for h in range(2):
        early.append(
            (
                w.push(view(h, 1, 2, 2), in2.at[h, 0, pl.ds(2, 2)], to(h, 0, 1)),
                w.push(view(h, 3, 0, 2), in2.at[h, 1, pl.ds(0, 2)], to(h, 0, -1)),
            )
        )
    yield
    third, early3 = [], []
    for h in range(2):
        if not resident:
            loads[h][4].wait()
        for copy in early[h] + second[h]:
            copy.wait_recv()
        at = [(lanes[h][1] + k) % 4 for k in range(4)]
        add_into(held(h, at[2]), in2.at[h, 0, at[2]], in2.at[h, 1, at[2]])
        far = held(h, at[2])
        third.append(
            (
                w.push(far.at[pl.ds(0, 32)], in3.at[h, 0], to(h, 1, 1)),
                w.push(far.at[pl.ds(32, 32)], in3.at[h, 1], to(h, 1, -1)),
            )
        )
        add_into(held(h, at[1]), in2.at[h, 0, at[1]], in2.at[h, 1, at[1]])
        one = w.push(held(h, at[1]).at[pl.ds(32, 32)], in4.at[h, 0, pl.ds(32, 32)], to(h, 1, 1))
        add_into(held(h, at[3]), in2.at[h, 0, at[3]], in2.at[h, 1, at[3]])
        two = w.push(held(h, at[3]).at[pl.ds(0, 32)], in4.at[h, 1, pl.ds(0, 32)], to(h, 1, -1))
        early3.append((one, two))
        add_into(held(h, at[0]), in2.at[h, 0, at[0]], in2.at[h, 1, at[0]])
    yield
    fourth = []
    for h in range(2):
        at = [(lanes[h][1] + k) % 4 for k in range(4)]
        third[h][0].wait_recv()
        piece = held(h, at[1]).at[pl.ds(0, 32)]
        add_into(piece, in3.at[h, 0])
        one = w.push(piece, in4.at[h, 0, pl.ds(0, 32)], to(h, 1, 1))
        third[h][1].wait_recv()
        piece = held(h, at[3]).at[pl.ds(32, 32)]
        add_into(piece, in3.at[h, 1])
        two = w.push(piece, in4.at[h, 1, pl.ds(32, 32)], to(h, 1, -1))
        fourth.append((one, two))
    yield
    for h in range(2):
        for copy in early3[h] + fourth[h]:
            copy.wait_recv()
        mine = held(h, lanes[h][1])
        target = full.at[rows[h]]

        def body(r):
            total = mine[r, :].astype(F32) + in4[h, 0, r, :].astype(F32)
            target[r, :] = (total + in4[h, 1, r, :].astype(F32)).astype(BF)

        by_rows(64, 16, body)
    theirs = full.at[pl.ds(pl.multiple_of((1 - c) * 64, 64), 64)]
    mine = full.at[pl.ds(pl.multiple_of(c * 64, 64), 64)]
    swap = w.push(theirs, both.at[c], spot.dev(other=True))

    def keep(r):
        both[c, r, :] = mine[r, :]

    by_rows(64, 16, keep)
    yield
    swap.wait_recv()


def mate_share(w, spot, both, outs):
    copies = []
    for out, low, size in outs:
        for core in range(2):
            piece = both.at[core, :, pl.ds(low, size)]
            at = pl.ds(pl.multiple_of((spot.lo * 2 + core) * size, size), size)
            copies.append((w.local(piece, out.at[:, at]), w.push(piece, out.at[:, at], spot.dp_mate())))
    yield
    for near, far in copies:
        near.wait()
        far.wait_recv()


def column_sum_scratch():
    return [
        pltpu.VMEM((4, 128, WIDTH), BF),
        pltpu.VMEM((4, 128, WIDTH), BF),
        pltpu.VMEM((2, 64, WIDTH), BF),
        pltpu.VMEM((2, 128, WIDTH), BF),
    ]


def column_sum(w, spot, part, scratch, finish, resident=False):
    own, got, in1, in2 = scratch
    x, c = spot.x, spot.c
    right, left = spot.dev(dx=1), spot.dev(dx=-1)
    places = [((x + k) % 4 % 2, (x + k) % 4 // 2) for k in range(4)]
    swaps, loads = {}, {}
    for k in (2, 1, 3, 0):
        swaps[k] = w.push(part.at[1 - c, places[k][0], places[k][1]], got.at[k], spot.dev(other=True))
    if resident:
        own = [part.at[c, lo, hi] for lo, hi in places]
    else:
        for k in (2, 1, 3, 0):
            loads[k] = w.local(part.at[c, places[k][0], places[k][1]], own.at[k])
        own = [own.at[k] for k in range(4)]
    yield

    def merge(k):
        if not resident:
            loads[k].wait()
        swaps[k].wait_recv()
        add_into(own[k], got.at[k])

    low, high = pl.ds(0, 64), pl.ds(64, 64)
    merge(2)
    far1 = w.push(own[2].at[low], in1.at[0], right)
    far2 = w.push(own[2].at[high], in1.at[1], left)
    merge(1)
    one = w.push(own[1].at[high], in2.at[0, high], right)
    merge(3)
    two = w.push(own[3].at[low], in2.at[1, low], left)
    merge(0)
    yield
    far1.wait_recv()
    add_into(own[1].at[low], in1.at[0])
    three = w.push(own[1].at[low], in2.at[0, low], right)
    far2.wait_recv()
    add_into(own[3].at[high], in1.at[1])
    four = w.push(own[3].at[high], in2.at[1, high], left)
    yield
    for copy in (one, two, three, four):
        copy.wait_recv()

    def total(rows):
        return own[0][rows, :].astype(F32) + in2[0, rows, :].astype(F32) + in2[1, rows, :].astype(F32)

    finish(total)


def column_share(w, spot, mine, out):
    x, c = spot.x, spot.c
    right, left, mate = spot.dev(dx=1), spot.dev(dx=-1), spot.dev(other=True)

    def slot(k):
        at = (x + k + 4) % 4
        return out.at[c, at % 2, at // 2]

    low, high = pl.ds(0, 64), pl.ds(64, 64)
    own = w.local(mine, slot(0))
    a = w.push(mine.at[low], slot(0).at[low], right)
    b = w.push(mine.at[high], slot(0).at[high], left)
    d = w.push(mine, slot(0), mate)
    a2 = w.push(mine.at[high], slot(0).at[high], right)
    b2 = w.push(mine.at[low], slot(0).at[low], left)
    yield
    a.wait_recv()
    e = w.push(slot(-1).at[low], slot(-1).at[low], right)
    last = [w.push(slot(-1).at[low], slot(-1).at[low], mate)]
    b.wait_recv()
    g = w.push(slot(1).at[high], slot(1).at[high], left)
    last.append(w.push(slot(1).at[high], slot(1).at[high], mate))
    yield
    a2.wait_recv()
    last.append(w.push(slot(-1).at[high], slot(-1).at[high], mate))
    b2.wait_recv()
    last.append(w.push(slot(1).at[low], slot(1).at[low], mate))
    e.wait_recv()
    last.append(w.push(slot(2).at[low], slot(2).at[low], mate))
    g.wait_recv()
    last.append(w.push(slot(2).at[high], slot(2).at[high], mate))
    yield
    own.wait()
    for copy in [d] + last:
        copy.wait_recv()


def token_share(w, spot, block, out):
    own_at, far_at = spot.c * 2 + spot.lo, spot.c * 2 + 1 - spot.lo
    right, left, mate = spot.dev(dx=1), spot.dev(dx=-1), spot.dev(other=True)
    low, high = pl.ds(0, 128), pl.ds(128, 128)
    own = w.local(block, out.at[own_at])
    a = w.push(block.at[low], out.at[own_at, low], right)
    b = w.push(block.at[high], out.at[own_at, high], left)
    d = w.push(block, out.at[own_at], mate)
    yield
    a.wait_recv()
    part = out.at[far_at, low]
    e = w.push(part, part, mate)
    b.wait_recv()
    part = out.at[far_at, high]
    f = w.push(part, part, mate)
    yield
    own.wait()
    for copy in (d, e, f):
        copy.wait_recv()


def pair_share(w, spot, mine, out):
    own = w.local(mine, out.at[spot.hi])
    a = w.push(mine, out.at[spot.hi], spot.dev(dx=2))
    yield
    own.wait()
    a.wait_recv()


def neighbours(spot, x=False, yz=False, core=False, pair=False, far=False):
    found = []
    if x:
        found += [spot.dev(dx=1), spot.dev(dx=-1)]
    if yz:
        found += [spot.dev(dy=1), spot.dev(dy=-1), spot.dev(dz=1), spot.dev(dz=-1)]
    if core:
        found += [spot.dev(other=True)]
    if pair:
        found += [spot.dev(dx=2)]
    if far:
        found += [spot.dev(dy=2), spot.dev(dz=2)]
    return found


BLOCK = 256
SPAN = COLUMN + BLOCK
NT = (((1,), (1,)), ((), ()))
TN = (((0,), (0,)), ((), ()))
NN = (((1,), (0,)), ((), ()))


def dot(a, b, dims):
    return lax.dot_general(a, b, dims, preferred_element_type=F32)


def rms_of(rows):
    inverse = lax.rsqrt(jnp.mean(rows * rows, axis=-1, keepdims=True) + EPS)
    return rows * inverse, inverse


def turn_half(rows):
    half = HEAD // 2
    return jnp.concatenate([-rows[:, half:], rows[:, :half]], axis=-1)


def params(collective_id):
    return pltpu.CompilerParams(
        collective_id=collective_id, has_side_effects=True, vmem_limit_bytes=LIMIT
    )


def own_block(ref, spot):
    return ref.at[spot.c, spot.lo, spot.hi]


def place_rows(spot, lengths, freq, doc_row, doc_col, cosine, sine):
    first = (spot.y * 4 + spot.z - 1) * COLUMN
    rows = lax.broadcasted_iota(jnp.int32, (16, 128), 0) * 128 + first
    rows = rows + lax.broadcasted_iota(jnp.int32, (16, 128), 1)
    document = jnp.zeros((16, 128), jnp.int32)
    start = jnp.zeros((16, 128), jnp.int32)
    bound = jnp.int32(0)
    for d in range(lengths.shape[1]):
        bound = bound + lengths[0, d]
        passed = rows >= bound
        document = document + passed.astype(jnp.int32)
        start = jnp.where(passed, bound, start)
    document = jnp.where(rows >= 0, document, -1).astype(F32)
    place = (rows - start).astype(F32)
    for g in range(16):
        line = document[g : g + 1, :]
        at = slice(g * 128, (g + 1) * 128)
        doc_row[:, at] = line
        doc_col[at, :] = jnp.transpose(jnp.broadcast_to(line, (128, 128)))
        if g >= 8:
            down = jnp.transpose(jnp.broadcast_to(place[g : g + 1, :], (128, 128)))
            angles = down * freq[...]
            at = slice((g - 8) * 128, (g - 7) * 128)
            cosine[at, :] = jnp.cos(angles)
            sine[at, :] = jnp.sin(angles)


def turned_head(raw, scale, cosine, sine):
    unit = rms_of(raw)[0] * scale
    return (unit * cosine + turn_half(unit) * sine).astype(BF)


def forward_kernel(
    tok, cot, x_q, x_k, x_v, x_o, x_gains, x_gate, x_up, x_down, lengths, freq, q_gain, k_gain,
    normed1, o_a, o_w, w_b, cot_all, o_raw, o_query, o_kv, o_before, o_attended, o_inverse, mid, normed2, o_cosine, o_sine, gains, doc_row, o_docs,
    w_a, w_w, raw, query, kv, before, attended, inverse, cosine, sine, doc_col,
    tok_all, low1, roots, top, total, branch, got, in1, in2, low, send, recv, here,
):
    spot = Spot()
    greet(neighbours(spot, x=True, yz=True, core=True) + [spot.column(1), spot.column(-1)])
    w = Wires(send, recv, here)
    first_pieces = ((x_q, 256, 0), (x_k, 128, 256), (x_v, 128, 384), (x_gains, 128, 512))
    take_a = plane_gather(w, spot, first_pieces, w_a, eager=True)
    take_w = plane_gather(w, spot, ((x_o, 256, 0),), w_w)
    take_b = plane_gather(w, spot, ((x_gate, 768, 0), (x_up, 768, 768), (x_down, 768, 1536)), w_b)
    take_tok = token_share(w, spot, tok, tok_all)
    take_cot = token_share(w, spot, cot, cot_all)
    keeps = []

    def keep(source, target):
        keeps.append(w.local(source, target))

    def go(*parts):
        for part in parts:
            next(part, None)

    go(take_a, take_tok, take_a, take_w, take_b)
    place_rows(spot, lengths, freq, doc_row, doc_col, cosine, sine)
    keep(cosine, o_cosine)
    keep(sine, o_sine)
    keep(doc_col, o_docs)
    go(take_a, take_a, take_w, take_tok, take_a, take_tok, take_w)

    def roots_of(i, _):
        rows = pl.ds(pl.multiple_of(i * 32, 32), 32)
        values = tok_all[i // 8, pl.ds(pl.multiple_of(i % 8 * 32, 32), 32), :].astype(F32)
        roots[rows, :] = lax.rsqrt(jnp.mean(values * values, axis=-1, keepdims=True) + EPS)
        return 0

    lax.fori_loop(0, 32, roots_of, 0)
    go(take_a, take_cot, take_b, take_w)
    keep(w_a, o_a)
    for i in range(16):
        block = jnp.transpose(w_a[i // 4, i % 4, :, 512:640].astype(F32))
        gains[:, i * 128 : (i + 1) * 128] = block[0:2, :]

    def norm_rows(i, _):
        rows = pl.ds(pl.multiple_of(i * 32, 32), 32)
        values = tok_all[i // 8, pl.ds(pl.multiple_of(i % 8 * 32, 32), 32), :].astype(F32)
        low1[rows, :] = (values * roots[rows, :] * gains[0:1, :]).astype(BF)
        return 0

    lax.fori_loop(0, 32, norm_rows, 0)
    keep(low1, normed1)

    def project_kv(i, _):
        rows = pl.ds(pl.multiple_of(i * BLOCK, BLOCK), BLOCK)
        out = dot(low1[rows, :], w_a[:, :, :, 256:512].reshape(WIDTH, 256), NN)
        raw[rows, 256:512] = out
        kv[rows, :HEAD] = turned_head(out[:, :HEAD], k_gain[...].astype(F32), cosine[rows, :], sine[rows, :])
        kv[rows, HEAD:] = out[:, HEAD:].astype(BF)
        return 0

    def project_q(i, _):
        rows = pl.ds(pl.multiple_of(i * BLOCK, BLOCK), BLOCK)
        out = dot(low1[rows, :], w_a[:, :, :, 0:256].reshape(WIDTH, 256), NN)
        raw[rows, 0:256] = out
        for h in range(2):
            span = slice(h * HEAD, (h + 1) * HEAD)
            query[rows, span] = turned_head(out[:, span], q_gain[...].astype(F32), cosine[rows, :], sine[rows, :])
        return 0

    pass_kv = []
    for i in range(4):
        project_kv(i, 0)
        rows = pl.ds(i * BLOCK, BLOCK)
        pass_kv.append(w.push(kv.at[rows], before.at[rows], spot.column(1)))
    keep(kv, o_kv)
    go(take_w, take_b)
    lax.fori_loop(0, 4, project_q, 0)
    keep(raw, o_raw)
    keep(query, o_query)
    go(take_cot)

    def weights_of(i, h, keys, docs, causal):
        rows = slice(i * BLOCK, (i + 1) * BLOCK)
        scores = dot(query[rows, h * HEAD : (h + 1) * HEAD], keys, NT) * SCALE
        valid = doc_col[COLUMN + i * BLOCK : COLUMN + (i + 1) * BLOCK, 0:1] == docs
        if causal:
            row = lax.broadcasted_iota(jnp.int32, scores.shape, 0) + i * BLOCK
            valid = valid & (lax.broadcasted_iota(jnp.int32, scores.shape, 1) <= row)
        return jnp.where(valid, jnp.exp(scores), 0.0)

    for i in range(4):
        rows, end = slice(i * BLOCK, (i + 1) * BLOCK), (i + 1) * BLOCK
        for h in range(2):
            weight = weights_of(i, h, kv[0:end, :HEAD], doc_row[:, COLUMN : COLUMN + end], True)
            total[rows, h : h + 1] = jnp.sum(weight, axis=-1, keepdims=True)
            top[rows, h * HEAD : (h + 1) * HEAD] = dot(weight.astype(BF), kv[0:end, HEAD:], NN)
    for copy in pass_kv:
        copy.wait_recv()
    keep(before, o_before)
    go(take_w, take_b)
    keep(w_w, o_w)
    for i in range(4):
        rows, low_key = slice(i * BLOCK, (i + 1) * BLOCK), i * BLOCK
        for h in range(2):
            span = slice(h * HEAD, (h + 1) * HEAD)
            weight = weights_of(i, h, before[low_key:, :HEAD], doc_row[:, low_key:COLUMN], False)
            back = 1.0 / (total[rows, h : h + 1] + jnp.sum(weight, axis=-1, keepdims=True))
            inverse[rows, h : h + 1] = back
            attended[rows, span] = ((top[rows, span] + dot(weight.astype(BF), before[low_key:, HEAD:], NN)) * back).astype(BF)
    keep(attended, o_attended)
    keep(inverse, o_inverse)

    def branch_of(core):
        def one(lo, _):
            rows = pl.ds(pl.multiple_of((core * 2 + lo) * BLOCK, BLOCK), BLOCK)
            out = dot(attended[rows, :], w_w[...].reshape(WIDTH, 256), NT)
            branch[core, lo] = out.astype(BF).reshape(2, 128, WIDTH)
            return 0

        lax.fori_loop(0, 2, one, 0)

    def finish(add):
        def body(rows):
            base = tok[pl.ds(pl.multiple_of(spot.hi * 128 + rows.start, 16), 16), :].astype(F32)
            middle = base + add(rows)
            mid[rows, :] = middle
            root = lax.rsqrt(jnp.mean(middle * middle, axis=-1, keepdims=True) + EPS)
            low[rows, :] = (middle * root * gains[1:2, :]).astype(BF)

        by_rows(128, 16, body)

    branch_of(1 - spot.c)
    fold = column_sum(w, spot, branch, (None, got, in1, in2), finish, resident=True)
    go(fold)
    branch_of(spot.c)
    go(fold, fold, fold, take_cot)
    share = column_share(w, spot, low, normed2)
    go(share, take_b, share, share, take_b, share)
    assert all(g.gi_frame is None for g in (take_a, take_w, take_b, take_tok, take_cot, fold, share))
    for copy in keeps:
        copy.wait()
    w.drain()


def forward_call(*args):
    def shape(*sizes, kind=BF):
        return jax.ShapeDtypeStruct(sizes, kind)

    kept = (
        shape(4, 4, 128, 640),
        shape(4, 4, 128, 256),
        shape(COLUMN, 512, kind=F32),
        shape(COLUMN, 256),
        shape(COLUMN, 256),
        shape(COLUMN, 256),
        shape(COLUMN, 256),
        shape(COLUMN, 2, kind=F32),
        shape(COLUMN, HEAD, kind=F32),
        shape(COLUMN, HEAD, kind=F32),
        shape(2 * COLUMN, 128, kind=F32),
    )
    outs = (
        (shape(COLUMN, WIDTH), HBM),
        (kept[0], HBM),
        (kept[1], HBM),
        (shape(4, 4, 128, 2304), HBM),
        (shape(4, 256, WIDTH), HBM),
        *((k, HBM) for k in kept[2:8]),
        (shape(128, WIDTH, kind=F32), VMEM),
        (shape(2, 2, 2, 128, WIDTH), HBM),
        (kept[8], HBM),
        (kept[9], HBM),
        (shape(2, WIDTH, kind=F32), VMEM),
        (shape(1, 2 * COLUMN, kind=F32), VMEM),
        (kept[10], HBM),
    )
    return pl.pallas_call(
        forward_kernel,
        out_shape=tuple(o[0] for o in outs),
        in_specs=[VMEM] * 10 + [pl.BlockSpec(memory_space=pltpu.SMEM)] + [VMEM] * 3,
        out_specs=tuple(o[1] for o in outs),
        scratch_shapes=[pltpu.VMEM(o.shape, o.dtype) for o in kept]
        + [
            pltpu.VMEM((4, 256, WIDTH), BF),
            pltpu.VMEM((COLUMN, WIDTH), BF),
            pltpu.VMEM((COLUMN, 1), F32),
            pltpu.VMEM((COLUMN, 256), F32),
            pltpu.VMEM((COLUMN, 2), F32),
            pltpu.VMEM((2, 2, 2, 128, WIDTH), BF),
        ]
        + column_sum_scratch()[1:]
        + [pltpu.VMEM((128, WIDTH), BF)]
        + wires_scratch(112, 36),
        compiler_params=params(1),
        name="forward",
    )(*args)


def rms_back(total, base, gain, rows, extra, out, gain_grad):
    values = base[rows, :].astype(F32)
    inverse = lax.rsqrt(jnp.mean(values * values, axis=-1, keepdims=True) + EPS)
    normed = values * inverse
    grad = total(rows)
    scaled = grad * gain[...]
    back = inverse * (scaled - normed * jnp.mean(scaled * normed, axis=-1, keepdims=True))
    gain_grad[...] += jnp.sum(grad * normed, axis=0, keepdims=True)
    out[rows, :] = (extra[rows, :].astype(F32) + back).astype(out.dtype)


def turn_kernel(
    normed, cot, w_b, mid, cot_own, gain, dmid, d_branch, mixed, g_in, gain_grad, both_out,
    nv, cv, wv, hidden, d_both, part, g_down, g_part, mixed_part, both_n, both_c, both_d, got, in1, in2, low, top,
    p0, p1, p2, p3, p4, p5, send, recv, here, tiles,
):
    spot = Spot()
    w = Wires(send, recv, here)

    def two(k):
        at = (spot.x + k) % 4
        lo, hi = at % 2, at // 2
        theirs = pl.ds(pl.multiple_of(((1 - spot.c) * 2 + lo) * 256 + hi * 128, 128), 128)
        mine = pl.ds(pl.multiple_of((spot.c * 2 + lo) * 256 + hi * 128, 128), 128)
        return lo, hi, theirs, mine

    def bring(k):
        _, _, theirs, mine = two(k)
        return [w.local(source.at[r], target.at[r]) for source, target in ((normed, nv), (cot, cv)) for r in (theirs, mine)]

    def bring_weights(j):
        columns = [pl.ds(j * 256 + low_column, 256) for low_column in (0, 768, 1536)]
        return [w.local(w_b.at[:, :, :, at], wv.at[:, :, :, at]) for at in columns]

    rows_in, weights_in = {2: bring(2)}, [bring_weights(0)]
    greet(neighbours(spot, x=True, yz=True, core=True))
    weights_in += [bring_weights(1), bring_weights(2)]
    for k in (1, 3, 0):
        rows_in[k] = bring(k)
    load = w.local(cot_own.at[spot.hi], top)
    gain_grad[...] = jnp.zeros_like(gain_grad)

    def weight(low_column, size):
        return wv[:, :, :, low_column : low_column + size].reshape(WIDTH, size)

    def units(k):
        _, _, theirs, mine = two(k)
        for copy in rows_in[k]:
            copy.wait()
        both_n[0:128, :] = nv[theirs, :]
        both_n[128:, :] = nv[mine, :]
        both_c[0:128, :] = cv[theirs, :]
        both_c[128:, :] = cv[mine, :]

        def one(j, _):
            a = pl.ds(pl.multiple_of(j * 256, 256), 256)
            b = pl.ds(pl.multiple_of(j * 256 + 768, 256), 256)
            d = pl.ds(pl.multiple_of(j * 256 + 1536, 256), 256)
            gate = dot(both_n[...], wv[:, :, :, a].reshape(WIDTH, 256), NN)
            up = dot(both_n[...], wv[:, :, :, b].reshape(WIDTH, 256), NN)
            d_hidden = dot(both_c[...], wv[:, :, :, d].reshape(WIDTH, 256), NN)
            sigma = lax.logistic(gate)
            active = gate * sigma
            unit = (active * up).astype(BF)
            d_gate = (d_hidden * up * sigma * (1.0 + gate * (1.0 - sigma))).astype(BF)
            d_up = (d_hidden * active).astype(BF)
            for half, rows in ((slice(0, 128), theirs), (slice(128, 256), mine)):
                hidden[rows, a] = unit[half, :]
                d_both[rows, a] = d_gate[half, :]
                d_both[rows, b] = d_up[half, :]
            return 0

        if k != 2:
            lax.fori_loop(0, 3, one, 0)
            return
        for j in range(3):
            for copy in weights_in[j]:
                copy.wait()
            one(j, 0)

    def back(k):
        lo, hi, theirs, mine = two(k)
        both_d[0:128, :] = d_both[theirs, :]
        both_d[128:, :] = d_both[mine, :]
        out = dot(both_d[...], weight(0, 1536), NT).astype(BF)
        part[1 - spot.c, lo, hi] = out[:128]
        part[spot.c, lo, hi] = out[128:]
        swaps[k] = w.push(part.at[1 - spot.c, lo, hi], got.at[k], spot.dev(other=True))

    swaps = {}

    def own(k):
        lo, hi, _, _ = two(k)
        return part.at[spot.c, lo, hi]

    def merge(k):
        swaps[k].wait_recv()
        add_into(own(k), got.at[k])

    def finish(total):
        load.wait()

        def body(rows):
            rms_back(total, mid, gain.at[1:2], rows, top, dmid, gain_grad)
            low[rows, :] = dmid[rows, :].astype(BF)

        by_rows(128, 16, body)

    def go(*parts):
        for one in parts:
            next(one, None)

    def down_tile(t, _):
        lanes = pl.ds(pl.multiple_of(t * BLOCK, BLOCK), BLOCK)
        out = dot(cv[:, lanes], hidden[...], TN)
        g_down[t // 2, pl.ds(t % 2 * 2, 2)] = out.astype(BF).reshape(2, 128, 768)
        return 0

    def in_copy(t):
        at = (t // 2, pl.ds(t % 2 * 2, 2))
        return pltpu.make_async_copy(g_part.at[at], g_in.at[at], tiles.at[2, t])

    def in_tile(t, _):
        lanes = pl.ds(pl.multiple_of(t * BLOCK, BLOCK), BLOCK)
        out = dot(nv[:, lanes], d_both[...], TN)
        g_part[t // 2, pl.ds(t % 2 * 2, 2)] = out.astype(BF).reshape(2, 128, 1536)
        in_copy(t).start()
        return 0

    def mixed_block(i, _):
        rows = pl.ds(pl.multiple_of(i * BLOCK, BLOCK), BLOCK)
        out = dot(hidden[rows, :], weight(1536, 768), NT)
        mixed_part[i // 2, i % 2] = out.astype(BF).reshape(2, 128, WIDTH)
        return 0

    right, left = spot.dev(dx=1), spot.dev(dx=-1)
    lows, highs = pl.ds(0, 64), pl.ds(64, 64)
    units(2)
    back(2)
    units(1)
    merge(2)
    far1 = w.push(own(2).at[lows], in1.at[0], right)
    far2 = w.push(own(2).at[highs], in1.at[1], left)
    back(1)
    units(3)
    merge(1)
    one = w.push(own(1).at[highs], in2.at[0, highs], right)
    back(3)
    units(0)
    merge(3)
    two_ = w.push(own(3).at[lows], in2.at[1, lows], left)
    far1.wait_recv()
    add_into(own(1).at[lows], in1.at[0])
    three = w.push(own(1).at[lows], in2.at[0, lows], right)
    far2.wait_recv()
    add_into(own(3).at[highs], in1.at[1])
    four = w.push(own(3).at[highs], in2.at[1, highs], left)
    back(0)
    lax.fori_loop(0, 8, down_tile, 0)
    down = plane_sum(w, spot, g_down, (p0, p1, p2, p3, p4, p5), resident=True)
    go(down)
    lax.fori_loop(0, 4, in_tile, 0)
    go(down)
    merge(0)
    for copy in (one, two_, three, four):
        copy.wait_recv()
    mine_ref = own(0)

    def total(rows):
        return mine_ref[rows, :].astype(F32) + in2[0, rows, :].astype(F32) + in2[1, rows, :].astype(F32)

    finish(total)
    share = column_share(w, spot, low, d_branch)
    go(share)
    lax.fori_loop(0, 4, mixed_block, 0)
    keep = w.local(mixed_part, mixed)
    go(share, down)
    lax.fori_loop(4, 8, in_tile, 0)
    go(share, down, share, down, down)
    assert share.gi_frame is None and down.gi_frame is None
    last = w.local(p5, both_out)
    for t in range(8):
        in_copy(t).wait()
    keep.wait()
    last.wait()
    w.drain()


def turn_call(normed, cot, w_b, mid, cot_own, gain):
    blocks = jax.ShapeDtypeStruct((2, 2, 2, 128, WIDTH), BF)
    return pl.pallas_call(
        turn_kernel,
        out_shape=(
            jax.ShapeDtypeStruct((128, WIDTH), F32),
            blocks,
            blocks,
            jax.ShapeDtypeStruct((4, 4, 128, 1536), BF),
            jax.ShapeDtypeStruct((1, WIDTH), F32),
            jax.ShapeDtypeStruct((2, 64, 768), BF),
        ),
        in_specs=[HBM, HBM, HBM, VMEM, HBM, VMEM],
        out_specs=(VMEM, HBM, HBM, HBM, VMEM, HBM),
        scratch_shapes=[
            pltpu.VMEM((COLUMN, WIDTH), BF),
            pltpu.VMEM((COLUMN, WIDTH), BF),
            pltpu.VMEM((4, 4, 128, 2304), BF),
            pltpu.VMEM((COLUMN, 768), BF),
            pltpu.VMEM((COLUMN, 1536), BF),
            pltpu.VMEM((2, 2, 2, 128, WIDTH), BF),
            pltpu.VMEM((4, 4, 128, 768), BF),
            pltpu.VMEM((4, 4, 128, 1536), BF),
            pltpu.VMEM((2, 2, 2, 128, WIDTH), BF),
            pltpu.VMEM((BLOCK, WIDTH), BF),
            pltpu.VMEM((BLOCK, WIDTH), BF),
            pltpu.VMEM((BLOCK, 1536), BF),
        ]
        + column_sum_scratch()[1:]
        + [pltpu.VMEM((128, WIDTH), BF)] * 2
        + plane_sum_scratch(768, True)
        + wires_scratch(64, 36)
        + [pltpu.SemaphoreType.DMA((3, 8))],
        compiler_params=params(4),
        name="turn",
    )(normed, cot, w_b, mid, cot_own, gain)


def sum_everywhere(w, spot, vector, pair, lines):
    a = w.push(vector, pair, spot.dev(other=True))
    yield
    a.wait_recv()
    w.sent_now(a)
    vector[...] = vector[...] + pair[...]
    yield
    for stage, (axis, at) in enumerate((("dx", spot.x), ("dy", spot.y), ("dz", spot.z))):
        slots = lines.at[stage]
        slots[at] = vector[...]
        copies = [w.push(vector, slots.at[at], spot.dev(**{axis: k})) for k in (1, 2, 3)]
        yield
        for copy in copies:
            copy.wait_recv()
            w.sent_now(copy)
        vector[...] = slots[0] + slots[1] + slots[2] + slots[3]
        yield


def as_row(column):
    return jnp.transpose(jnp.broadcast_to(column, (column.shape[0], HEAD)))[0:1, :]


def close_kernel(
    d_branch, h_w, h_a, h_attended, h_query, h_before, h_kv, h_raw, h_cosine, h_sine, doc_row, h_docs, h_inverse, q_gain, k_gain,
    g_in, both_down, mixed, mid, dmid, tok, gain, normed1, g_mlp,
    out, g_tok, o_gate, o_up, o_down, o_q, o_k, o_v, o_out, vector,
    w_w, w_a, attended, query, before, kv, raw, cosine, sine, doc_col, inverse,
    db, do, dq, dkv, d_before, came, d_raw, part, g_out, got, in1, in2,
    m_own, m_got, m_in1, m_in2, result, base, gain_grad, low, delta, back,
    a0, a1, a2, a3, a4, a5, a6, a7, a8, b0, b1, b2, b3, b4, b5, pair, lines, send, recv, here, tiles,
):
    spot = Spot()
    w = Wires(send, recv, here)

    def block(i):
        rows = pl.ds(pl.multiple_of(i * BLOCK, BLOCK), BLOCK)
        return pltpu.make_async_copy(d_branch.at[rows], db.at[rows], tiles.at[i])

    for i in range(4):
        block(i).start()
    fetched_w = w.local(h_w, w_w)
    fetched = [
        w.local(source, target)
        for source, target in (
            (h_attended, attended), (h_query, query), (h_before, before), (h_inverse, inverse), (h_docs, doc_col),
            (h_kv, kv), (h_raw, raw), (h_cosine, cosine), (h_sine, sine), (h_a, w_a),
        )
    ]
    load_tok = w.local(tok.at[spot.hi], base)
    greet(
        neighbours(spot, x=True, yz=True, core=True, pair=True, far=True)
        + [spot.column(1), spot.column(-1)]
    )

    def go(*parts):
        for one in parts:
            next(one, None)

    sum_in = plane_sum(w, spot, g_in, (a0, a1, a2, a3, a4, a5, a6, a7, a8))
    go(sum_in)

    def finish_out(total):
        def body(rows):
            result[rows, :] = (mid[rows, :] + total(rows)).astype(BF)

        by_rows(128, 16, body)

    fold_out = column_sum(w, spot, mixed, (m_own, m_got, m_in1, m_in2), finish_out)
    share_out = pair_share(w, spot, result, out)
    share_down = mate_share(w, spot, both_down, ((o_down, 0, 768),))
    go(fold_out, share_down)
    gain_grad[...] = jnp.zeros_like(gain_grad)
    vector[...] = jnp.zeros_like(vector)
    dkv[...] = jnp.zeros_like(dkv)
    dq[...] = jnp.zeros_like(dq)

    fetched_w.wait()

    def upstream_of(i, _):
        block(i).wait()
        rows = pl.ds(pl.multiple_of(i * BLOCK, BLOCK), BLOCK)
        do[rows, :] = dot(db[rows, :], w_w[...], NN).astype(BF)
        return 0

    lax.fori_loop(0, 4, upstream_of, 0)
    go(fold_out)
    for copy in fetched:
        copy.wait()

    def tile_out(t, _):
        lanes = pl.ds(pl.multiple_of(t * BLOCK, BLOCK), BLOCK)
        at = (t // 2, pl.ds(t % 2 * 2, 2), slice(None), slice(512, 768))
        g_out[at] = dot(db[:, lanes], attended[...], TN).astype(BF).reshape(2, 128, 256)
        return 0

    def tile(t, _):
        lanes = pl.ds(pl.multiple_of(t * BLOCK, BLOCK), BLOCK)
        at = (t // 2, pl.ds(t % 2 * 2, 2), slice(None), slice(0, 512))
        g_out[at] = dot(db[:, lanes], d_raw[...], TN).astype(BF).reshape(2, 128, 512)
        return 0


    for i in range(4):
        rows = slice(i * BLOCK, (i + 1) * BLOCK)
        product = attended[rows, :].astype(F32) * do[rows, :].astype(F32)
        for h in range(2):
            delta[h : h + 1, rows] = as_row(jnp.sum(product[:, h * HEAD : (h + 1) * HEAD], axis=-1, keepdims=True))
            back[h : h + 1, rows] = as_row(inverse[rows, h : h + 1])

    def attend_back(rows, keys_of, docs, causal, grads):
        valid = docs == doc_row[:, COLUMN + rows.start : COLUMN + rows.stop]
        if causal:
            row = lax.broadcasted_iota(jnp.int32, valid.shape, 0)
            valid = valid & (row <= lax.broadcasted_iota(jnp.int32, valid.shape, 1) + rows.start)
        for h in range(2):
            span = slice(h * HEAD, (h + 1) * HEAD)
            asked, upstream = query[rows, span], do[rows, span]
            scores = dot(keys_of[:, :HEAD], asked, NT) * SCALE
            probs = jnp.where(valid, jnp.exp(scores), 0.0) * back[h : h + 1, rows]
            d_probs = dot(keys_of[:, HEAD:], upstream, NT)
            d_scores = (probs * (d_probs - delta[h : h + 1, rows])).astype(BF)
            grads[:, :HEAD] += dot(d_scores, asked, NN) * SCALE
            grads[:, HEAD:] += dot(probs.astype(BF), upstream, NN)
            d_asked = dot(d_scores, keys_of[:, :HEAD], TN) * SCALE
            dq[rows, span] += d_asked

    back_kv = []
    for j in range(4):
        end, keys = (j + 1) * BLOCK, slice(j * BLOCK, (j + 1) * BLOCK)
        attend_back(slice(0, end), before.at[keys], doc_col[keys, 0:1], False, dkv.at[keys])
        d_before[keys, :] = dkv[keys, :].astype(BF)
        back_kv.append(w.push(d_before.at[keys], came.at[keys], spot.column(-1)))
    go(fold_out)
    lax.fori_loop(0, 8, tile_out, 0)
    load_n1 = w.local(normed1, db)
    for i in range(4):
        end = (i + 1) * BLOCK
        attend_back(
            slice(i * BLOCK, end), kv.at[0:end], doc_col[COLUMN : COLUMN + end, 0:1], True, dkv.at[COLUMN : COLUMN + end]
        )
        if i == 1:
            go(fold_out, share_out)
    for copy in back_kv:
        copy.wait_recv()
    go(sum_in)

    def project_back(i, _):
        rows = pl.ds(pl.multiple_of(i * BLOCK, BLOCK), BLOCK)
        own = pl.ds(pl.multiple_of(i * BLOCK + COLUMN, BLOCK), BLOCK)
        for h, scale in enumerate((q_gain, q_gain, k_gain)):
            span = slice(h * HEAD, (h + 1) * HEAD)
            if h < 2:
                grad = dq[rows, span]
            else:
                grad = dkv[own, :HEAD] + came[rows, :HEAD].astype(F32)
            grad = grad * cosine[rows, :] - turn_half(grad) * sine[rows, :]
            unit, root = rms_of(raw[rows, span])
            scaled = grad * scale[...].astype(F32)
            back = root * (scaled - unit * jnp.mean(scaled * unit, axis=-1, keepdims=True))
            d_raw[rows, span] = back.astype(BF)
            at = 32 + h // 2
            vector[at : at + 1, :] += jnp.sum(grad * unit, axis=0, keepdims=True)
        d_raw[rows, 3 * HEAD :] = (dkv[own, HEAD:] + came[rows, HEAD:].astype(F32)).astype(BF)
        return 0

    def norm_of(core):
        def one(lo, _):
            rows = pl.ds(pl.multiple_of((core * 2 + lo) * BLOCK, BLOCK), BLOCK)
            value = dot(d_raw[rows, :], w_a[:, :512], NT)
            part[core, lo] = value.astype(BF).reshape(2, 128, WIDTH)
            return 0

        lax.fori_loop(0, 2, one, 0)

    def finish(total):
        load_tok.wait()

        def body(rows):
            rms_back(total, base, gain.at[0:1], rows, dmid, low, gain_grad)

        by_rows(128, 16, body)

    lax.fori_loop(0, 4, project_back, 0)
    load_n1.wait()
    sum_out = plane_sum(w, spot, g_out, (b0, b1, b2, b3, b4, b5), resident=True)
    fold = column_sum(w, spot, part, (None, got, in1, in2), finish, resident=True)
    norm_of(1 - spot.c)
    go(fold)
    norm_of(spot.c)
    go(fold)
    lax.fori_loop(0, 8, tile, 0)
    go(sum_out, fold, sum_in, sum_out, fold)
    share_tok = pair_share(w, spot, low, g_tok)
    vector[16:32, :] = g_mlp[...]
    for i in range(16):
        vector[i : i + 1, :] = gain_grad[:, i * 128 : (i + 1) * 128]
    share_in = mate_share(w, spot, a8, ((o_gate, 0, 768), (o_up, 768, 768)))
    everywhere = sum_everywhere(w, spot, vector, pair, lines)
    go(share_tok, sum_in, everywhere, sum_out, everywhere, everywhere, sum_in, sum_out, sum_in, share_in, everywhere, everywhere, sum_out, sum_out)
    share_grads = mate_share(
        w, spot, b5, ((o_q, 0, 256), (o_k, 256, 128), (o_v, 384, 128), (o_out, 512, 256))
    )
    go(share_grads, everywhere, everywhere, share_out, share_down, everywhere, everywhere, share_in, share_tok, share_grads)
    for part_left in (sum_in, fold_out, share_out, share_down, fold, sum_out, everywhere, share_in, share_grads, share_tok):
        assert part_left.gi_frame is None
    w.drain()


def close_call(*args):
    def shape(*sizes, kind=BF):
        return jax.ShapeDtypeStruct(sizes, kind)

    return pl.pallas_call(
        close_kernel,
        out_shape=(
            shape(2, 128, WIDTH),
            shape(2, 128, WIDTH),
            shape(64, 3072),
            shape(64, 3072),
            shape(64, 3072),
            shape(64, 1024),
            shape(64, 512),
            shape(64, 512),
            shape(64, 1024),
            shape(40, 128, kind=F32),
        ),
        in_specs=[HBM] * 10 + [VMEM, HBM, HBM, VMEM, VMEM] + [HBM, VMEM, HBM, VMEM, VMEM, HBM, VMEM, HBM, VMEM],
        out_specs=(HBM,) * 9 + (VMEM,),
        scratch_shapes=[
            pltpu.VMEM((WIDTH, 256), BF),
            pltpu.VMEM((WIDTH, 640), BF),
            pltpu.VMEM((COLUMN, 256), BF),
            pltpu.VMEM((COLUMN, 256), BF),
            pltpu.VMEM((COLUMN, 256), BF),
            pltpu.VMEM((COLUMN, 256), BF),
            pltpu.VMEM((COLUMN, 512), F32),
            pltpu.VMEM((COLUMN, HEAD), F32),
            pltpu.VMEM((COLUMN, HEAD), F32),
            pltpu.VMEM((2 * COLUMN, 128), F32),
            pltpu.VMEM((COLUMN, 2), F32),
            pltpu.VMEM((COLUMN, WIDTH), BF),
            pltpu.VMEM((COLUMN, 256), BF),
            pltpu.VMEM((COLUMN, 256), F32),
            pltpu.VMEM((2 * COLUMN, 256), F32),
            pltpu.VMEM((COLUMN, 256), BF),
            pltpu.VMEM((COLUMN, 256), BF),
            pltpu.VMEM((COLUMN, 512), BF),
            pltpu.VMEM((2, 2, 2, 128, WIDTH), BF),
            pltpu.VMEM((4, 4, 128, 768), BF),
        ]
        + column_sum_scratch()[1:]
        + column_sum_scratch()
        + [
            pltpu.VMEM((128, WIDTH), BF),
            pltpu.VMEM((128, WIDTH), BF),
            pltpu.VMEM((1, WIDTH), F32),
            pltpu.VMEM((128, WIDTH), BF),
            pltpu.VMEM((2, COLUMN), F32),
            pltpu.VMEM((2, COLUMN), F32),
        ]
        + plane_sum_scratch(1536, False)
        + plane_sum_scratch(768, True)
        + [pltpu.VMEM((40, 128), F32), pltpu.VMEM((3, 4, 40, 128), F32)]
        + wires_scratch(120, 50)
        + [pltpu.SemaphoreType.DMA((4,))],
        compiler_params=params(6),
        name="close",
    )(*args)


def finish_kernel(*refs):
    ins, outs = refs[:10], refs[10:]
    vector = ins[9]
    outs[0][...] = ins[0][...]
    for source, target in zip(ins[1:9], outs[1:9]):
        target[...] = source[...].astype(F32)
    shard = lax.axis_index("shard")
    for first, target in ((0, outs[9]), (16, outs[10])):
        line = vector[pl.ds(first + shard // 2, 1), :]
        target[...] = jnp.where(shard % 2 == 0, line[:, 0:64], line[:, 64:128])
    outs[11][...] = vector[32:33, :]
    outs[12][...] = vector[33:34, :]


def finish_call(out, g_tok, *rest):
    tall = pl.BlockSpec((64, WIDTH), lambda i: (i, 0))
    grads, vector = rest[:-1], rest[-1]
    wide = [pl.BlockSpec((64, g.shape[1] // 4), lambda i: (0, i)) for g in grads]
    tops = [jax.ShapeDtypeStruct((1, n), F32) for n in (64, 64, 128, 128)]
    return pl.pallas_call(
        finish_kernel,
        grid=(4,),
        out_shape=(
            jax.ShapeDtypeStruct(out.shape, BF),
            jax.ShapeDtypeStruct(g_tok.shape, F32),
            *(jax.ShapeDtypeStruct(g.shape, F32) for g in grads),
            *tops,
        ),
        in_specs=[tall, tall] + wide + [VMEM],
        out_specs=[tall, tall] + wide + [VMEM] * 4,
        compiler_params=pltpu.CompilerParams(vmem_limit_bytes=LIMIT),
        name="finish",
    )(out, g_tok, *grads, vector)


def on_device(
    tokens, lengths, attn_norm, w_query, w_key, w_value, w_output, q_gain, k_gain, mlp_norm, w_gate, w_up, w_down, cotangent,
):
    freq = THETA ** (-np.arange(0, HEAD, 2).astype(np.float32) / np.float32(HEAD))
    freq = jnp.asarray(np.concatenate([freq, freq])[None].astype(np.float32))
    both_gains = jnp.tile(jnp.pad(jnp.stack([attn_norm, mlp_norm], axis=1), ((0, 0), (0, 126))), (1, 4))
    (
        normed1, w_a, w_w, w_b, cot, raw, query, kv, before, attended, inverse, middle, normed2, cosine, sine, gains, doc_row, doc_col,
    ) = forward_call(
        tokens, cotangent, w_query, w_key, w_value, w_output.T, both_gains, w_gate, w_up, w_down.T, lengths, freq, q_gain[None], k_gain[None]
    )
    w_a, w_w = w_a.reshape(WIDTH, 640), w_w.reshape(WIDTH, 256)
    d_middle, d_branch, mixed, g_in, g_mlp, both_down = turn_call(
        normed2.reshape(COLUMN, WIDTH),
        cot.reshape(COLUMN, WIDTH),
        w_b,
        middle,
        cotangent.reshape(2, 128, WIDTH),
        gains,
    )
    out, g_tokens, g_gate, g_up, g_down, g_query, g_key, g_value, g_output, sums = close_call(
        d_branch.reshape(COLUMN, WIDTH), w_w, w_a, attended, query, before, kv, raw, cosine, sine, doc_row, doc_col, inverse,
        q_gain[None], k_gain[None], g_in, both_down, mixed, middle, d_middle, tokens.reshape(2, 128, WIDTH), gains,
        normed1, g_mlp.reshape(16, 128),
    )

    (
        out, g_tokens, g_gate, g_up, g_down, g_query, g_key, g_value, g_output, g_attn, g_mlp, g_q_gain, g_k_gain,
    ) = finish_call(
        out.reshape(256, WIDTH), g_tokens.reshape(256, WIDTH), g_gate, g_up, g_down, g_query, g_key, g_value, g_output, sums
    )
    return (
        out, g_tokens, g_attn[0], g_query, g_key, g_value, g_output.T, g_q_gain[0], g_k_gain[0], g_mlp[0], g_gate, g_up, g_down.T,
    )


def solution(mesh):
    rows = P(("shard", "dp"), None)
    down = P("shard", "tensor")
    across = P("tensor", "shard")
    one = P("shard")
    return jax.shard_map(
        on_device,
        mesh=mesh,
        in_specs=(rows, P(), one, down, down, down, across, P(), P(), one, down, down, across, rows),
        out_specs=(rows, rows, one, down, down, down, across, P(), P(), one, down, down, across),
        check_vma=False,
    )
```

```python
import functools

import jax
import jax.numpy as jnp
import numpy as np
from jax import lax
from jax.experimental import pallas as pl
from jax.experimental.pallas import tpu as pltpu
from jax.sharding import PartitionSpec as P

HEAD = 128
EPS = 1e-06
THETA = 1000000.0
SCALE = HEAD ** (-0.5)
WIDTH = 2048
COLUMN = 1024
MESH = pl.DeviceIdType.MESH
BF = jnp.bfloat16
F32 = jnp.float32
HBM = pl.BlockSpec(memory_space=pl.ANY)
VMEM = pl.BlockSpec(memory_space=pltpu.VMEM)
LIMIT = 60 * 2**20


class Spot:
    def __init__(self):
        shard = lax.axis_index("shard")
        self.lo = lax.axis_index("dp")
        self.hi = lax.axis_index("tensor")
        self.x = self.hi * 2 + self.lo
        self.y = shard // 8
        self.z = (shard // 2) % 4
        self.c = shard % 2

    def dev(self, dx=0, dy=0, dz=0, other=False):
        x = (self.x + dx) % 4
        y = (self.y + dy) % 4
        z = (self.z + dz) % 4
        c = 1 - self.c if other else self.c
        return ((y * 4 + z) * 2 + c, x % 2, x // 2)

    def dp_mate(self):
        return ((self.y * 4 + self.z) * 2 + self.c, 1 - self.lo, self.hi)

    def column(self, step):
        flat = (self.y * 4 + self.z + step + 16) % 16
        return (flat * 2 + self.c, self.lo, self.hi)


def greet(devices):
    barrier = pltpu.get_barrier_semaphore()
    for device in devices:
        pl.semaphore_signal(barrier, inc=1, device_id=device, device_id_type=MESH)
    pl.semaphore_wait(barrier, len(devices))


class Wires:
    def __init__(self, send, recv, local):
        self.send, self.recv, self.here = send, recv, local
        self.count, self.near = 0, 0
        self.sent = []

    def push(self, src, dst, device):
        i = self.count
        self.count += 1
        copy = pltpu.make_async_remote_copy(
            src_ref=src,
            dst_ref=dst,
            send_sem=self.send.at[i],
            recv_sem=self.recv.at[i],
            device_id=device,
            device_id_type=MESH,
        )
        copy.start()
        self.sent.append(copy)
        return copy

    def local(self, src, dst):
        copy = pltpu.make_async_copy(src, dst, self.here.at[self.near])
        self.near += 1
        copy.start()
        return copy

    def sent_now(self, copy):
        copy.wait_send()
        self.sent = [other for other in self.sent if other is not copy]

    def drain(self):
        assert self.count <= self.send.shape[0] and self.near <= self.here.shape[0]
        for copy in self.sent:
            copy.wait_send()


def wires_scratch(remote, local):
    return [
        pltpu.SemaphoreType.DMA((remote,)),
        pltpu.SemaphoreType.DMA((remote,)),
        pltpu.SemaphoreType.DMA((max(local, 1),)),
    ]


def by_rows(count, step, body):
    def run(i, _):
        body(pl.ds(pl.multiple_of(i * step, step), step))
        return 0

    lax.fori_loop(0, count // step, run, 0)


def add_into(dst, *sources):
    def body(rows):
        total = dst[rows, :].astype(F32)
        for source in sources:
            total = total + source[rows, :].astype(F32)
        dst[rows, :] = total.astype(dst.dtype)

    by_rows(dst.shape[0], 16, body)


def run_all(*parts):
    parts = list(parts)
    while parts:
        for part in list(parts):
            if next(part, StopIteration) is StopIteration:
                parts.remove(part)


def plane_gather(w, spot, pieces, out, eager=False):
    y, z, c = spot.y, spot.z, spot.c
    rows = pl.ds(pl.multiple_of(c * 64, 64), 64)
    swaps, owns = [], []
    for source, size, low in pieces:
        theirs = pl.ds(pl.multiple_of((spot.lo * 2 + 1 - c) * size, size), size)
        mine = pl.ds(pl.multiple_of((spot.lo * 2 + c) * size, size), size)
        at = out.at[y, z, rows, pl.ds(low, size)]
        swaps.append(w.push(source.at[:, theirs], at, spot.dev(other=True)))
        owns.append(w.local(source.at[:, mine], at))
    yield
    for swap, own in zip(swaps, owns):
        swap.wait_recv()
        own.wait()
    ym, yp, zm, zp = (y + 3) % 4, (y + 1) % 4, (z + 3) % 4, (z + 1) % 4
    to_zp, to_zm = spot.dev(dz=1), spot.dev(dz=-1)
    to_yp, to_ym = spot.dev(dy=1), spot.dev(dy=-1)
    a, b = pl.ds(0, 64), pl.ds(64, 64)
    mine_a, mine_b = out.at[y, z, a], out.at[y, z, b]
    a1 = w.push(mine_a, mine_a, to_zp)
    a2 = w.push(mine_a, mine_a, to_zm)
    b1 = w.push(mine_b, mine_b, to_yp)
    b2 = w.push(mine_b, mine_b, to_ym)
    yield
    a1.wait_recv()
    part = out.at[y, zm, pl.ds(0, 32)]
    a3 = w.push(part, part, to_zp)
    b1.wait_recv()
    part = out.at[ym, z, pl.ds(64, 32)]
    b3 = w.push(part, part, to_yp)
    a2.wait_recv()
    part = out.at[y, zp, pl.ds(32, 32)]
    a4 = w.push(part, part, to_zm)
    b2.wait_recv()
    part = out.at[yp, z, pl.ds(96, 32)]
    b4 = w.push(part, part, to_ym)
    lines = ([], [], [], [])

    def pass_on(in_a, in_b):
        for chunk, near, one, two in ((in_a, 0, to_yp, to_ym), (in_b, 2, to_zp, to_zm)):
            lines[near].append(w.push(chunk, chunk, one))
            lines[near + 1].append(w.push(chunk, chunk, two))

    if eager:
        pass_on(mine_a, mine_b)
        pass_on(out.at[y, zm, a], out.at[ym, z, b])
        pass_on(out.at[y, zp, a], out.at[yp, z, b])
    yield
    for copy in (a3, a4, b3, b4):
        copy.wait_recv()
    if eager:
        pass_on(out.at[y, (z + 2) % 4, a], out.at[(y + 2) % 4, z, b])
    else:
        pass_on(out.at[y, :, a], out.at[:, z, b])
    yield

    def arrived(line):
        for copy in lines[line]:
            copy.wait_recv()

    arrived(0)
    part = out.at[ym, pl.ds(0, 2), a]
    a7 = w.push(part, part, to_yp)
    arrived(2)
    part = out.at[pl.ds(0, 2), zm, b]
    b7 = w.push(part, part, to_zp)
    arrived(1)
    part = out.at[yp, pl.ds(2, 2), a]
    a8 = w.push(part, part, to_ym)
    arrived(3)
    part = out.at[pl.ds(2, 2), zp, b]
    b8 = w.push(part, part, to_zm)
    yield
    for copy in (a7, b7, a8, b8):
        copy.wait_recv()


def plane_sum_scratch(columns, resident):
    kept = [
        pltpu.VMEM((2, 2, 64, columns), BF),
        pltpu.VMEM((2, 2, 64, columns), BF),
        pltpu.VMEM((2, 4, 64, columns), BF),
    ]
    return ([] if resident else kept) + [
        pltpu.VMEM((2, 2, 2, 64, columns), BF),
        pltpu.VMEM((2, 2, 4, 64, columns), BF),
        pltpu.VMEM((2, 2, 32, columns), BF),
        pltpu.VMEM((2, 2, 64, columns), BF),
        pltpu.VMEM((128, columns), BF),
        pltpu.VMEM((2, 64, columns), BF),
    ]


def plane_sum(w, spot, part, scratch, resident=False):
    in1, in2, in3, in4, full, both = scratch[-6:]
    c = spot.c
    rows = (pl.ds(0, 64), pl.ds(64, 64))
    lanes = ((spot.y, spot.z), (spot.z, spot.y))
    steps = (("dy", "dz"), ("dz", "dy"))

    def view(h, k, low, size):
        at = (lanes[h][0] + k) % 4
        if h == 0:
            return part.at[at, pl.ds(low, size), rows[h]]
        return part.at[pl.ds(low, size), at, rows[h]]

    def held(h, j):
        if not resident:
            return scratch[2].at[h, j]
        if h == 0:
            return part.at[spot.y, j, rows[h]]
        return part.at[j, spot.z, rows[h]]

    def to(h, stage, step):
        return spot.dev(**{steps[h][stage]: step})

    loads, first, second, early = [], [], [], []
    for h in range(2):
        first.append(
            (
                w.push(view(h, 2, 0, 2), in1.at[h, 0], to(h, 0, 1)),
                w.push(view(h, 2, 2, 2), in1.at[h, 1], to(h, 0, -1)),
            )
        )
    for h in range(2):
        if resident:
            plus, minus = view(h, 1, 0, 2), view(h, 3, 2, 2)
            loads.append((plus, minus))
            continue
        plus, minus = scratch[0].at[h], scratch[1].at[h]
        loads.append(
            (
                plus,
                minus,
                w.local(view(h, 1, 0, 2), plus),
                w.local(view(h, 3, 2, 2), minus),
                w.local(view(h, 0, 0, 4), scratch[2].at[h]),
            )
        )
    yield
    for h in range(2):
        plus, minus = loads[h][:2]
        if not resident:
            loads[h][2].wait()
        first[h][0].wait_recv()
        for j in range(2):
            add_into(plus.at[j], in1.at[h, 0, j])
        one = w.push(plus, in2.at[h, 0, pl.ds(0, 2)], to(h, 0, 1))
        if not resident:
            loads[h][3].wait()
        first[h][1].wait_recv()
        for j in range(2):
            add_into(minus.at[j], in1.at[h, 1, j])
        two = w.push(minus, in2.at[h, 1, pl.ds(2, 2)], to(h, 0, -1))
        second.append((one, two))
    for h in range(2):
        early.append(
            (
                w.push(view(h, 1, 2, 2), in2.at[h, 0, pl.ds(2, 2)], to(h, 0, 1)),
                w.push(view(h, 3, 0, 2), in2.at[h, 1, pl.ds(0, 2)], to(h, 0, -1)),
            )
        )
    yield
    third, early3 = [], []
    for h in range(2):
        if not resident:
            loads[h][4].wait()
        for copy in early[h] + second[h]:
            copy.wait_recv()
        at = [(lanes[h][1] + k) % 4 for k in range(4)]
        add_into(held(h, at[2]), in2.at[h, 0, at[2]], in2.at[h, 1, at[2]])
        far = held(h, at[2])
        third.append(
            (
                w.push(far.at[pl.ds(0, 32)], in3.at[h, 0], to(h, 1, 1)),
                w.push(far.at[pl.ds(32, 32)], in3.at[h, 1], to(h, 1, -1)),
            )
        )
        add_into(held(h, at[1]), in2.at[h, 0, at[1]], in2.at[h, 1, at[1]])
        one = w.push(held(h, at[1]).at[pl.ds(32, 32)], in4.at[h, 0, pl.ds(32, 32)], to(h, 1, 1))
        add_into(held(h, at[3]), in2.at[h, 0, at[3]], in2.at[h, 1, at[3]])
        two = w.push(held(h, at[3]).at[pl.ds(0, 32)], in4.at[h, 1, pl.ds(0, 32)], to(h, 1, -1))
        early3.append((one, two))
        add_into(held(h, at[0]), in2.at[h, 0, at[0]], in2.at[h, 1, at[0]])
    yield
    fourth = []
    for h in range(2):
        at = [(lanes[h][1] + k) % 4 for k in range(4)]
        third[h][0].wait_recv()
        piece = held(h, at[1]).at[pl.ds(0, 32)]
        add_into(piece, in3.at[h, 0])
        one = w.push(piece, in4.at[h, 0, pl.ds(0, 32)], to(h, 1, 1))
        third[h][1].wait_recv()
        piece = held(h, at[3]).at[pl.ds(32, 32)]
        add_into(piece, in3.at[h, 1])
        two = w.push(piece, in4.at[h, 1, pl.ds(32, 32)], to(h, 1, -1))
        fourth.append((one, two))
    yield
    for h in range(2):
        for copy in early3[h] + fourth[h]:
            copy.wait_recv()
        mine = held(h, lanes[h][1])
        target = full.at[rows[h]]

        def body(r):
            total = mine[r, :].astype(F32) + in4[h, 0, r, :].astype(F32)
            target[r, :] = (total + in4[h, 1, r, :].astype(F32)).astype(BF)

        by_rows(64, 16, body)
    theirs = full.at[pl.ds(pl.multiple_of((1 - c) * 64, 64), 64)]
    mine = full.at[pl.ds(pl.multiple_of(c * 64, 64), 64)]
    swap = w.push(theirs, both.at[c], spot.dev(other=True))

    def keep(r):
        both[c, r, :] = mine[r, :]

    by_rows(64, 16, keep)
    yield
    swap.wait_recv()


def mate_share(w, spot, both, outs):
    copies = []
    for out, low, size in outs:
        for core in range(2):
            piece = both.at[core, :, pl.ds(low, size)]
            at = pl.ds(pl.multiple_of((spot.lo * 2 + core) * size, size), size)
            copies.append((w.local(piece, out.at[:, at]), w.push(piece, out.at[:, at], spot.dp_mate())))
    yield
    for near, far in copies:
        near.wait()
        far.wait_recv()


def column_sum_scratch():
    return [
        pltpu.VMEM((4, 128, WIDTH), BF),
        pltpu.VMEM((4, 128, WIDTH), BF),
        pltpu.VMEM((2, 64, WIDTH), BF),
        pltpu.VMEM((2, 128, WIDTH), BF),
    ]


def column_sum(w, spot, part, scratch, finish, resident=False):
    own, got, in1, in2 = scratch
    x, c = spot.x, spot.c
    right, left = spot.dev(dx=1), spot.dev(dx=-1)
    places = [((x + k) % 4 % 2, (x + k) % 4 // 2) for k in range(4)]
    swaps, loads = {}, {}
    for k in (2, 1, 3, 0):
        swaps[k] = w.push(part.at[1 - c, places[k][0], places[k][1]], got.at[k], spot.dev(other=True))
    if resident:
        own = [part.at[c, lo, hi] for lo, hi in places]
    else:
        for k in (2, 1, 3, 0):
            loads[k] = w.local(part.at[c, places[k][0], places[k][1]], own.at[k])
        own = [own.at[k] for k in range(4)]
    yield

    def merge(k):
        if not resident:
            loads[k].wait()
        swaps[k].wait_recv()
        add_into(own[k], got.at[k])

    low, high = pl.ds(0, 64), pl.ds(64, 64)
    merge(2)
    far1 = w.push(own[2].at[low], in1.at[0], right)
    far2 = w.push(own[2].at[high], in1.at[1], left)
    merge(1)
    one = w.push(own[1].at[high], in2.at[0, high], right)
    merge(3)
    two = w.push(own[3].at[low], in2.at[1, low], left)
    merge(0)
    yield
    far1.wait_recv()
    add_into(own[1].at[low], in1.at[0])
    three = w.push(own[1].at[low], in2.at[0, low], right)
    far2.wait_recv()
    add_into(own[3].at[high], in1.at[1])
    four = w.push(own[3].at[high], in2.at[1, high], left)
    yield
    for copy in (one, two, three, four):
        copy.wait_recv()

    def total(rows):
        return own[0][rows, :].astype(F32) + in2[0, rows, :].astype(F32) + in2[1, rows, :].astype(F32)

    finish(total)


def column_share(w, spot, mine, out):
    x, c = spot.x, spot.c
    right, left, mate = spot.dev(dx=1), spot.dev(dx=-1), spot.dev(other=True)

    def slot(k):
        at = (x + k + 4) % 4
        return out.at[c, at % 2, at // 2]

    low, high = pl.ds(0, 64), pl.ds(64, 64)
    own = w.local(mine, slot(0))
    a = w.push(mine.at[low], slot(0).at[low], right)
    b = w.push(mine.at[high], slot(0).at[high], left)
    d = w.push(mine, slot(0), mate)
    a2 = w.push(mine.at[high], slot(0).at[high], right)
    b2 = w.push(mine.at[low], slot(0).at[low], left)
    yield
    a.wait_recv()
    e = w.push(slot(-1).at[low], slot(-1).at[low], right)
    last = [w.push(slot(-1).at[low], slot(-1).at[low], mate)]
    b.wait_recv()
    g = w.push(slot(1).at[high], slot(1).at[high], left)
    last.append(w.push(slot(1).at[high], slot(1).at[high], mate))
    yield
    a2.wait_recv()
    last.append(w.push(slot(-1).at[high], slot(-1).at[high], mate))
    b2.wait_recv()
    last.append(w.push(slot(1).at[low], slot(1).at[low], mate))
    e.wait_recv()
    last.append(w.push(slot(2).at[low], slot(2).at[low], mate))
    g.wait_recv()
    last.append(w.push(slot(2).at[high], slot(2).at[high], mate))
    yield
    own.wait()
    for copy in [d] + last:
        copy.wait_recv()


def token_share(w, spot, block, out):
    own_at, far_at = spot.c * 2 + spot.lo, spot.c * 2 + 1 - spot.lo
    right, left, mate = spot.dev(dx=1), spot.dev(dx=-1), spot.dev(other=True)
    low, high = pl.ds(0, 128), pl.ds(128, 128)
    own = w.local(block, out.at[own_at])
    a = w.push(block.at[low], out.at[own_at, low], right)
    b = w.push(block.at[high], out.at[own_at, high], left)
    d = w.push(block, out.at[own_at], mate)
    yield
    a.wait_recv()
    part = out.at[far_at, low]
    e = w.push(part, part, mate)
    b.wait_recv()
    part = out.at[far_at, high]
    f = w.push(part, part, mate)
    yield
    own.wait()
    for copy in (d, e, f):
        copy.wait_recv()


def pair_share(w, spot, mine, out):
    own = w.local(mine, out.at[spot.hi])
    a = w.push(mine, out.at[spot.hi], spot.dev(dx=2))
    yield
    own.wait()
    a.wait_recv()


def neighbours(spot, x=False, yz=False, core=False, pair=False, far=False):
    found = []
    if x:
        found += [spot.dev(dx=1), spot.dev(dx=-1)]
    if yz:
        found += [spot.dev(dy=1), spot.dev(dy=-1), spot.dev(dz=1), spot.dev(dz=-1)]
    if core:
        found += [spot.dev(other=True)]
    if pair:
        found += [spot.dev(dx=2)]
    if far:
        found += [spot.dev(dy=2), spot.dev(dz=2)]
    return found


BLOCK = 256
SPAN = COLUMN + BLOCK
NT = (((1,), (1,)), ((), ()))
TN = (((0,), (0,)), ((), ()))
NN = (((1,), (0,)), ((), ()))


def dot(a, b, dims):
    return lax.dot_general(a, b, dims, preferred_element_type=F32)


def rms_of(rows):
    inverse = lax.rsqrt(jnp.mean(rows * rows, axis=-1, keepdims=True) + EPS)
    return rows * inverse, inverse


def turn_half(rows):
    half = HEAD // 2
    return jnp.concatenate([-rows[:, half:], rows[:, :half]], axis=-1)


def params(collective_id):
    return pltpu.CompilerParams(
        collective_id=collective_id, has_side_effects=True, vmem_limit_bytes=LIMIT
    )


def own_block(ref, spot):
    return ref.at[spot.c, spot.lo, spot.hi]


def place_rows(spot, lengths, freq, doc_row, doc_col, cosine, sine):
    first = (spot.y * 4 + spot.z - 1) * COLUMN
    rows = lax.broadcasted_iota(jnp.int32, (16, 128), 0) * 128 + first
    rows = rows + lax.broadcasted_iota(jnp.int32, (16, 128), 1)
    document = jnp.zeros((16, 128), jnp.int32)
    start = jnp.zeros((16, 128), jnp.int32)
    bound = jnp.int32(0)
    for d in range(lengths.shape[1]):
        bound = bound + lengths[0, d]
        passed = rows >= bound
        document = document + passed.astype(jnp.int32)
        start = jnp.where(passed, bound, start)
    document = jnp.where(rows >= 0, document, -1).astype(F32)
    place = (rows - start).astype(F32)
    for g in range(16):
        line = document[g : g + 1, :]
        at = slice(g * 128, (g + 1) * 128)
        doc_row[:, at] = line
        doc_col[at, :] = jnp.transpose(jnp.broadcast_to(line, (128, 128)))
        if g >= 8:
            down = jnp.transpose(jnp.broadcast_to(place[g : g + 1, :], (128, 128)))
            angles = down * freq[...]
            at = slice((g - 8) * 128, (g - 7) * 128)
            cosine[at, :] = jnp.cos(angles)
            sine[at, :] = jnp.sin(angles)


def turned_head(raw, scale, cosine, sine):
    unit = rms_of(raw)[0] * scale
    return (unit * cosine + turn_half(unit) * sine).astype(BF)


def forward_kernel(
    tok, cot, x_q, x_k, x_v, x_o, x_gains, x_gate, x_up, x_down, lengths, freq, q_gain, k_gain,
    normed1, o_a, o_w, w_b, cot_all, o_raw, o_query, o_kv, o_before, o_attended, o_inverse, mid, normed2, o_cosine, o_sine, gains, doc_row, o_docs,
    w_a, w_w, raw, query, kv, before, attended, inverse, cosine, sine, doc_col,
    tok_all, low1, roots, top, total, branch, got, in1, in2, low, send, recv, here,
):
    spot = Spot()
    greet(neighbours(spot, x=True, yz=True, core=True) + [spot.column(1), spot.column(-1)])
    w = Wires(send, recv, here)
    first_pieces = ((x_q, 256, 0), (x_k, 128, 256), (x_v, 128, 384), (x_gains, 128, 512))
    take_a = plane_gather(w, spot, first_pieces, w_a, eager=True)
    take_w = plane_gather(w, spot, ((x_o, 256, 0),), w_w)
    take_b = plane_gather(w, spot, ((x_gate, 768, 0), (x_up, 768, 768), (x_down, 768, 1536)), w_b)
    take_tok = token_share(w, spot, tok, tok_all)
    take_cot = token_share(w, spot, cot, cot_all)
    keeps = []

    def keep(source, target):
        keeps.append(w.local(source, target))

    def go(*parts):
        for part in parts:
            next(part, None)

    go(take_a, take_tok, take_a, take_w, take_b)
    place_rows(spot, lengths, freq, doc_row, doc_col, cosine, sine)
    keep(cosine, o_cosine)
    keep(sine, o_sine)
    keep(doc_col, o_docs)
    go(take_a, take_a, take_w, take_tok, take_a, take_tok, take_w)

    def roots_of(i, _):
        rows = pl.ds(pl.multiple_of(i * 32, 32), 32)
        values = tok_all[i // 8, pl.ds(pl.multiple_of(i % 8 * 32, 32), 32), :].astype(F32)
        roots[rows, :] = lax.rsqrt(jnp.mean(values * values, axis=-1, keepdims=True) + EPS)
        return 0

    lax.fori_loop(0, 32, roots_of, 0)
    go(take_a, take_cot, take_b, take_w)
    keep(w_a, o_a)
    for i in range(16):
        block = jnp.transpose(w_a[i // 4, i % 4, :, 512:640].astype(F32))
        gains[:, i * 128 : (i + 1) * 128] = block[0:2, :]

    def norm_rows(i, _):
        rows = pl.ds(pl.multiple_of(i * 32, 32), 32)
        values = tok_all[i // 8, pl.ds(pl.multiple_of(i % 8 * 32, 32), 32), :].astype(F32)
        low1[rows, :] = (values * roots[rows, :] * gains[0:1, :]).astype(BF)
        return 0

    lax.fori_loop(0, 32, norm_rows, 0)
    keep(low1, normed1)

    def project_kv(i, _):
        rows = pl.ds(pl.multiple_of(i * BLOCK, BLOCK), BLOCK)
        out = dot(low1[rows, :], w_a[:, :, :, 256:512].reshape(WIDTH, 256), NN)
        raw[rows, 256:512] = out
        kv[rows, :HEAD] = turned_head(out[:, :HEAD], k_gain[...].astype(F32), cosine[rows, :], sine[rows, :])
        kv[rows, HEAD:] = out[:, HEAD:].astype(BF)
        return 0

    def project_q(i, _):
        rows = pl.ds(pl.multiple_of(i * BLOCK, BLOCK), BLOCK)
        out = dot(low1[rows, :], w_a[:, :, :, 0:256].reshape(WIDTH, 256), NN)
        raw[rows, 0:256] = out
        for h in range(2):
            span = slice(h * HEAD, (h + 1) * HEAD)
            query[rows, span] = turned_head(out[:, span], q_gain[...].astype(F32), cosine[rows, :], sine[rows, :])
        return 0

    pass_kv = []
    for i in range(4):
        project_kv(i, 0)
        rows = pl.ds(i * BLOCK, BLOCK)
        pass_kv.append(w.push(kv.at[rows], before.at[rows], spot.column(1)))
    keep(kv, o_kv)
    go(take_w, take_b)
    lax.fori_loop(0, 4, project_q, 0)
    keep(raw, o_raw)
    keep(query, o_query)

    def weights_of(i, h, keys, docs, causal):
        rows = slice(i * BLOCK, (i + 1) * BLOCK)
        scores = dot(query[rows, h * HEAD : (h + 1) * HEAD], keys, NT) * SCALE
        valid = doc_col[COLUMN + i * BLOCK : COLUMN + (i + 1) * BLOCK, 0:1] == docs
        if causal:
            row = lax.broadcasted_iota(jnp.int32, scores.shape, 0) + i * BLOCK
            valid = valid & (lax.broadcasted_iota(jnp.int32, scores.shape, 1) <= row)
        return jnp.where(valid, jnp.exp(scores), 0.0)

    for i in range(4):
        rows, end = slice(i * BLOCK, (i + 1) * BLOCK), (i + 1) * BLOCK
        for h in range(2):
            weight = weights_of(i, h, kv[0:end, :HEAD], doc_row[:, COLUMN : COLUMN + end], True)
            total[rows, h : h + 1] = jnp.sum(weight, axis=-1, keepdims=True)
            top[rows, h * HEAD : (h + 1) * HEAD] = dot(weight.astype(BF), kv[0:end, HEAD:], NN)
    for copy in pass_kv:
        copy.wait_recv()
    go(take_cot)
    keep(before, o_before)
    go(take_w, take_b)
    keep(w_w, o_w)
    for i in range(4):
        rows, low_key = slice(i * BLOCK, (i + 1) * BLOCK), i * BLOCK
        for h in range(2):
            span = slice(h * HEAD, (h + 1) * HEAD)
            weight = weights_of(i, h, before[low_key:, :HEAD], doc_row[:, low_key:COLUMN], False)
            back = 1.0 / (total[rows, h : h + 1] + jnp.sum(weight, axis=-1, keepdims=True))
            inverse[rows, h : h + 1] = back
            attended[rows, span] = ((top[rows, span] + dot(weight.astype(BF), before[low_key:, HEAD:], NN)) * back).astype(BF)
    keep(attended, o_attended)
    keep(inverse, o_inverse)

    def branch_of(core):
        def one(lo, _):
            rows = pl.ds(pl.multiple_of((core * 2 + lo) * BLOCK, BLOCK), BLOCK)
            out = dot(attended[rows, :], w_w[...].reshape(WIDTH, 256), NT)
            branch[core, lo] = out.astype(BF).reshape(2, 128, WIDTH)
            return 0

        lax.fori_loop(0, 2, one, 0)

    def finish(add):
        def body(rows):
            base = tok[pl.ds(pl.multiple_of(spot.hi * 128 + rows.start, 16), 16), :].astype(F32)
            middle = base + add(rows)
            mid[rows, :] = middle
            root = lax.rsqrt(jnp.mean(middle * middle, axis=-1, keepdims=True) + EPS)
            low[rows, :] = (middle * root * gains[1:2, :]).astype(BF)

        by_rows(128, 16, body)

    branch_of(1 - spot.c)
    fold = column_sum(w, spot, branch, (None, got, in1, in2), finish, resident=True)
    go(fold)
    branch_of(spot.c)
    go(fold, fold, fold, take_cot)
    share = column_share(w, spot, low, normed2)
    go(share, take_b, share, share, take_b, share)
    assert all(g.gi_frame is None for g in (take_a, take_w, take_b, take_tok, take_cot, fold, share))
    for copy in keeps:
        copy.wait()
    w.drain()


def forward_call(*args):
    def shape(*sizes, kind=BF):
        return jax.ShapeDtypeStruct(sizes, kind)

    kept = (
        shape(4, 4, 128, 640),
        shape(4, 4, 128, 256),
        shape(COLUMN, 512, kind=F32),
        shape(COLUMN, 256),
        shape(COLUMN, 256),
        shape(COLUMN, 256),
        shape(COLUMN, 256),
        shape(COLUMN, 2, kind=F32),
        shape(COLUMN, HEAD, kind=F32),
        shape(COLUMN, HEAD, kind=F32),
        shape(2 * COLUMN, 128, kind=F32),
    )
    outs = (
        (shape(COLUMN, WIDTH), HBM),
        (kept[0], HBM),
        (kept[1], HBM),
        (shape(4, 4, 128, 2304), HBM),
        (shape(4, 256, WIDTH), HBM),
        *((k, HBM) for k in kept[2:8]),
        (shape(128, WIDTH, kind=F32), VMEM),
        (shape(2, 2, 2, 128, WIDTH), HBM),
        (kept[8], HBM),
        (kept[9], HBM),
        (shape(2, WIDTH, kind=F32), VMEM),
        (shape(1, 2 * COLUMN, kind=F32), VMEM),
        (kept[10], HBM),
    )
    return pl.pallas_call(
        forward_kernel,
        out_shape=tuple(o[0] for o in outs),
        in_specs=[VMEM] * 10 + [pl.BlockSpec(memory_space=pltpu.SMEM)] + [VMEM] * 3,
        out_specs=tuple(o[1] for o in outs),
        scratch_shapes=[pltpu.VMEM(o.shape, o.dtype) for o in kept]
        + [
            pltpu.VMEM((4, 256, WIDTH), BF),
            pltpu.VMEM((COLUMN, WIDTH), BF),
            pltpu.VMEM((COLUMN, 1), F32),
            pltpu.VMEM((COLUMN, 256), F32),
            pltpu.VMEM((COLUMN, 2), F32),
            pltpu.VMEM((2, 2, 2, 128, WIDTH), BF),
        ]
        + column_sum_scratch()[1:]
        + [pltpu.VMEM((128, WIDTH), BF)]
        + wires_scratch(112, 36),
        compiler_params=params(1),
        name="forward",
    )(*args)


def rms_back(total, base, gain, rows, extra, out, gain_grad):
    values = base[rows, :].astype(F32)
    inverse = lax.rsqrt(jnp.mean(values * values, axis=-1, keepdims=True) + EPS)
    normed = values * inverse
    grad = total(rows)
    scaled = grad * gain[...]
    back = inverse * (scaled - normed * jnp.mean(scaled * normed, axis=-1, keepdims=True))
    gain_grad[...] += jnp.sum(grad * normed, axis=0, keepdims=True)
    out[rows, :] = (extra[rows, :].astype(F32) + back).astype(out.dtype)


def turn_kernel(
    normed, cot, w_b, mid, cot_own, gain, dmid, d_branch, mixed, g_in, gain_grad, both_out,
    nv, cv, wv, hidden, d_both, part, g_down, g_part, mixed_part, both_n, both_c, both_d, got, in1, in2, low, top,
    p0, p1, p2, p3, p4, p5, send, recv, here, tiles,
):
    spot = Spot()
    w = Wires(send, recv, here)

    def two(k):
        at = (spot.x + k) % 4
        lo, hi = at % 2, at // 2
        theirs = pl.ds(pl.multiple_of(((1 - spot.c) * 2 + lo) * 256 + hi * 128, 128), 128)
        mine = pl.ds(pl.multiple_of((spot.c * 2 + lo) * 256 + hi * 128, 128), 128)
        return lo, hi, theirs, mine

    def bring(k):
        _, _, theirs, mine = two(k)
        return [w.local(source.at[r], target.at[r]) for source, target in ((normed, nv), (cot, cv)) for r in (theirs, mine)]

    def bring_weights(j):
        columns = [pl.ds(j * 256 + low_column, 256) for low_column in (0, 768, 1536)]
        return [w.local(w_b.at[:, :, :, at], wv.at[:, :, :, at]) for at in columns]

    rows_in, weights_in = {2: bring(2)}, [bring_weights(0)]
    greet(neighbours(spot, x=True, yz=True, core=True))
    weights_in += [bring_weights(1), bring_weights(2)]
    for k in (1, 3, 0):
        rows_in[k] = bring(k)
    load = w.local(cot_own.at[spot.hi], top)
    gain_grad[...] = jnp.zeros_like(gain_grad)

    def weight(low_column, size):
        return wv[:, :, :, low_column : low_column + size].reshape(WIDTH, size)

    def units(k):
        _, _, theirs, mine = two(k)
        for copy in rows_in[k]:
            copy.wait()
        both_n[0:128, :] = nv[theirs, :]
        both_n[128:, :] = nv[mine, :]
        both_c[0:128, :] = cv[theirs, :]
        both_c[128:, :] = cv[mine, :]

        def one(j, _):
            a = pl.ds(pl.multiple_of(j * 256, 256), 256)
            b = pl.ds(pl.multiple_of(j * 256 + 768, 256), 256)
            d = pl.ds(pl.multiple_of(j * 256 + 1536, 256), 256)
            gate = dot(both_n[...], wv[:, :, :, a].reshape(WIDTH, 256), NN)
            up = dot(both_n[...], wv[:, :, :, b].reshape(WIDTH, 256), NN)
            d_hidden = dot(both_c[...], wv[:, :, :, d].reshape(WIDTH, 256), NN)
            sigma = lax.logistic(gate)
            active = gate * sigma
            unit = (active * up).astype(BF)
            d_gate = (d_hidden * up * sigma * (1.0 + gate * (1.0 - sigma))).astype(BF)
            d_up = (d_hidden * active).astype(BF)
            for half, rows in ((slice(0, 128), theirs), (slice(128, 256), mine)):
                hidden[rows, a] = unit[half, :]
                d_both[rows, a] = d_gate[half, :]
                d_both[rows, b] = d_up[half, :]
            return 0

        if k != 2:
            lax.fori_loop(0, 3, one, 0)
            return
        for j in range(3):
            for copy in weights_in[j]:
                copy.wait()
            one(j, 0)

    def back(k):
        lo, hi, theirs, mine = two(k)
        both_d[0:128, :] = d_both[theirs, :]
        both_d[128:, :] = d_both[mine, :]
        out = dot(both_d[...], weight(0, 1536), NT).astype(BF)
        part[1 - spot.c, lo, hi] = out[:128]
        part[spot.c, lo, hi] = out[128:]
        swaps[k] = w.push(part.at[1 - spot.c, lo, hi], got.at[k], spot.dev(other=True))

    swaps = {}

    def own(k):
        lo, hi, _, _ = two(k)
        return part.at[spot.c, lo, hi]

    def merge(k):
        swaps[k].wait_recv()
        add_into(own(k), got.at[k])

    def finish(total):
        load.wait()

        def body(rows):
            rms_back(total, mid, gain.at[1:2], rows, top, dmid, gain_grad)
            low[rows, :] = dmid[rows, :].astype(BF)

        by_rows(128, 16, body)

    def go(*parts):
        for one in parts:
            next(one, None)

    def down_tile(t, _):
        lanes = pl.ds(pl.multiple_of(t * BLOCK, BLOCK), BLOCK)
        out = dot(cv[:, lanes], hidden[...], TN)
        g_down[t // 2, pl.ds(t % 2 * 2, 2)] = out.astype(BF).reshape(2, 128, 768)
        return 0

    def in_copy(t):
        at = (t // 2, pl.ds(t % 2 * 2, 2))
        return pltpu.make_async_copy(g_part.at[at], g_in.at[at], tiles.at[2, t])

    def in_tile(t, _):
        lanes = pl.ds(pl.multiple_of(t * BLOCK, BLOCK), BLOCK)
        out = dot(nv[:, lanes], d_both[...], TN)
        g_part[t // 2, pl.ds(t % 2 * 2, 2)] = out.astype(BF).reshape(2, 128, 1536)
        in_copy(t).start()
        return 0

    def mixed_block(i, _):
        rows = pl.ds(pl.multiple_of(i * BLOCK, BLOCK), BLOCK)
        out = dot(hidden[rows, :], weight(1536, 768), NT)
        mixed_part[i // 2, i % 2] = out.astype(BF).reshape(2, 128, WIDTH)
        return 0

    right, left = spot.dev(dx=1), spot.dev(dx=-1)
    lows, highs = pl.ds(0, 64), pl.ds(64, 64)
    units(2)
    back(2)
    units(1)
    merge(2)
    far1 = w.push(own(2).at[lows], in1.at[0], right)
    far2 = w.push(own(2).at[highs], in1.at[1], left)
    back(1)
    units(3)
    merge(1)
    one = w.push(own(1).at[highs], in2.at[0, highs], right)
    back(3)
    units(0)
    merge(3)
    two_ = w.push(own(3).at[lows], in2.at[1, lows], left)
    far1.wait_recv()
    add_into(own(1).at[lows], in1.at[0])
    three = w.push(own(1).at[lows], in2.at[0, lows], right)
    far2.wait_recv()
    add_into(own(3).at[highs], in1.at[1])
    four = w.push(own(3).at[highs], in2.at[1, highs], left)
    back(0)
    lax.fori_loop(0, 8, down_tile, 0)
    down = plane_sum(w, spot, g_down, (p0, p1, p2, p3, p4, p5), resident=True)
    go(down)
    lax.fori_loop(0, 4, in_tile, 0)
    go(down)
    merge(0)
    for copy in (one, two_, three, four):
        copy.wait_recv()
    mine_ref = own(0)

    def total(rows):
        return mine_ref[rows, :].astype(F32) + in2[0, rows, :].astype(F32) + in2[1, rows, :].astype(F32)

    finish(total)
    share = column_share(w, spot, low, d_branch)
    go(share)
    lax.fori_loop(0, 4, mixed_block, 0)
    keep = w.local(mixed_part, mixed)
    go(share, down)
    lax.fori_loop(4, 8, in_tile, 0)
    go(share, down, share, down, down)
    assert share.gi_frame is None and down.gi_frame is None
    last = w.local(p5, both_out)
    for t in range(8):
        in_copy(t).wait()
    keep.wait()
    last.wait()
    w.drain()


def turn_call(normed, cot, w_b, mid, cot_own, gain):
    blocks = jax.ShapeDtypeStruct((2, 2, 2, 128, WIDTH), BF)
    return pl.pallas_call(
        turn_kernel,
        out_shape=(
            jax.ShapeDtypeStruct((128, WIDTH), F32),
            blocks,
            blocks,
            jax.ShapeDtypeStruct((4, 4, 128, 1536), BF),
            jax.ShapeDtypeStruct((1, WIDTH), F32),
            jax.ShapeDtypeStruct((2, 64, 768), BF),
        ),
        in_specs=[HBM, HBM, HBM, VMEM, HBM, VMEM],
        out_specs=(VMEM, HBM, HBM, HBM, VMEM, HBM),
        scratch_shapes=[
            pltpu.VMEM((COLUMN, WIDTH), BF),
            pltpu.VMEM((COLUMN, WIDTH), BF),
            pltpu.VMEM((4, 4, 128, 2304), BF),
            pltpu.VMEM((COLUMN, 768), BF),
            pltpu.VMEM((COLUMN, 1536), BF),
            pltpu.VMEM((2, 2, 2, 128, WIDTH), BF),
            pltpu.VMEM((4, 4, 128, 768), BF),
            pltpu.VMEM((4, 4, 128, 1536), BF),
            pltpu.VMEM((2, 2, 2, 128, WIDTH), BF),
            pltpu.VMEM((BLOCK, WIDTH), BF),
            pltpu.VMEM((BLOCK, WIDTH), BF),
            pltpu.VMEM((BLOCK, 1536), BF),
        ]
        + column_sum_scratch()[1:]
        + [pltpu.VMEM((128, WIDTH), BF)] * 2
        + plane_sum_scratch(768, True)
        + wires_scratch(64, 36)
        + [pltpu.SemaphoreType.DMA((3, 8))],
        compiler_params=params(4),
        name="turn",
    )(normed, cot, w_b, mid, cot_own, gain)


def sum_everywhere(w, spot, vector, pair, lines):
    a = w.push(vector, pair, spot.dev(other=True))
    yield
    a.wait_recv()
    w.sent_now(a)
    vector[...] = vector[...] + pair[...]
    yield
    for stage, (axis, at) in enumerate((("dx", spot.x), ("dy", spot.y), ("dz", spot.z))):
        slots = lines.at[stage]
        slots[at] = vector[...]
        copies = [w.push(vector, slots.at[at], spot.dev(**{axis: k})) for k in (1, 2, 3)]
        yield
        for copy in copies:
            copy.wait_recv()
            w.sent_now(copy)
        vector[...] = slots[0] + slots[1] + slots[2] + slots[3]
        yield


def as_row(column):
    return jnp.transpose(jnp.broadcast_to(column, (column.shape[0], HEAD)))[0:1, :]


def close_kernel(
    d_branch, h_w, h_a, h_attended, h_query, h_before, h_kv, h_raw, h_cosine, h_sine, doc_row, h_docs, h_inverse, q_gain, k_gain,
    g_in, both_down, mixed, mid, dmid, tok, gain, normed1, g_mlp,
    out, g_tok, o_gate, o_up, o_down, o_q, o_k, o_v, o_out, vector,
    w_w, w_a, attended, query, before, kv, raw, cosine, sine, doc_col, inverse,
    db, do, dq, dkv, d_before, came, d_raw, part, g_out, got, in1, in2,
    m_own, m_got, m_in1, m_in2, result, base, gain_grad, low, delta, back,
    a0, a1, a2, a3, a4, a5, a6, a7, a8, b0, b1, b2, b3, b4, b5, pair, lines, send, recv, here, tiles,
):
    spot = Spot()
    w = Wires(send, recv, here)

    def block(i):
        rows = pl.ds(pl.multiple_of(i * BLOCK, BLOCK), BLOCK)
        return pltpu.make_async_copy(d_branch.at[rows], db.at[rows], tiles.at[i])

    for i in range(4):
        block(i).start()
    fetched_w = w.local(h_w, w_w)
    fetched = [
        w.local(source, target)
        for source, target in (
            (h_attended, attended), (h_query, query), (h_before, before), (h_inverse, inverse), (h_docs, doc_col),
            (h_kv, kv), (h_raw, raw), (h_cosine, cosine), (h_sine, sine), (h_a, w_a),
        )
    ]
    load_tok = w.local(tok.at[spot.hi], base)
    greet(
        neighbours(spot, x=True, yz=True, core=True, pair=True, far=True)
        + [spot.column(1), spot.column(-1)]
    )

    def go(*parts):
        for one in parts:
            next(one, None)

    sum_in = plane_sum(w, spot, g_in, (a0, a1, a2, a3, a4, a5, a6, a7, a8))
    go(sum_in)

    def finish_out(total):
        def body(rows):
            result[rows, :] = (mid[rows, :] + total(rows)).astype(BF)

        by_rows(128, 16, body)

    fold_out = column_sum(w, spot, mixed, (m_own, m_got, m_in1, m_in2), finish_out)
    share_out = pair_share(w, spot, result, out)
    share_down = mate_share(w, spot, both_down, ((o_down, 0, 768),))
    go(fold_out, share_down)
    gain_grad[...] = jnp.zeros_like(gain_grad)
    vector[...] = jnp.zeros_like(vector)
    dkv[...] = jnp.zeros_like(dkv)
    dq[...] = jnp.zeros_like(dq)

    fetched_w.wait()

    def upstream_of(i, _):
        block(i).wait()
        rows = pl.ds(pl.multiple_of(i * BLOCK, BLOCK), BLOCK)
        do[rows, :] = dot(db[rows, :], w_w[...], NN).astype(BF)
        return 0

    lax.fori_loop(0, 4, upstream_of, 0)
    go(fold_out)
    for copy in fetched:
        copy.wait()

    def tile_out(t, _):
        lanes = pl.ds(pl.multiple_of(t * BLOCK, BLOCK), BLOCK)
        at = (t // 2, pl.ds(t % 2 * 2, 2), slice(None), slice(512, 768))
        g_out[at] = dot(db[:, lanes], attended[...], TN).astype(BF).reshape(2, 128, 256)
        return 0

    def tile(t, _):
        lanes = pl.ds(pl.multiple_of(t * BLOCK, BLOCK), BLOCK)
        at = (t // 2, pl.ds(t % 2 * 2, 2), slice(None), slice(0, 512))
        g_out[at] = dot(db[:, lanes], d_raw[...], TN).astype(BF).reshape(2, 128, 512)
        return 0


    for i in range(4):
        rows = slice(i * BLOCK, (i + 1) * BLOCK)
        product = attended[rows, :].astype(F32) * do[rows, :].astype(F32)
        for h in range(2):
            delta[h : h + 1, rows] = as_row(jnp.sum(product[:, h * HEAD : (h + 1) * HEAD], axis=-1, keepdims=True))
            back[h : h + 1, rows] = as_row(inverse[rows, h : h + 1])

    def attend_back(rows, keys_of, docs, causal, grads):
        valid = docs == doc_row[:, COLUMN + rows.start : COLUMN + rows.stop]
        if causal:
            row = lax.broadcasted_iota(jnp.int32, valid.shape, 0)
            valid = valid & (row <= lax.broadcasted_iota(jnp.int32, valid.shape, 1) + rows.start)
        for h in range(2):
            span = slice(h * HEAD, (h + 1) * HEAD)
            asked, upstream = query[rows, span], do[rows, span]
            scores = dot(keys_of[:, :HEAD], asked, NT) * SCALE
            probs = jnp.where(valid, jnp.exp(scores), 0.0) * back[h : h + 1, rows]
            d_probs = dot(keys_of[:, HEAD:], upstream, NT)
            d_scores = (probs * (d_probs - delta[h : h + 1, rows])).astype(BF)
            grads[:, :HEAD] += dot(d_scores, asked, NN) * SCALE
            grads[:, HEAD:] += dot(probs.astype(BF), upstream, NN)
            d_asked = dot(d_scores, keys_of[:, :HEAD], TN) * SCALE
            dq[rows, span] += d_asked

    back_kv = []
    for j in range(4):
        end, keys = (j + 1) * BLOCK, slice(j * BLOCK, (j + 1) * BLOCK)
        attend_back(slice(0, end), before.at[keys], doc_col[keys, 0:1], False, dkv.at[keys])
        d_before[keys, :] = dkv[keys, :].astype(BF)
        back_kv.append(w.push(d_before.at[keys], came.at[keys], spot.column(-1)))
    go(fold_out)
    lax.fori_loop(0, 8, tile_out, 0)
    load_n1 = w.local(normed1, db)
    for i in range(4):
        end = (i + 1) * BLOCK
        attend_back(
            slice(i * BLOCK, end), kv.at[0:end], doc_col[COLUMN : COLUMN + end, 0:1], True, dkv.at[COLUMN : COLUMN + end]
        )
        if i == 1:
            go(fold_out, share_out)
    for copy in back_kv:
        copy.wait_recv()
    go(sum_in)

    def project_back(i, _):
        rows = pl.ds(pl.multiple_of(i * BLOCK, BLOCK), BLOCK)
        own = pl.ds(pl.multiple_of(i * BLOCK + COLUMN, BLOCK), BLOCK)
        for h, scale in enumerate((q_gain, q_gain, k_gain)):
            span = slice(h * HEAD, (h + 1) * HEAD)
            if h < 2:
                grad = dq[rows, span]
            else:
                grad = dkv[own, :HEAD] + came[rows, :HEAD].astype(F32)
            grad = grad * cosine[rows, :] - turn_half(grad) * sine[rows, :]
            unit, root = rms_of(raw[rows, span])
            scaled = grad * scale[...].astype(F32)
            back = root * (scaled - unit * jnp.mean(scaled * unit, axis=-1, keepdims=True))
            d_raw[rows, span] = back.astype(BF)
            at = 32 + h // 2
            vector[at : at + 1, :] += jnp.sum(grad * unit, axis=0, keepdims=True)
        d_raw[rows, 3 * HEAD :] = (dkv[own, HEAD:] + came[rows, HEAD:].astype(F32)).astype(BF)
        return 0

    def norm_of(core):
        def one(lo, _):
            rows = pl.ds(pl.multiple_of((core * 2 + lo) * BLOCK, BLOCK), BLOCK)
            value = dot(d_raw[rows, :], w_a[:, :512], NT)
            part[core, lo] = value.astype(BF).reshape(2, 128, WIDTH)
            return 0

        lax.fori_loop(0, 2, one, 0)

    def finish(total):
        load_tok.wait()

        def body(rows):
            rms_back(total, base, gain.at[0:1], rows, dmid, low, gain_grad)

        by_rows(128, 16, body)

    lax.fori_loop(0, 4, project_back, 0)
    load_n1.wait()
    sum_out = plane_sum(w, spot, g_out, (b0, b1, b2, b3, b4, b5), resident=True)
    fold = column_sum(w, spot, part, (None, got, in1, in2), finish, resident=True)
    norm_of(1 - spot.c)
    go(fold)
    norm_of(spot.c)
    go(fold)
    lax.fori_loop(0, 8, tile, 0)
    go(sum_out, fold, sum_in, sum_out, fold)
    share_tok = pair_share(w, spot, low, g_tok)
    vector[16:32, :] = g_mlp[...]
    for i in range(16):
        vector[i : i + 1, :] = gain_grad[:, i * 128 : (i + 1) * 128]
    share_in = mate_share(w, spot, a8, ((o_gate, 0, 768), (o_up, 768, 768)))
    everywhere = sum_everywhere(w, spot, vector, pair, lines)
    go(share_tok, sum_in, everywhere, sum_out, everywhere, everywhere, sum_in, sum_out, sum_in, share_in, everywhere, everywhere, sum_out, sum_out)
    share_grads = mate_share(
        w, spot, b5, ((o_q, 0, 256), (o_k, 256, 128), (o_v, 384, 128), (o_out, 512, 256))
    )
    go(share_grads, everywhere, everywhere, share_out, share_down, everywhere, everywhere, share_in, share_tok, share_grads)
    for part_left in (sum_in, fold_out, share_out, share_down, fold, sum_out, everywhere, share_in, share_grads, share_tok):
        assert part_left.gi_frame is None
    w.drain()


def close_call(*args):
    def shape(*sizes, kind=BF):
        return jax.ShapeDtypeStruct(sizes, kind)

    return pl.pallas_call(
        close_kernel,
        out_shape=(
            shape(2, 128, WIDTH),
            shape(2, 128, WIDTH),
            shape(64, 3072),
            shape(64, 3072),
            shape(64, 3072),
            shape(64, 1024),
            shape(64, 512),
            shape(64, 512),
            shape(64, 1024),
            shape(40, 128, kind=F32),
        ),
        in_specs=[HBM] * 10 + [VMEM, HBM, HBM, VMEM, VMEM] + [HBM, VMEM, HBM, VMEM, VMEM, HBM, VMEM, HBM, VMEM],
        out_specs=(HBM,) * 9 + (VMEM,),
        scratch_shapes=[
            pltpu.VMEM((WIDTH, 256), BF),
            pltpu.VMEM((WIDTH, 640), BF),
            pltpu.VMEM((COLUMN, 256), BF),
            pltpu.VMEM((COLUMN, 256), BF),
            pltpu.VMEM((COLUMN, 256), BF),
            pltpu.VMEM((COLUMN, 256), BF),
            pltpu.VMEM((COLUMN, 512), F32),
            pltpu.VMEM((COLUMN, HEAD), F32),
            pltpu.VMEM((COLUMN, HEAD), F32),
            pltpu.VMEM((2 * COLUMN, 128), F32),
            pltpu.VMEM((COLUMN, 2), F32),
            pltpu.VMEM((COLUMN, WIDTH), BF),
            pltpu.VMEM((COLUMN, 256), BF),
            pltpu.VMEM((COLUMN, 256), F32),
            pltpu.VMEM((2 * COLUMN, 256), F32),
            pltpu.VMEM((COLUMN, 256), BF),
            pltpu.VMEM((COLUMN, 256), BF),
            pltpu.VMEM((COLUMN, 512), BF),
            pltpu.VMEM((2, 2, 2, 128, WIDTH), BF),
            pltpu.VMEM((4, 4, 128, 768), BF),
        ]
        + column_sum_scratch()[1:]
        + column_sum_scratch()
        + [
            pltpu.VMEM((128, WIDTH), BF),
            pltpu.VMEM((128, WIDTH), BF),
            pltpu.VMEM((1, WIDTH), F32),
            pltpu.VMEM((128, WIDTH), BF),
            pltpu.VMEM((2, COLUMN), F32),
            pltpu.VMEM((2, COLUMN), F32),
        ]
        + plane_sum_scratch(1536, False)
        + plane_sum_scratch(768, True)
        + [pltpu.VMEM((40, 128), F32), pltpu.VMEM((3, 4, 40, 128), F32)]
        + wires_scratch(120, 50)
        + [pltpu.SemaphoreType.DMA((4,))],
        compiler_params=params(6),
        name="close",
    )(*args)


def finish_kernel(*refs):
    ins, outs = refs[:10], refs[10:]
    vector = ins[9]
    outs[0][...] = ins[0][...]
    for source, target in zip(ins[1:9], outs[1:9]):
        target[...] = source[...].astype(F32)
    shard = lax.axis_index("shard")
    for first, target in ((0, outs[9]), (16, outs[10])):
        line = vector[pl.ds(first + shard // 2, 1), :]
        target[...] = jnp.where(shard % 2 == 0, line[:, 0:64], line[:, 64:128])
    outs[11][...] = vector[32:33, :]
    outs[12][...] = vector[33:34, :]


def finish_call(out, g_tok, *rest):
    tall = pl.BlockSpec((64, WIDTH), lambda i: (i, 0))
    grads, vector = rest[:-1], rest[-1]
    wide = [pl.BlockSpec((64, g.shape[1] // 4), lambda i: (0, i)) for g in grads]
    tops = [jax.ShapeDtypeStruct((1, n), F32) for n in (64, 64, 128, 128)]
    return pl.pallas_call(
        finish_kernel,
        grid=(4,),
        out_shape=(
            jax.ShapeDtypeStruct(out.shape, BF),
            jax.ShapeDtypeStruct(g_tok.shape, F32),
            *(jax.ShapeDtypeStruct(g.shape, F32) for g in grads),
            *tops,
        ),
        in_specs=[tall, tall] + wide + [VMEM],
        out_specs=[tall, tall] + wide + [VMEM] * 4,
        compiler_params=pltpu.CompilerParams(vmem_limit_bytes=LIMIT),
        name="finish",
    )(out, g_tok, *grads, vector)


def on_device(
    tokens, lengths, attn_norm, w_query, w_key, w_value, w_output, q_gain, k_gain, mlp_norm, w_gate, w_up, w_down, cotangent,
):
    freq = THETA ** (-np.arange(0, HEAD, 2).astype(np.float32) / np.float32(HEAD))
    freq = jnp.asarray(np.concatenate([freq, freq])[None].astype(np.float32))
    both_gains = jnp.tile(jnp.pad(jnp.stack([attn_norm, mlp_norm], axis=1), ((0, 0), (0, 126))), (1, 4))
    (
        normed1, w_a, w_w, w_b, cot, raw, query, kv, before, attended, inverse, middle, normed2, cosine, sine, gains, doc_row, doc_col,
    ) = forward_call(
        tokens, cotangent, w_query, w_key, w_value, w_output.T, both_gains, w_gate, w_up, w_down.T, lengths, freq, q_gain[None], k_gain[None]
    )
    w_a, w_w = w_a.reshape(WIDTH, 640), w_w.reshape(WIDTH, 256)
    d_middle, d_branch, mixed, g_in, g_mlp, both_down = turn_call(
        normed2.reshape(COLUMN, WIDTH),
        cot.reshape(COLUMN, WIDTH),
        w_b,
        middle,
        cotangent.reshape(2, 128, WIDTH),
        gains,
    )
    out, g_tokens, g_gate, g_up, g_down, g_query, g_key, g_value, g_output, sums = close_call(
        d_branch.reshape(COLUMN, WIDTH), w_w, w_a, attended, query, before, kv, raw, cosine, sine, doc_row, doc_col, inverse,
        q_gain[None], k_gain[None], g_in, both_down, mixed, middle, d_middle, tokens.reshape(2, 128, WIDTH), gains,
        normed1, g_mlp.reshape(16, 128),
    )

    (
        out, g_tokens, g_gate, g_up, g_down, g_query, g_key, g_value, g_output, g_attn, g_mlp, g_q_gain, g_k_gain,
    ) = finish_call(
        out.reshape(256, WIDTH), g_tokens.reshape(256, WIDTH), g_gate, g_up, g_down, g_query, g_key, g_value, g_output, sums
    )
    return (
        out, g_tokens, g_attn[0], g_query, g_key, g_value, g_output.T, g_q_gain[0], g_k_gain[0], g_mlp[0], g_gate, g_up, g_down.T,
    )


def solution(mesh):
    rows = P(("shard", "dp"), None)
    down = P("shard", "tensor")
    across = P("tensor", "shard")
    one = P("shard")
    return jax.shard_map(
        on_device,
        mesh=mesh,
        in_specs=(rows, P(), one, down, down, down, across, P(), P(), one, down, down, across, rows),
        out_specs=(rows, rows, one, down, down, down, across, P(), P(), one, down, down, across),
        check_vma=False,
    )
```
